128 devices in a mesh: dp: 8 (over x, core), seq: 16 (over y, z).
Axes of the slice: x: 4, y: 4, z: 4, core: 2. Of those that a mesh axis runs over, the one named last changes fastest.
Arguments:
- candidates: bfloat16 [32768, 256], P(('dp', 'seq')), may hold values from -6 to 6
- scenarios: int32 [32768], P(('dp', 'seq')), may hold values from 0 to 15
- candidate_user: int32 [32768], P(('dp', 'seq')), may hold values from 0 to 15, as said below
- gate_table: float32 [16, 256], replicated, may hold values from 0.1 to 1.9
- log_normalizer: float32 [32768], P(('dp', 'seq')), as said below
- forward_out: bfloat16 [32768, 256], P(('dp', 'seq')), may hold values from -1.5 to 1.5
- out_grad: bfloat16 [32768, 256], P(('dp', 'seq')), may hold values from -96 to 96
- history: bfloat16 [16, 8192, 256], P('dp', 'seq'), may hold values from -6 to 6
- history_length: int32 [16], P('dp'), may hold values from 1024 to 8192, as said below
- history_items: int32 [16, 8192], P('dp', 'seq'), may hold values from 0 to 524287, as said below
Outputs:
- candidate_grad: float32 [32768, 256], P(('dp', 'seq'))
- table_grad: float32 [524288, 256], P(('dp', 'seq'))
The draws below stay inside these ranges and needn't reach their ends.
Inputs may be any that keep to these rules, and one draw needn't show every extreme that they name: `candidate_user`: candidate c belongs to one of the 2 users numbered from (c // (256 * 16)) * 2; all 256 candidates held by one device belong to the same user, and each of those 2 users owns the candidates of exactly 16 // 2 of the group's devices. `history_length`: every user has at least 1024 valid positions; some user has all 8192. `log_normalizer`: within 1.5 of 0.5 plus the log of the length of the candidate's user. `history_items`: the table rows k * 4096 to (k + 1) * 4096 - 1 are owner k's; of the history positions held by one device, at most 16 name rows of one owner, and in every draw some owner is named by exactly 16 positions of every device.
All inputs are finite; a program needn't handle non-finite values.
Results may differ from the reference program's by a relative error of at most 0.0045.
Values may be sent and summed in bfloat16 or wider, within the bound.
A program may use at most 64 MiB of HBM per device.

```python
import math
import jax
import jax.numpy as jnp
from jax import lax

D = 256
SCEN = 16
CAND_DEV = 256
U_DEV = 2
HIST_DEV = 512
ITEM_DEV = 4096
HIST = 8192
USERS = 16
CANDS = 32768
ITEMS = 524288
CAP = 16
N_DP = 8
N_SEQ = 16
DEVICES = 128


def shared_users(key):
    key_length, key_forced, key_picked = jax.random.split(key, 3)
    lengths = jax.random.randint(key_length, (USERS,), HIST // 8, HIST + 1)
    forced = jax.random.randint(key_forced, (), 0, USERS)
    lengths = jnp.where(jnp.arange(USERS) == forced, HIST, lengths).astype(jnp.int32)
    pick_keys = jax.random.split(key_picked, N_DP)
    picks = jax.vmap(lambda seed_key: jax.random.permutation(seed_key, N_SEQ))(pick_keys)
    device_user = jnp.arange(N_DP)[:, None] * U_DEV + picks % U_DEV
    owners = jnp.broadcast_to(device_user[:, :, None], (N_DP, N_SEQ, CAND_DEV)).reshape(CANDS)
    return (lengths, owners.astype(jnp.int32))


def draw_history_length(key, part):
    lengths, owners = shared_users(key)
    return lengths


def draw_candidate_user(key, part):
    lengths, owners = shared_users(key)
    return owners


def draw_log_normalizer(key, part):
    lengths, owners = shared_users(key)
    key = jax.random.fold_in(key, 5)
    noise = jax.random.uniform(key, (CANDS,), jnp.float32, -0.5, 0.5)
    return jnp.log(lengths[owners].astype(jnp.float32)) + 0.5 + noise


def draw_history_items(key, part):
    key = jax.random.fold_in(key, 11)
    key_full, key_slots, key_order, key_low, key_high = jax.random.split(key, 5)
    rows_device = U_DEV * HIST_DEV
    full_owner = jax.random.randint(key_full, (), 0, DEVICES)
    slot_keys = jax.random.split(key_slots, DEVICES)
    slots = jax.vmap(lambda seed_key: jax.random.permutation(seed_key, (DEVICES - 1) * CAP)[:rows_device - CAP])(slot_keys)
    others = slots // CAP
    others = others + (others >= full_owner).astype(others.dtype)
    owners = jnp.concatenate([jnp.full((DEVICES, CAP), full_owner, others.dtype), others], axis=1)
    order_keys = jax.random.split(key_order, DEVICES)
    orders = jax.vmap(lambda seed_key: jax.random.permutation(seed_key, rows_device))(order_keys)
    owners = jnp.take_along_axis(owners, orders, axis=1)
    lower = jax.random.randint(key_low, (DEVICES, rows_device), 0, ITEM_DEV)
    upper = jax.random.randint(key_high, (DEVICES, rows_device), 0, ITEM_DEV)
    items = owners * ITEM_DEV + jnp.minimum(lower, upper)
    items = items.reshape(N_DP, N_SEQ, U_DEV, HIST_DEV).transpose(0, 2, 1, 3).reshape(USERS, HIST)
    return items.astype(jnp.int32)


def with_ends(values, rng, least, top_value):
    longest = values.shape.index(max(values.shape))
    spots = []
    for shift in (0, 1):
        where = [jax.random.randint(jax.random.fold_in(rng, axis), (), 0, length) for axis, length in enumerate(values.shape)]
        where[longest] = (where[longest] + shift) % values.shape[longest]
        spots.append(tuple(where))
    return values.at[spots[0]].set(least).at[spots[1]].set(top_value)


def block_levels(own_key, shape, pieces, least, largest):
    loudness, own = 1.0, jax.random.fold_in(own_key, 6)
    for position, blocks in pieces:
        steps = jnp.exp(jax.random.uniform(jax.random.fold_in(own, position), (blocks,), jnp.float32, least / len(pieces), largest / len(pieces)))
        loudness = loudness * jnp.repeat(steps, shape[position] // blocks).reshape([-1 if axis == position else 1 for axis in range(len(shape))])
    return loudness


def normal_values(key, extent, width, most, cuts=(), kind=jnp.bfloat16):
    factor_of = block_levels(key, extent, cuts, -0.22, 0.18) if cuts else 1.0
    values = jax.random.normal(key, extent, jnp.float32) * width * factor_of
    return jnp.minimum(jnp.maximum(values, -most), most).astype(kind)


def setup_inputs(seed: int = 0) -> dict:
    keys = jax.random.split(jax.random.key(seed), 11)
    candidates = normal_values(keys[0], (CANDS, D), 1.0, 6.0, ((0, 128),))
    scenarios = with_ends(jax.random.randint(keys[1], (CANDS,), 0, SCEN), jax.random.fold_in(keys[1], 1), 0, SCEN - 1).astype(jnp.int32)
    candidate_user = draw_candidate_user(jax.random.fold_in(keys[10], 71), 0)
    gate_table = jnp.clip(1.0 + 0.18 * jax.random.normal(keys[3], (SCEN, D), jnp.float32), 0.1, 1.9)
    log_normalizer = draw_log_normalizer(jax.random.fold_in(keys[10], 71), 0)
    forward_out = normal_values(keys[5], (CANDS, D), 0.25, 1.5, ((0, 128),))
    out_grad = normal_values(keys[6], (CANDS, D), 16.0, 96.0, ((0, 128),))
    history = normal_values(keys[7], (USERS, HIST, D), 1.0, 6.0, ((0, 8), (1, 16)))
    history_length = draw_history_length(jax.random.fold_in(keys[10], 71), 0)
    history_items = draw_history_items(jax.random.fold_in(keys[10], 71), 0)
    return {"candidates": candidates, "scenarios": scenarios, "candidate_user": candidate_user, "gate_table": gate_table, "log_normalizer": log_normalizer, "forward_out": forward_out, "out_grad": out_grad, "history": history, "history_length": history_length, "history_items": history_items}


def block_grads(queries, grads_out, normalizer, inner_sum, owners, key_rows, user_id, first_pos, length, score_scale):
    scores = jnp.dot(queries, key_rows.T, preferred_element_type=jnp.float32) * score_scale
    positions = first_pos + jnp.arange(key_rows.shape[0], dtype=jnp.int32)
    allowed = (owners[:, None] == user_id) & (positions[None, :] < length)
    probability = jnp.where(allowed, jnp.exp(scores - normalizer[:, None]), jnp.zeros_like(scores))
    probability_low = probability.astype(jnp.bfloat16)
    prob_grad = jnp.dot(grads_out, key_rows.T, preferred_element_type=jnp.float32)
    score_grad = (probability * (prob_grad - inner_sum[:, None])).astype(jnp.bfloat16)
    query_part = jnp.dot(score_grad, key_rows, preferred_element_type=jnp.float32)
    key_part = jnp.dot(score_grad.T, queries, preferred_element_type=jnp.float32) * score_scale
    key_part = key_part + jnp.dot(probability_low.T, grads_out, preferred_element_type=jnp.float32)
    return (query_part, key_part)

def reference(candidates, scenarios, candidate_user, gate_table, log_normalizer, forward_out, out_grad, history, history_length, history_items):
    score_scale = 1.0 / math.sqrt(D)
    gate_rows = gate_table[scenarios]
    queries = (candidates.astype(jnp.float32) * gate_rows).astype(jnp.bfloat16)
    inner_sum = lax.optimization_barrier(jnp.sum(out_grad.astype(jnp.float32) * forward_out.astype(jnp.float32), axis=1))
    group_rows = CAND_DEV * N_SEQ
    block_rows = min(HIST_DEV, 1024)
    per_user = HIST // block_rows

    def one_group(group_id):
        row_start = (group_id * group_rows).astype(jnp.int32)
        user_start = (group_id * U_DEV).astype(jnp.int32)
        group_queries = lax.dynamic_slice_in_dim(queries, row_start, group_rows, 0)
        group_grads = lax.dynamic_slice_in_dim(out_grad, row_start, group_rows, 0)
        group_norm = lax.dynamic_slice_in_dim(log_normalizer, row_start, group_rows, 0)
        group_inner = lax.dynamic_slice_in_dim(inner_sum, row_start, group_rows, 0)
        group_owner = lax.dynamic_slice_in_dim(candidate_user, row_start, group_rows, 0)
        group_keys = lax.dynamic_slice_in_dim(history, user_start, U_DEV, 0).reshape(U_DEV * per_user, block_rows, D)
        lengths = lax.dynamic_slice_in_dim(history_length, user_start, U_DEV, 0)

        def sweep_step(running, inputs):
            number, key_block = inputs
            local_user = number // per_user
            first_pos = (number % per_user * block_rows).astype(jnp.int32)
            query_part, key_part = block_grads(group_queries, group_grads, group_norm, group_inner, group_owner, key_block, user_start + local_user, first_pos, lengths[local_user], score_scale)
            return (running + query_part, key_part)
        numbers = jnp.arange(U_DEV * per_user, dtype=jnp.int32)
        running, key_parts = lax.scan(sweep_step, jnp.zeros((group_rows, D), jnp.float32), (numbers, group_keys))
        return (running, key_parts.reshape(U_DEV, HIST, D))
    query_total, history_grad = lax.map(one_group, jnp.arange(N_DP, dtype=jnp.int32))
    candidate_grad = query_total.reshape(CANDS, D) * score_scale * gate_rows
    table_grad = jax.ops.segment_sum(history_grad.reshape(USERS * HIST, D), history_items.reshape(USERS * HIST), num_segments=ITEMS)
    return (candidate_grad, table_grad)
```

```python
import math

import jax
import jax.numpy as jnp
from jax import lax
from jax.experimental import pallas as pl
from jax.experimental.pallas import tpu as pltpu
from jax.sharding import PartitionSpec as P

ITEM_DEV = 4096
MESH = pl.DeviceIdType.MESH

ORDER = [
    (0, 0), (0, 1), (0, 3), (1, 0), (3, 0), (0, 2), (2, 0),
    (1, 1), (1, 3), (3, 1), (3, 3), (1, 2), (3, 2), (2, 1), (2, 3), (2, 2),
]
SLOT = {offset: i for i, offset in enumerate(ORDER)}
QUARTERS = [(0, 128), (128, 128), (256, 128), (384, 144)]
BLOCK = 528
YP, YM, ZP, ZM = (1, 0), (-1, 0), (0, 1), (0, -1)


def forward_plan():
    plan = {i: [] for i in range(16)}

    def wait(step, offset, quarters):
        plan[step].append(("wait", offset, quarters))

    def send(step, offset, quarter, direction):
        plan[step].append(("send", offset, quarter, direction))

    a, b = (0, 1), (2, 3)
    for q in a:
        send(0, (0, 0), q, ZP)
        send(0, (0, 0), q, ZM)
    for q in b:
        send(0, (0, 0), q, YP)
        send(0, (0, 0), q, YM)
    for q in a:
        send(0, (0, 0), q, YP)
        send(0, (0, 0), q, YM)
    for q in b:
        send(0, (0, 0), q, ZP)
        send(0, (0, 0), q, ZM)
    for offset in ((0, 1), (0, 3)):
        wait(1, offset, a)
    for offset in ((1, 0), (3, 0)):
        wait(1, offset, b)
    send(1, (0, 3), 0, ZP)
    send(1, (0, 1), 1, ZM)
    send(1, (3, 0), 2, YP)
    send(1, (1, 0), 3, YM)
    for q in a:
        for offset in ((0, 1), (0, 3)):
            send(1, offset, q, YP)
            send(1, offset, q, YM)
    for q in b:
        for offset in ((1, 0), (3, 0)):
            send(1, offset, q, ZP)
            send(1, offset, q, ZM)
    for offset in ((0, 1), (0, 3)):
        wait(1, offset, b)
    for offset in ((1, 0), (3, 0)):
        wait(1, offset, a)
    send(1, (0, 3), 2, ZP)
    send(1, (0, 1), 3, ZM)
    send(1, (3, 0), 0, YP)
    send(1, (1, 0), 1, YM)
    wait(5, (0, 2), a)
    wait(5, (2, 0), b)
    for q in a:
        send(5, (0, 2), q, YP)
        send(5, (0, 2), q, YM)
    for q in b:
        send(5, (2, 0), q, ZP)
        send(5, (2, 0), q, ZM)
    wait(5, (0, 2), b)
    wait(5, (2, 0), a)
    for dz in (1, 3):
        wait(7, (3, dz), a)
        wait(7, (1, dz), a)
        send(7, (3, dz), 0, YP)
        send(7, (1, dz), 1, YM)
    for dy in (1, 3):
        wait(7, (dy, 3), b)
        wait(7, (dy, 1), b)
        send(7, (dy, 3), 2, ZP)
        send(7, (dy, 1), 3, ZM)
    wait(11, (3, 2), a)
    wait(11, (1, 2), a)
    send(11, (3, 2), 0, YP)
    send(11, (1, 2), 1, YM)
    wait(11, (2, 3), b)
    wait(11, (2, 1), b)
    send(11, (2, 3), 2, ZP)
    send(11, (2, 1), 3, ZM)
    wait(11, (1, 2), b)
    wait(11, (3, 2), b)
    wait(11, (2, 1), a)
    wait(11, (2, 3), a)
    wait(15, (2, 2), a + b)
    return plan


PLAN = forward_plan()
SENDS = [e for i in range(16) for e in PLAN[i] if e[0] == "send"]


def split3(x):
    hi = x.astype(jnp.bfloat16).astype(jnp.float32)
    rest = x - hi
    mid = rest.astype(jnp.bfloat16).astype(jnp.float32)
    return hi, mid, rest - mid


def nt(a, b):
    return lax.dot_general(a, b, (((1,), (1,)), ((), ())), preferred_element_type=jnp.float32)


def tn(a, b):
    return lax.dot_general(a, b, (((0,), (0,)), ((), ())), preferred_element_type=jnp.float32)


def quantized(x):
    top = jnp.max(jnp.abs(x), axis=0, keepdims=True)
    power = jnp.ceil(jnp.log(jnp.maximum(top, 1e-33)) * (1.0 / math.log(2.0)))
    power = jnp.clip(power, -110.0, 127.0)
    q = jnp.round(x * (jnp.exp2(15.0 - power) * 0.99)).astype(jnp.int32)
    half = x.shape[0] // 2
    words = (q[half:] << 16) | (q[:half] & 0xFFFF)
    return words, jnp.broadcast_to(power.astype(jnp.int32), (8, x.shape[1]))


def restored(words, power):
    scale = jnp.exp2(power.astype(jnp.float32) - 15.0) * (1.0 / 0.99)
    low = ((words << 16) >> 16).astype(jnp.float32) * scale
    high = (words >> 16).astype(jnp.float32) * scale
    return low, high


def attention_kernel(
    cand_ref, scen_ref, user_ref, gate_ref, norm_ref, fwd_ref, grad_ref, hist_ref, length_ref,
    cand_out, hist_out,
    buf, keys, gates, total, part_out, part_in, send_sem, recv_sem, part_send, part_recv,
):
    dp = lax.axis_index("dp")
    seq = lax.axis_index("seq")
    y, z = seq // 4, seq % 4

    def device(dy, dz):
        return (dp, (y + dy + 4) % 4 * 4 + (z + dz + 4) % 4)

    barrier = pltpu.get_barrier_semaphore()
    for offset in ORDER[1:]:
        pl.semaphore_signal(barrier, inc=1, device_id=device(*offset), device_id_type=MESH)

    def block_copy(number):
        _, offset, quarter, (dy, dz) = SENDS[number]
        there = SLOT[(offset[0] - dy) % 4, (offset[1] - dz) % 4]
        rows = pl.ds(*QUARTERS[quarter])
        return pltpu.make_async_remote_copy(
            src_ref=buf.at[SLOT[offset], rows],
            dst_ref=buf.at[there, rows],
            send_sem=send_sem.at[number],
            recv_sem=recv_sem.at[there, quarter],
            device_id=device(dy, dz),
            device_id_type=MESH,
        )

    def block_arrival(offset, quarter):
        rows = pl.ds(*QUARTERS[quarter])
        slot = SLOT[offset]
        return pltpu.make_async_remote_copy(
            src_ref=buf.at[slot, rows],
            dst_ref=buf.at[slot, rows],
            send_sem=send_sem.at[0],
            recv_sem=recv_sem.at[slot, quarter],
            device_id=device(0, 1),
            device_id_type=MESH,
        )

    def part_copy(i):
        dy, dz = ORDER[i]
        there = SLOT[-dy % 4, -dz % 4]
        return pltpu.make_async_remote_copy(
            src_ref=part_out.at[i],
            dst_ref=part_in.at[there],
            send_sem=part_send.at[i],
            recv_sem=part_recv.at[there],
            device_id=device(dy, dz),
            device_id_type=MESH,
        )

    scen_rows = scen_ref[...] == lax.broadcasted_iota(jnp.int32, (16, 256), 0)
    gates[...] = lax.dot_general(
        scen_rows.astype(jnp.float32), gate_ref[...], (((0,), (0,)), ((), ())),
        precision=lax.Precision.HIGHEST, preferred_element_type=jnp.float32,
    )
    queries = (cand_ref[...].astype(jnp.float32) * gates[...]).astype(jnp.bfloat16)
    buf[0, 0:256] = queries * jnp.bfloat16(0.0625)
    grads = grad_ref[...]
    buf[0, 256:512] = grads
    inner = lax.dot_general(
        jnp.ones((8, 256), jnp.float32),
        grads.astype(jnp.float32) * fwd_ref[...].astype(jnp.float32),
        (((1,), (1,)), ((), ())),
        precision=lax.Precision.HIGHEST, preferred_element_type=jnp.float32,
    )[0:1]
    user = (user_ref[...] - 2 * dp).astype(jnp.float32)
    numbers = [*split3(norm_ref[...]), *split3(inner), 1.0 - user, user]
    numbers = jnp.concatenate(numbers + [jnp.zeros((8, 256), jnp.float32)], axis=0)
    buf[0, 512:528] = numbers.astype(jnp.bfloat16)

    pl.semaphore_wait(barrier, 15)

    def run_plan(step):
        for event in PLAN[step]:
            if event[0] == "wait":
                for quarter in event[2]:
                    block_arrival(event[1], quarter).wait_recv()
            else:
                block_copy(SENDS.index(event)).start()

    run_plan(0)

    first = seq * 512
    places = first + lax.broadcasted_iota(jnp.int32, (512, 256), 0)
    for u in range(2):
        rows = hist_ref[u].astype(jnp.float32)
        keys[u] = jnp.where(places < length_ref[u], rows, 0.0).astype(jnp.bfloat16)
    hist_out[...] = jnp.zeros_like(hist_out)

    def step(k, carry):
        for i in range(1, 16):
            if PLAN[i]:
                pl.when(k == i)(lambda i=i: run_plan(i))
        numbers = buf[k, 512:528].astype(jnp.float32)
        normalizer = numbers[0:1] + numbers[1:2] + numbers[2:3]
        inner_sum = numbers[3:4] + numbers[4:5] + numbers[5:6]
        pick = [numbers[6:7], numbers[7:8]]
        low = [w.astype(jnp.bfloat16) for w in pick]
        both = buf[k, 0:512]
        query_part = jnp.zeros((256, 256), jnp.float32)
        for c in range(2):
            rows = pl.ds(c * 256, 256)
            mine = keys[0, rows] * low[0] + keys[1, rows] * low[1]
            products = nt(mine, both)
            probability = jnp.exp(products[:, :256] - normalizer)
            score_grad = (probability * (products[:, 256:] - inner_sum)).astype(jnp.bfloat16)
            weights = jnp.concatenate([score_grad, probability.astype(jnp.bfloat16)], axis=1)
            key_part = jnp.dot(weights, both, preferred_element_type=jnp.float32)
            hist_out[0, rows] += key_part * pick[0]
            hist_out[1, rows] += key_part * pick[1]
            query_part += tn(score_grad, mine)

        @pl.when(k == 0)
        def _():
            total[...] = query_part

        @pl.when(k > 0)
        def _():
            words, power = quantized(query_part)
            part_out[k, 0:128] = words
            part_out[k, 128:136] = power

        for i in range(1, 16):
            pl.when(k == i)(lambda i=i: part_copy(i).start())
        return carry

    lax.fori_loop(0, 16, step, 0)

    for u in range(2):
        hist_out[u] = jnp.where(places < length_ref[u], hist_out[u], 0.0)
    for i in range(1, 16):
        pltpu.make_async_remote_copy(
            src_ref=part_out.at[i],
            dst_ref=part_in.at[i],
            send_sem=part_send.at[i],
            recv_sem=part_recv.at[i],
            device_id=device(0, 1),
            device_id_type=MESH,
        ).wait_recv()

    low, high = total[0:128], total[128:256]
    for i in range(1, 16):
        a, b = restored(part_in[i, 0:128], part_in[i, 128:129])
        low, high = low + a, high + b
    cand_out[0:128] = low * 0.0625 * gates[0:128]
    cand_out[128:256] = high * 0.0625 * gates[128:256]
    for number in range(len(SENDS)):
        block_copy(number).wait_send()
    for i in range(1, 16):
        part_copy(i).wait_send()


def attention(candidates, scenarios, users, gate_table, normalizer, forward_out, out_grad, history, lengths):
    vmem = pl.BlockSpec(memory_space=pltpu.VMEM)
    return pl.pallas_call(
        attention_kernel,
        out_shape=(
            jax.ShapeDtypeStruct((256, 256), jnp.float32),
            jax.ShapeDtypeStruct((2, 512, 256), jnp.float32),
        ),
        in_specs=[vmem] * 8 + [pl.BlockSpec(memory_space=pltpu.SMEM)],
        out_specs=(vmem, vmem),
        scratch_shapes=[
            pltpu.VMEM((16, BLOCK, 256), jnp.bfloat16),
            pltpu.VMEM((2, 512, 256), jnp.bfloat16),
            pltpu.VMEM((256, 256), jnp.float32),
            pltpu.VMEM((256, 256), jnp.float32),
            pltpu.VMEM((16, 136, 256), jnp.int32),
            pltpu.VMEM((16, 136, 256), jnp.int32),
            pltpu.SemaphoreType.DMA((len(SENDS),)),
            pltpu.SemaphoreType.DMA((16, 4)),
            pltpu.SemaphoreType.DMA((16,)),
            pltpu.SemaphoreType.DMA((16,)),
        ],
        compiler_params=pltpu.CompilerParams(
            collective_id=0, has_side_effects=True, vmem_limit_bytes=48 * 1024 * 1024
        ),
        cost_estimate=pl.CostEstimate(
            flops=5_400_000_000, bytes_accessed=4_000_000, transcendentals=2_100_000
        ),
        name="attention_grads",
    )(
        candidates, scenarios.reshape(1, -1), users.reshape(1, -1), gate_table, normalizer.reshape(1, -1),
        forward_out, out_grad, history, lengths,
    )


def local(
    candidates,
    scenarios,
    candidate_user,
    gate_table,
    log_normalizer,
    forward_out,
    out_grad,
    history,
    history_length,
    history_items,
):
    feature_width = candidates.shape[1]
    seq_count = lax.axis_size("seq")
    data_count = lax.axis_size("dp")
    users_local, hist_local = history.shape[:2]
    candidate_grad, key_parts = attention(
        candidates, scenarios, candidate_user, gate_table, log_normalizer,
        forward_out, out_grad, history, history_length,
    )
    row_grads = key_parts.reshape(users_local * hist_local, feature_width)
    row_items = history_items.reshape(users_local * hist_local)
    devices = data_count * seq_count
    capacity = 2 * row_items.shape[0] // devices
    owner_ids = row_items // ITEM_DEV
    matches = (owner_ids[:, None] == jnp.arange(devices, dtype=jnp.int32)[None, :]).astype(
        jnp.int32
    )
    ranking = jnp.sum(jnp.cumsum(matches, axis=0) * matches, axis=1) - 1
    slot_index = owner_ids * capacity + ranking
    send_rows = (
        jnp.zeros((devices * capacity, feature_width), jnp.float32).at[slot_index].set(row_grads)
    )
    send_items = jnp.full((devices * capacity,), -1, jnp.int32).at[slot_index].set(row_items)
    got_rows, got_items = (
        lax.all_to_all(
            send_rows.reshape(devices, capacity, feature_width),
            ("dp", "seq"),
            split_axis=0,
            concat_axis=0,
            tiled=True,
        ),
        lax.all_to_all(
            send_items.reshape(devices, capacity),
            ("dp", "seq"),
            split_axis=0,
            concat_axis=0,
            tiled=True,
        ),
    )
    own_index = lax.axis_index("dp") * seq_count + lax.axis_index("seq")
    flat_items = got_items.reshape(devices * capacity)
    target = jnp.where(flat_items >= 0, flat_items - own_index * ITEM_DEV, ITEM_DEV)
    table_grad = (
        jnp.zeros((ITEM_DEV, feature_width), jnp.float32)
        .at[target]
        .add(got_rows.reshape(devices * capacity, feature_width), mode="drop")
    )
    return (candidate_grad, table_grad)


def solution(mesh):
    return jax.shard_map(
        local,
        mesh=mesh,
        in_specs=(
            P(("dp", "seq"), None),
            P(("dp", "seq")),
            P(("dp", "seq")),
            P(),
            P(("dp", "seq")),
            P(("dp", "seq"), None),
            P(("dp", "seq"), None),
            P("dp", "seq", None),
            P("dp"),
            P("dp", "seq"),
        ),
        out_specs=(P(("dp", "seq"), None), P(("dp", "seq"), None)),
        check_vma=False,
    )
```

```python
import math

import jax
import jax.numpy as jnp
from jax import lax
from jax.experimental import pallas as pl
from jax.experimental.pallas import tpu as pltpu
from jax.sharding import PartitionSpec as P

ITEM_DEV = 4096
MESH = pl.DeviceIdType.MESH

ORDER = [
    (0, 0), (0, 1), (0, 3), (1, 0), (3, 0), (0, 2), (2, 0),
    (1, 1), (1, 3), (3, 1), (3, 3), (1, 2), (3, 2), (2, 1), (2, 3), (2, 2),
]
SLOT = {offset: i for i, offset in enumerate(ORDER)}
QUARTERS = [(0, 128), (128, 128), (256, 128), (384, 144)]
BLOCK = 528
YP, YM, ZP, ZM = (1, 0), (-1, 0), (0, 1), (0, -1)


def forward_plan():
    plan = {i: [] for i in range(16)}

    def wait(step, offset, quarters):
        plan[step].append(("wait", offset, quarters))

    def send(step, offset, quarter, direction):
        plan[step].append(("send", offset, quarter, direction))

    a, b = (0, 1), (2, 3)
    for q in a:
        send(0, (0, 0), q, ZP)
        send(0, (0, 0), q, ZM)
    for q in b:
        send(0, (0, 0), q, YP)
        send(0, (0, 0), q, YM)
    for q in a:
        send(0, (0, 0), q, YP)
        send(0, (0, 0), q, YM)
    for q in b:
        send(0, (0, 0), q, ZP)
        send(0, (0, 0), q, ZM)
    for offset in ((0, 1), (0, 3)):
        wait(1, offset, a)
    for offset in ((1, 0), (3, 0)):
        wait(1, offset, b)
    send(1, (0, 3), 0, ZP)
    send(1, (0, 1), 1, ZM)
    send(1, (3, 0), 2, YP)
    send(1, (1, 0), 3, YM)
    for q in a:
        for offset in ((0, 1), (0, 3)):
            send(1, offset, q, YP)
            send(1, offset, q, YM)
    for q in b:
        for offset in ((1, 0), (3, 0)):
            send(1, offset, q, ZP)
            send(1, offset, q, ZM)
    for offset in ((0, 1), (0, 3)):
        wait(1, offset, b)
    for offset in ((1, 0), (3, 0)):
        wait(1, offset, a)
    send(1, (0, 3), 2, ZP)
    send(1, (0, 1), 3, ZM)
    send(1, (3, 0), 0, YP)
    send(1, (1, 0), 1, YM)
    wait(5, (0, 2), a)
    wait(5, (2, 0), b)
    for q in a:
        send(5, (0, 2), q, YP)
        send(5, (0, 2), q, YM)
    for q in b:
        send(5, (2, 0), q, ZP)
        send(5, (2, 0), q, ZM)
    wait(5, (0, 2), b)
    wait(5, (2, 0), a)
    for dz in (1, 3):
        wait(7, (3, dz), a)
        wait(7, (1, dz), a)
        send(7, (3, dz), 0, YP)
        send(7, (1, dz), 1, YM)
    for dy in (1, 3):
        wait(7, (dy, 3), b)
        wait(7, (dy, 1), b)
        send(7, (dy, 3), 2, ZP)
        send(7, (dy, 1), 3, ZM)
    wait(11, (3, 2), a)
    wait(11, (1, 2), a)
    send(11, (3, 2), 0, YP)
    send(11, (1, 2), 1, YM)
    wait(11, (2, 3), b)
    wait(11, (2, 1), b)
    send(11, (2, 3), 2, ZP)
    send(11, (2, 1), 3, ZM)
    wait(11, (1, 2), b)
    wait(11, (3, 2), b)
    wait(11, (2, 1), a)
    wait(11, (2, 3), a)
    wait(15, (2, 2), a + b)
    return plan


PLAN = forward_plan()
SENDS = [e for i in range(16) for e in PLAN[i] if e[0] == "send"]


def split3(x):
    hi = x.astype(jnp.bfloat16).astype(jnp.float32)
    rest = x - hi
    mid = rest.astype(jnp.bfloat16).astype(jnp.float32)
    return hi, mid, rest - mid


def nt(a, b):
    return lax.dot_general(a, b, (((1,), (1,)), ((), ())), preferred_element_type=jnp.float32)


def tn(a, b):
    return lax.dot_general(a, b, (((0,), (0,)), ((), ())), preferred_element_type=jnp.float32)


def power_of(top):
    power = jnp.ceil(jnp.log(jnp.maximum(top, 1e-33)) * (1.0 / math.log(2.0)))
    return jnp.clip(power, -110.0, 127.0)


def quantized(x):
    top = jnp.max(jnp.abs(x), axis=0, keepdims=True)
    power = power_of(top)
    q = jnp.round(x * (jnp.exp2(15.0 - power) * 0.99)).astype(jnp.int32)
    half = x.shape[0] // 2
    words = (q[half:] << 16) | (q[:half] & 0xFFFF)
    return words, jnp.broadcast_to(power.astype(jnp.int32), (8, x.shape[1]))


def restored(words, power):
    scale = jnp.exp2(power.astype(jnp.float32) - 15.0) * (1.0 / 0.99)
    low = ((words << 16) >> 16).astype(jnp.float32) * scale
    high = (words >> 16).astype(jnp.float32) * scale
    return low, high


def attention_kernel(
    cand_ref, scen_ref, user_ref, gate_ref, norm_ref, fwd_ref, grad_ref, hist_ref, item_ref, length_ref,
    cand_out, rows_in, codes_in,
    buf, keys, gates, total, part_out, part_in, hist_sum, matches, places_of, halves, rows_out, codes_out,
    send_sem, recv_sem, part_send, part_recv, rows_send, rows_recv, codes_send, codes_recv, own_sem,
):
    dp = lax.axis_index("dp")
    seq = lax.axis_index("seq")
    x, core = dp // 2, dp % 2
    y, z = seq // 4, seq % 4

    def owner_device(m):
        to_x = (x + m // 4 % 4) % 4
        to_core = (core + m // 64) % 2
        to_y = (y + m // 16 % 4) % 4
        to_z = (z + m % 4) % 4
        return (to_x * 2 + to_core, to_y * 4 + to_z)

    def device(dy, dz):
        return (dp, (y + dy + 4) % 4 * 4 + (z + dz + 4) % 4)

    barrier = pltpu.get_barrier_semaphore()

    def greet(m, carry):
        pl.semaphore_signal(barrier, inc=1, device_id=owner_device(m), device_id_type=MESH)
        return carry

    lax.fori_loop(1, 128, greet, 0)

    def block_copy(number):
        _, offset, quarter, (dy, dz) = SENDS[number]
        there = SLOT[(offset[0] - dy) % 4, (offset[1] - dz) % 4]
        rows = pl.ds(*QUARTERS[quarter])
        return pltpu.make_async_remote_copy(
            src_ref=buf.at[SLOT[offset], rows],
            dst_ref=buf.at[there, rows],
            send_sem=send_sem.at[number],
            recv_sem=recv_sem.at[there, quarter],
            device_id=device(dy, dz),
            device_id_type=MESH,
        )

    def block_arrival(offset, quarter):
        rows = pl.ds(*QUARTERS[quarter])
        slot = SLOT[offset]
        return pltpu.make_async_remote_copy(
            src_ref=buf.at[slot, rows],
            dst_ref=buf.at[slot, rows],
            send_sem=send_sem.at[0],
            recv_sem=recv_sem.at[slot, quarter],
            device_id=device(0, 1),
            device_id_type=MESH,
        )

    def part_copy(i):
        dy, dz = ORDER[i]
        there = SLOT[-dy % 4, -dz % 4]
        return pltpu.make_async_remote_copy(
            src_ref=part_out.at[i],
            dst_ref=part_in.at[there],
            send_sem=part_send.at[i],
            recv_sem=part_recv.at[there],
            device_id=device(dy, dz),
            device_id_type=MESH,
        )

    scen_rows = scen_ref[...] == lax.broadcasted_iota(jnp.int32, (16, 256), 0)
    gates[...] = lax.dot_general(
        scen_rows.astype(jnp.float32), gate_ref[...], (((0,), (0,)), ((), ())),
        precision=lax.Precision.HIGHEST, preferred_element_type=jnp.float32,
    )
    queries = (cand_ref[...].astype(jnp.float32) * gates[...]).astype(jnp.bfloat16)
    buf[0, 0:256] = queries * jnp.bfloat16(0.0625)
    grads = grad_ref[...]
    buf[0, 256:512] = grads
    inner = lax.dot_general(
        jnp.ones((8, 256), jnp.float32),
        grads.astype(jnp.float32) * fwd_ref[...].astype(jnp.float32),
        (((1,), (1,)), ((), ())),
        precision=lax.Precision.HIGHEST, preferred_element_type=jnp.float32,
    )[0:1]
    user = (user_ref[...] - 2 * dp).astype(jnp.float32)
    numbers = [*split3(norm_ref[...]), *split3(inner), 1.0 - user, user]
    numbers = jnp.concatenate(numbers + [jnp.zeros((8, 256), jnp.float32)], axis=0)
    buf[0, 512:528] = numbers.astype(jnp.bfloat16)

    pl.semaphore_wait(barrier, 127)

    def run_plan(step):
        for event in PLAN[step]:
            if event[0] == "wait":
                for quarter in event[2]:
                    block_arrival(event[1], quarter).wait_recv()
            else:
                block_copy(SENDS.index(event)).start()

    run_plan(0)

    first = seq * 512
    places = first + lax.broadcasted_iota(jnp.int32, (512, 256), 0)
    for u in range(2):
        rows = hist_ref[u].astype(jnp.float32)
        keys[u] = jnp.where(places < length_ref[u], rows, 0.0).astype(jnp.bfloat16)
    hist_sum[...] = jnp.zeros_like(hist_sum)
    items = item_ref[...]
    owner = items // ITEM_DEV
    other = [owner // 32, owner // 16 % 2, owner // 4 % 4, owner % 4]
    message = (other[1] + core) % 2 * 64 + (other[2] - y + 4) % 4 * 16 + (other[0] - x + 4) % 4 * 4
    message = message + (other[3] - z + 4) % 4
    found = lax.broadcasted_iota(jnp.int32, (128, 1024), 0) == message
    matches[...] = jnp.where(found, 1.0, 0.0)
    earlier = lax.broadcasted_iota(jnp.int32, (1024, 1024), 0) <= lax.broadcasted_iota(jnp.int32, (1024, 1024), 1)
    counts = jnp.dot(
        matches[...].astype(jnp.bfloat16), jnp.where(earlier, 1.0, 0.0).astype(jnp.bfloat16),
        preferred_element_type=jnp.float32,
    )
    rank = jnp.sum(matches[...] * counts, axis=0, keepdims=True).astype(jnp.int32) - 1
    places_of[0:1] = message * 16 + rank
    places_of[1:2] = rank
    places_of[2:3] = items % ITEM_DEV + 8

    def step(k, carry):
        for i in range(1, 16):
            if PLAN[i]:
                pl.when(k == i)(lambda i=i: run_plan(i))
        numbers = buf[k, 512:528].astype(jnp.float32)
        normalizer = numbers[0:1] + numbers[1:2] + numbers[2:3]
        inner_sum = numbers[3:4] + numbers[4:5] + numbers[5:6]
        pick = [numbers[6:7], numbers[7:8]]
        low = [w.astype(jnp.bfloat16) for w in pick]
        both = buf[k, 0:512]
        query_part = jnp.zeros((256, 256), jnp.float32)
        for c in range(2):
            rows = pl.ds(c * 256, 256)
            mine = keys[0, rows] * low[0] + keys[1, rows] * low[1]
            products = nt(mine, both)
            probability = jnp.exp(products[:, :256] - normalizer)
            score_grad = (probability * (products[:, 256:] - inner_sum)).astype(jnp.bfloat16)
            weights = jnp.concatenate([score_grad, probability.astype(jnp.bfloat16)], axis=1)
            key_part = jnp.dot(weights, both, preferred_element_type=jnp.float32)
            hist_sum[0, rows] += key_part * pick[0]
            hist_sum[1, rows] += key_part * pick[1]
            query_part += tn(score_grad, mine)

        @pl.when(k == 0)
        def _():
            total[...] = query_part

        @pl.when(k > 0)
        def _():
            words, power = quantized(query_part)
            part_out[k, 0:128] = words
            part_out[k, 128:136] = power

        for i in range(1, 16):
            pl.when(k == i)(lambda i=i: part_copy(i).start())
        return carry

    lax.fori_loop(0, 16, step, 0)

    first_lane = lax.broadcasted_iota(jnp.int32, (512, 128), 1) == 0
    powers = []
    for u in range(2):
        grads = jnp.where(places < length_ref[u], hist_sum[u], 0.0)
        power = power_of(jnp.max(jnp.abs(grads), axis=1, keepdims=True))
        q = jnp.round(grads * (jnp.exp2(15.0 - power) * 0.99)).astype(jnp.int32)
        rows = pl.ds(u * 512, 512)
        halves[rows, 0:256] = (q >> 8).astype(jnp.float32).astype(jnp.bfloat16)
        halves[rows, 256:512] = (q & 255).astype(jnp.float32).astype(jnp.bfloat16)
        powers.append(nt(jnp.ones((8, 128), jnp.bfloat16), jnp.where(first_lane, power, 0.0).astype(jnp.bfloat16))[0:1])
    codes = (jnp.concatenate(powers, axis=1) + 128.0) * 8192.0 + places_of[2:3].astype(jnp.float32)
    ranked = lax.broadcasted_iota(jnp.int32, (128, 1024), 0) == places_of[1:2]
    codes = lax.dot_general(
        matches[...], jnp.where(ranked, codes, 0.0), (((1,), (1,)), ((), ())),
        precision=lax.Precision.HIGHEST, preferred_element_type=jnp.float32,
    )
    codes_out[...] = codes.astype(jnp.int32).reshape(128, 1, 128)

    def rows_copy(m):
        return pltpu.make_async_remote_copy(
            src_ref=rows_out.at[m], dst_ref=rows_in.at[m], send_sem=rows_send, recv_sem=rows_recv,
            device_id=owner_device(m), device_id_type=MESH,
        )

    def codes_copy(m):
        return pltpu.make_async_remote_copy(
            src_ref=codes_out.at[m], dst_ref=codes_in.at[m], send_sem=codes_send, recv_sem=codes_recv,
            device_id=owner_device(m), device_id_type=MESH,
        )

    own_rows = pltpu.make_async_copy(rows_out.at[0], rows_in.at[0], own_sem.at[0])
    own_codes = pltpu.make_async_copy(codes_out.at[0], codes_in.at[0], own_sem.at[1])

    def send_chunk(c, carry):
        slots = lax.broadcasted_iota(jnp.int32, (256, 1024), 0) + c * 256
        chosen = jnp.where(slots == places_of[0:1], 1.0, 0.0).astype(jnp.bfloat16)
        moved = jnp.dot(chosen, halves[...], preferred_element_type=jnp.float32).astype(jnp.int32)
        value = (moved[:, 0:256] << 8) + moved[:, 256:512]
        words = (value[:, 128:256] << 16) | (value[:, 0:128] & 0xFFFF)
        rows_out[pl.ds(c * 16, 16)] = words.reshape(16, 16, 128)

        def send_one(j, carry):
            m = c * 16 + j

            @pl.when(m > 0)
            def _():
                rows_copy(m).start()
                codes_copy(m).start()

            return carry

        lax.fori_loop(0, 16, send_one, 0)
        return carry

    lax.fori_loop(0, 8, send_chunk, 0)
    own_rows.start()
    own_codes.start()

    for i in range(1, 16):
        pltpu.make_async_remote_copy(
            src_ref=part_out.at[i],
            dst_ref=part_in.at[i],
            send_sem=part_send.at[i],
            recv_sem=part_recv.at[i],
            device_id=device(0, 1),
            device_id_type=MESH,
        ).wait_recv()

    low, high = total[0:128], total[128:256]
    for i in range(1, 16):
        a, b = restored(part_in[i, 0:128], part_in[i, 128:129])
        low, high = low + a, high + b
    cand_out[0:128] = low * 0.0625 * gates[0:128]
    cand_out[128:256] = high * 0.0625 * gates[128:256]
    for number in range(len(SENDS)):
        block_copy(number).wait_send()
    for i in range(1, 16):
        part_copy(i).wait_send()
    own_rows.wait()
    own_codes.wait()
    others = pl.ds(1, 127)
    all_rows = pltpu.make_async_remote_copy(
        src_ref=rows_out.at[others], dst_ref=rows_in.at[others], send_sem=rows_send, recv_sem=rows_recv,
        device_id=owner_device(1), device_id_type=MESH,
    )
    all_codes = pltpu.make_async_remote_copy(
        src_ref=codes_out.at[others], dst_ref=codes_in.at[others], send_sem=codes_send, recv_sem=codes_recv,
        device_id=owner_device(1), device_id_type=MESH,
    )
    all_rows.wait()
    all_codes.wait()


def table_kernel(rows_ref, codes_ref, scale_ref, table_out, values, t0, t1, t2, t3, sem):
    tables = (t0, t1, t2, t3)

    def clear(c, carry):
        for t in tables:
            t[pl.ds(c * 512, 512)] = jnp.zeros((512, 256), jnp.float32)
        return carry

    lax.fori_loop(0, 8, clear, 0)
    for t in tables:
        t[4096:4104] = jnp.zeros((8, 256), jnp.float32)

    def unpack(c, carry):
        rows = pl.ds(c * 256, 256)
        words = rows_ref[rows]
        values[rows, 0:128] = ((words << 16) >> 16).astype(jnp.float32)
        values[rows, 128:256] = (words >> 16).astype(jnp.float32)
        return carry

    lax.fori_loop(0, 8, unpack, 0)

    def add_message(m, carry):
        for j in range(16):
            code = codes_ref[m, j]
            place = pl.ds(code & 8191, 1)
            table = tables[j % 4]
            table[place] = table[place] + values[pl.ds(m * 16 + j, 1)] * scale_ref[code >> 13]
        return carry

    lax.fori_loop(0, 128, add_message, 0)

    def out_copy(c):
        return pltpu.make_async_copy(
            t0.at[pl.ds(8 + c * 512, 512)], table_out.at[pl.ds(c * 512, 512)], sem.at[c]
        )

    def finish(c, carry):
        rows = pl.ds(8 + c * 512, 512)
        t0[rows] = (t0[rows] + t1[rows]) + (t2[rows] + t3[rows])
        out_copy(c).start()
        return carry

    lax.fori_loop(0, 8, finish, 0)
    for c in range(8):
        out_copy(c).wait()


def add_rows(rows, codes):
    scales = jnp.exp2(jnp.arange(256, dtype=jnp.float32) - (128.0 + 15.0)) / 0.99
    smem = pl.BlockSpec(memory_space=pltpu.SMEM)
    return pl.pallas_call(
        table_kernel,
        out_shape=jax.ShapeDtypeStruct((ITEM_DEV, 256), jnp.float32),
        in_specs=[pl.BlockSpec(memory_space=pltpu.VMEM), smem, smem],
        out_specs=pl.BlockSpec(memory_space=pl.ANY),
        scratch_shapes=[pltpu.VMEM((2048, 256), jnp.float32)]
        + [pltpu.VMEM((ITEM_DEV + 8, 256), jnp.float32)] * 4
        + [pltpu.SemaphoreType.DMA((8,))],
        compiler_params=pltpu.CompilerParams(vmem_limit_bytes=40 * 1024 * 1024),
        cost_estimate=pl.CostEstimate(flops=2_000_000, bytes_accessed=5_500_000, transcendentals=0),
        name="table_rows",
    )(rows, codes, scales)


def attention(candidates, scenarios, users, gate_table, normalizer, forward_out, out_grad, history, items, lengths):
    vmem = pl.BlockSpec(memory_space=pltpu.VMEM)
    return pl.pallas_call(
        attention_kernel,
        out_shape=(
            jax.ShapeDtypeStruct((256, 256), jnp.float32),
            jax.ShapeDtypeStruct((128, 16, 128), jnp.int32),
            jax.ShapeDtypeStruct((128, 1, 128), jnp.int32),
        ),
        in_specs=[vmem] * 9 + [pl.BlockSpec(memory_space=pltpu.SMEM)],
        out_specs=(vmem, pl.BlockSpec(memory_space=pl.ANY), pl.BlockSpec(memory_space=pl.ANY)),
        scratch_shapes=[
            pltpu.VMEM((16, BLOCK, 256), jnp.bfloat16),
            pltpu.VMEM((2, 512, 256), jnp.bfloat16),
            pltpu.VMEM((256, 256), jnp.float32),
            pltpu.VMEM((256, 256), jnp.float32),
            pltpu.VMEM((16, 136, 256), jnp.int32),
            pltpu.VMEM((16, 136, 256), jnp.int32),
            pltpu.VMEM((2, 512, 256), jnp.float32),
            pltpu.VMEM((128, 1024), jnp.float32),
            pltpu.VMEM((8, 1024), jnp.int32),
            pltpu.VMEM((1024, 512), jnp.bfloat16),
            pltpu.VMEM((128, 16, 128), jnp.int32),
            pltpu.VMEM((128, 1, 128), jnp.int32),
            pltpu.SemaphoreType.DMA((len(SENDS),)),
            pltpu.SemaphoreType.DMA((16, 4)),
            pltpu.SemaphoreType.DMA((16,)),
            pltpu.SemaphoreType.DMA((16,)),
            pltpu.SemaphoreType.DMA,
            pltpu.SemaphoreType.DMA,
            pltpu.SemaphoreType.DMA,
            pltpu.SemaphoreType.DMA,
            pltpu.SemaphoreType.DMA((2,)),
        ],
        compiler_params=pltpu.CompilerParams(
            collective_id=0, has_side_effects=True, vmem_limit_bytes=48 * 1024 * 1024
        ),
        cost_estimate=pl.CostEstimate(
            flops=5_400_000_000, bytes_accessed=4_000_000, transcendentals=2_100_000
        ),
        name="attention_grads",
    )(
        candidates, scenarios.reshape(1, -1), users.reshape(1, -1), gate_table, normalizer.reshape(1, -1),
        forward_out, out_grad, history, items.reshape(1, -1), lengths,
    )


def local(
    candidates,
    scenarios,
    candidate_user,
    gate_table,
    log_normalizer,
    forward_out,
    out_grad,
    history,
    history_length,
    history_items,
):
    candidate_grad, rows, codes = attention(
        candidates, scenarios, candidate_user, gate_table, log_normalizer,
        forward_out, out_grad, history, history_items, history_length,
    )
    table_grad = add_rows(rows.reshape(2048, 128), codes.reshape(128, 128))
    return (candidate_grad, table_grad)


def solution(mesh):
    return jax.shard_map(
        local,
        mesh=mesh,
        in_specs=(
            P(("dp", "seq"), None),
            P(("dp", "seq")),
            P(("dp", "seq")),
            P(),
            P(("dp", "seq")),
            P(("dp", "seq"), None),
            P(("dp", "seq"), None),
            P("dp", "seq", None),
            P("dp"),
            P("dp", "seq"),
        ),
        out_specs=(P(("dp", "seq"), None), P(("dp", "seq"), None)),
        check_vma=False,
    )
```

```python
import math

import jax
import jax.numpy as jnp
from jax import lax
from jax.experimental import pallas as pl
from jax.experimental.pallas import tpu as pltpu
from jax.sharding import PartitionSpec as P

ITEM_DEV = 4096
MESH = pl.DeviceIdType.MESH

ORDER = [
    (0, 0), (0, 1), (0, 3), (1, 0), (3, 0), (0, 2), (2, 0),
    (1, 1), (1, 3), (3, 1), (3, 3), (1, 2), (3, 2), (2, 1), (2, 3), (2, 2),
]
SLOT = {offset: i for i, offset in enumerate(ORDER)}
QUARTERS = [(0, 128), (128, 128), (256, 128), (384, 144)]
BLOCK = 528
YP, YM, ZP, ZM = (1, 0), (-1, 0), (0, 1), (0, -1)


def forward_plan():
    plan = {i: [] for i in range(16)}

    def wait(step, offset, quarters):
        plan[step].append(("wait", offset, quarters))

    def send(step, offset, quarter, direction):
        plan[step].append(("send", offset, quarter, direction))

    a, b = (0, 1), (2, 3)
    for q in a:
        send(0, (0, 0), q, ZP)
        send(0, (0, 0), q, ZM)
    for q in b:
        send(0, (0, 0), q, YP)
        send(0, (0, 0), q, YM)
    for q in a:
        send(0, (0, 0), q, YP)
        send(0, (0, 0), q, YM)
    for q in b:
        send(0, (0, 0), q, ZP)
        send(0, (0, 0), q, ZM)
    for offset in ((0, 1), (0, 3)):
        wait(1, offset, a)
    for offset in ((1, 0), (3, 0)):
        wait(1, offset, b)
    send(1, (0, 3), 0, ZP)
    send(1, (0, 1), 1, ZM)
    send(1, (3, 0), 2, YP)
    send(1, (1, 0), 3, YM)
    for q in a:
        for offset in ((0, 1), (0, 3)):
            send(1, offset, q, YP)
            send(1, offset, q, YM)
    for q in b:
        for offset in ((1, 0), (3, 0)):
            send(1, offset, q, ZP)
            send(1, offset, q, ZM)
    for offset in ((0, 1), (0, 3)):
        wait(1, offset, b)
    for offset in ((1, 0), (3, 0)):
        wait(1, offset, a)
    send(1, (0, 3), 2, ZP)
    send(1, (0, 1), 3, ZM)
    send(1, (3, 0), 0, YP)
    send(1, (1, 0), 1, YM)
    wait(5, (0, 2), a)
    wait(5, (2, 0), b)
    for q in a:
        send(5, (0, 2), q, YP)
        send(5, (0, 2), q, YM)
    for q in b:
        send(5, (2, 0), q, ZP)
        send(5, (2, 0), q, ZM)
    wait(5, (0, 2), b)
    wait(5, (2, 0), a)
    for dz in (1, 3):
        wait(7, (3, dz), a)
        wait(7, (1, dz), a)
        send(7, (3, dz), 0, YP)
        send(7, (1, dz), 1, YM)
    for dy in (1, 3):
        wait(7, (dy, 3), b)
        wait(7, (dy, 1), b)
        send(7, (dy, 3), 2, ZP)
        send(7, (dy, 1), 3, ZM)
    wait(11, (3, 2), a)
    wait(11, (1, 2), a)
    send(11, (3, 2), 0, YP)
    send(11, (1, 2), 1, YM)
    wait(11, (2, 3), b)
    wait(11, (2, 1), b)
    send(11, (2, 3), 2, ZP)
    send(11, (2, 1), 3, ZM)
    wait(11, (1, 2), b)
    wait(11, (3, 2), b)
    wait(11, (2, 1), a)
    wait(11, (2, 3), a)
    wait(15, (2, 2), a + b)
    return plan


PLAN = forward_plan()
SENDS = [e for i in range(16) for e in PLAN[i] if e[0] == "send"]


def split3(x):
    hi = x.astype(jnp.bfloat16).astype(jnp.float32)
    rest = x - hi
    mid = rest.astype(jnp.bfloat16).astype(jnp.float32)
    return hi, mid, rest - mid


def nt(a, b):
    return lax.dot_general(a, b, (((1,), (1,)), ((), ())), preferred_element_type=jnp.float32)


def tn(a, b):
    return lax.dot_general(a, b, (((0,), (0,)), ((), ())), preferred_element_type=jnp.float32)


def power_of(top):
    power = jnp.ceil(jnp.log(jnp.maximum(top, 1e-33)) * (1.0 / math.log(2.0)))
    return jnp.clip(power, -110.0, 127.0)


def quantized(x):
    top = jnp.max(jnp.abs(x), axis=0, keepdims=True)
    power = power_of(top)
    q = jnp.round(x * (jnp.exp2(15.0 - power) * 0.99)).astype(jnp.int32)
    half = x.shape[0] // 2
    words = (q[half:] << 16) | (q[:half] & 0xFFFF)
    return words, jnp.broadcast_to(power.astype(jnp.int32), (8, x.shape[1]))


def restored(words, power):
    scale = jnp.exp2(power.astype(jnp.float32) - 15.0) * (1.0 / 0.99)
    low = ((words << 16) >> 16).astype(jnp.float32) * scale
    high = (words >> 16).astype(jnp.float32) * scale
    return low, high


def attention_kernel(
    cand_hbm, scen_hbm, user_hbm, gate_hbm, norm_hbm, fwd_hbm, grad_hbm, hist_hbm, item_hbm, length_hbm,
    cand_out, rows_in, codes_in,
    cand_ref, scen_ref, user_ref, gate_ref, norm_ref, fwd_ref, grad_ref, hist_ref, item_ref, length_ref,
    buf, keys, gates, part_out, part_in, sums_out, sums_in, hist_sum, matches, places_of, halves, rows_out, codes_out,
    load_sem, send_sem, recv_sem, part_send, part_recv, sums_send, sums_recv,
    rows_send, rows_recv, codes_send, codes_recv, own_sem,
):
    loads = [
        pltpu.make_async_copy(there, here, load_sem.at[i])
        for i, (there, here) in enumerate([
            (scen_hbm, scen_ref), (gate_hbm, gate_ref), (user_hbm, user_ref), (norm_hbm, norm_ref),
            (cand_hbm, cand_ref), (grad_hbm, grad_ref), (fwd_hbm, fwd_ref),
            (hist_hbm, hist_ref), (length_hbm, length_ref), (item_hbm, item_ref),
        ])
    ]
    for load in loads:
        load.start()

    dp = lax.axis_index("dp")
    seq = lax.axis_index("seq")
    x, core = dp // 2, dp % 2
    y, z = seq // 4, seq % 4

    xs = [(x + d) % 4 for d in range(4)]
    ys = [(y + d) % 4 for d in range(4)]
    zs = [(z + d) % 4 for d in range(4)]
    cores = [core, 1 - core]

    def device(dy, dz):
        return (dp, ys[dy % 4] * 4 + zs[dz % 4])

    barrier = pltpu.get_barrier_semaphore()

    for m in range(1, 128):
        there = (xs[m // 4 % 4] * 2 + cores[m // 64], ys[m // 16 % 4] * 4 + zs[m % 4])
        pl.semaphore_signal(barrier, inc=1, device_id=there, device_id_type=MESH)

    def block_copy(number):
        _, offset, quarter, (dy, dz) = SENDS[number]
        there = SLOT[(offset[0] - dy) % 4, (offset[1] - dz) % 4]
        rows = pl.ds(*QUARTERS[quarter])
        return pltpu.make_async_remote_copy(
            src_ref=buf.at[SLOT[offset], rows],
            dst_ref=buf.at[there, rows],
            send_sem=send_sem.at[number],
            recv_sem=recv_sem.at[there, quarter],
            device_id=device(dy, dz),
            device_id_type=MESH,
        )

    def block_arrival(offset, quarter):
        rows = pl.ds(*QUARTERS[quarter])
        slot = SLOT[offset]
        return pltpu.make_async_remote_copy(
            src_ref=buf.at[slot, rows],
            dst_ref=buf.at[slot, rows],
            send_sem=send_sem.at[0],
            recv_sem=recv_sem.at[slot, quarter],
            device_id=device(0, 1),
            device_id_type=MESH,
        )

    def part_copy(i, half):
        dy, dz = ORDER[i]
        step, across = (dz, dy) if half == 0 else (dy, dz)
        there = part_in.at[half, 3 - step, across]
        return pltpu.make_async_remote_copy(
            src_ref=part_out.at[i, half],
            dst_ref=there,
            send_sem=part_send.at[i, half],
            recv_sem=part_recv.at[half, 3 - step, across],
            device_id=device(0, step) if half == 0 else device(step, 0),
            device_id_type=MESH,
        )

    parts = [(i, h) for i in range(1, 16) for h in range(2) if ORDER[i][1 - h]]

    def sums_copy(half, step):
        return pltpu.make_async_remote_copy(
            src_ref=sums_out.at[half, step - 1],
            dst_ref=sums_in.at[half, 3 - step],
            send_sem=sums_send.at[half, step - 1],
            recv_sem=sums_recv.at[half, 3 - step],
            device_id=device(step, 0) if half == 0 else device(0, step),
            device_id_type=MESH,
        )

    for load in loads[:7]:
        load.wait()
    scen_rows = scen_ref[...] == lax.broadcasted_iota(jnp.int32, (16, 256), 0)
    gates[...] = lax.dot_general(
        scen_rows.astype(jnp.float32), gate_ref[...], (((0,), (0,)), ((), ())),
        precision=lax.Precision.HIGHEST, preferred_element_type=jnp.float32,
    )
    queries = (cand_ref[...].astype(jnp.float32) * gates[...]).astype(jnp.bfloat16)
    buf[0, 0:256] = queries * jnp.bfloat16(0.0625)
    grads = grad_ref[...]
    buf[0, 256:512] = grads
    inner = lax.dot_general(
        jnp.ones((8, 256), jnp.float32),
        grads.astype(jnp.float32) * fwd_ref[...].astype(jnp.float32),
        (((1,), (1,)), ((), ())),
        precision=lax.Precision.HIGHEST, preferred_element_type=jnp.float32,
    )[0:1]
    user = (user_ref[...] - 2 * dp).astype(jnp.float32)
    numbers = [*split3(norm_ref[...]), *split3(inner), 1.0 - user, user]
    numbers = jnp.concatenate(numbers + [jnp.zeros((8, 256), jnp.float32)], axis=0)
    buf[0, 512:528] = numbers.astype(jnp.bfloat16)

    pl.semaphore_wait(barrier, 127)

    def run_plan(step):
        for event in PLAN[step]:
            if event[0] == "wait":
                for quarter in event[2]:
                    block_arrival(event[1], quarter).wait_recv()
            else:
                block_copy(SENDS.index(event)).start()

    run_plan(0)

    first = seq * 512
    places = first + lax.broadcasted_iota(jnp.int32, (512, 256), 0)
    for load in loads[7:]:
        load.wait()
    for u in range(2):
        rows = hist_ref[u].astype(jnp.float32)
        keys[u] = jnp.where(places < length_ref[u], rows, 0.0).astype(jnp.bfloat16)
    hist_sum[...] = jnp.zeros_like(hist_sum)
    def rank_items():
        items = jnp.concatenate([item_ref[0:1], item_ref[1:2]], axis=1)
        owner = items // ITEM_DEV
        other = [owner // 32, owner // 16 % 2, owner // 4 % 4, owner % 4]
        message = (other[1] + core) % 2 * 64 + (other[2] - y + 4) % 4 * 16 + (other[0] - x + 4) % 4 * 4
        message = message + (other[3] - z + 4) % 4
        found = lax.broadcasted_iota(jnp.int32, (128, 1024), 0) == message
        matches[...] = jnp.where(found, 1.0, 0.0)
        earlier = lax.broadcasted_iota(jnp.int32, (1024, 1024), 0) <= lax.broadcasted_iota(jnp.int32, (1024, 1024), 1)
        counts = jnp.dot(
            matches[...].astype(jnp.bfloat16), jnp.where(earlier, 1.0, 0.0).astype(jnp.bfloat16),
            preferred_element_type=jnp.float32,
        )
        rank = jnp.sum(matches[...] * counts, axis=0, keepdims=True).astype(jnp.int32) - 1
        places_of[0:1] = message * 16 + rank
        places_of[1:2] = rank
        places_of[2:3] = items % ITEM_DEV + 8

    def step(k, carry):
        for i in range(1, 16):
            if PLAN[i]:
                pl.when(k == i)(lambda i=i: run_plan(i))
        numbers = buf[k, 512:528].astype(jnp.float32)
        normalizer = numbers[0:1] + numbers[1:2] + numbers[2:3]
        inner_sum = numbers[3:4] + numbers[4:5] + numbers[5:6]
        pick = [numbers[6:7], numbers[7:8]]
        low = [w.astype(jnp.bfloat16) for w in pick]
        both = buf[k, 0:512]
        query_part = jnp.zeros((256, 256), jnp.float32)
        for c in range(2):
            rows = pl.ds(c * 256, 256)
            mine = keys[0, rows] * low[0] + keys[1, rows] * low[1]
            products = nt(mine, both)
            probability = jnp.exp(products[:, :256] - normalizer)
            score_grad = (probability * (products[:, 256:] - inner_sum)).astype(jnp.bfloat16)
            weights = jnp.concatenate([score_grad, probability.astype(jnp.bfloat16)], axis=1)
            key_part = jnp.dot(weights, both, preferred_element_type=jnp.float32)
            hist_sum[0, rows] += key_part * pick[0]
            hist_sum[1, rows] += key_part * pick[1]
            query_part += tn(score_grad, mine)

        words, power = quantized(query_part)
        for h in range(2):
            columns = slice(h * 128, (h + 1) * 128)
            part_out[k, h, 0:128] = words[:, columns]
            part_out[k, h, 128:136] = power[:, columns]
        for i in range(1, 16):

            @pl.when(k == i)
            def _(i=i):
                for h in range(2):
                    if (i, h) in parts:
                        part_copy(i, h).start()

        pl.when(k == 6)(rank_items)
        return carry

    lax.fori_loop(0, 16, step, 0)

    first_lane = lax.broadcasted_iota(jnp.int32, (512, 128), 1) == 0
    powers = []
    for u in range(2):
        grads = jnp.where(places < length_ref[u], hist_sum[u], 0.0)
        power = power_of(jnp.max(jnp.abs(grads), axis=1, keepdims=True))
        q = jnp.round(grads * (jnp.exp2(15.0 - power) * 0.99)).astype(jnp.int32)
        rows = pl.ds(u * 512, 512)
        halves[rows, 0:256] = (q >> 8).astype(jnp.float32).astype(jnp.bfloat16)
        halves[rows, 256:512] = (q & 255).astype(jnp.float32).astype(jnp.bfloat16)
        powers.append(nt(jnp.ones((8, 128), jnp.bfloat16), jnp.where(first_lane, power, 0.0).astype(jnp.bfloat16))[0:1])
    column = lax.broadcasted_iota(jnp.int32, (128, 1024), 0)
    codes = jnp.where(column < 16, places_of[2:3].astype(jnp.float32), jnp.concatenate(powers, axis=1) + 128.0)
    ranked = (column % 16 == places_of[1:2]) & (column < 32)
    codes = lax.dot_general(
        matches[...], jnp.where(ranked, codes, 0.0), (((1,), (1,)), ((), ())),
        precision=lax.Precision.HIGHEST, preferred_element_type=jnp.float32,
    )
    codes_out[...] = codes.astype(jnp.int32).reshape(128, 1, 128)

    def rows_copy(m, there):
        return pltpu.make_async_remote_copy(
            src_ref=rows_out.at[m], dst_ref=rows_in.at[m], send_sem=rows_send, recv_sem=rows_recv,
            device_id=there, device_id_type=MESH,
        )

    def codes_copy(m, there):
        return pltpu.make_async_remote_copy(
            src_ref=codes_out.at[m], dst_ref=codes_in.at[m], send_sem=codes_send, recv_sem=codes_recv,
            device_id=there, device_id_type=MESH,
        )

    own_rows = pltpu.make_async_copy(rows_out.at[0], rows_in.at[0], own_sem.at[0])
    own_codes = pltpu.make_async_copy(codes_out.at[0], codes_in.at[0], own_sem.at[1])

    def send_chunk(c, carry):
        slots = lax.broadcasted_iota(jnp.int32, (256, 1024), 0) + c * 256
        chosen = jnp.where(slots == places_of[0:1], 1.0, 0.0).astype(jnp.bfloat16)
        moved = jnp.dot(chosen, halves[...], preferred_element_type=jnp.float32).astype(jnp.int32)
        value = (moved[:, 0:256] << 8) + moved[:, 256:512]
        words = (value[:, 128:256] << 16) | (value[:, 0:128] & 0xFFFF)
        rows_out[pl.ds(c * 16, 16)] = words.reshape(16, 16, 128)

        to_core = (core + c // 4) % 2
        to_y = (y + c % 4) % 4
        for j in range(16):
            m = c * 16 + j
            there = (xs[j // 4] * 2 + to_core, to_y * 4 + zs[j % 4])

            def send_one(m=m, there=there):
                rows_copy(m, there).start()
                codes_copy(m, there).start()

            if j == 0:
                pl.when(c > 0)(send_one)
            else:
                send_one()
        return carry

    lax.fori_loop(0, 8, send_chunk, 0)
    own_rows.start()
    own_codes.start()

    for i, h in parts:
        part_copy(i, h).wait_recv()
    firsts = []
    for h in range(2):
        for d in range(4):
            own = SLOT[(d, 0) if h == 0 else (0, d)]
            low, high = restored(part_out[own, h, 0:128], part_out[own, h, 128:129])
            for source in range(3):
                a, b = restored(part_in[h, source, d, 0:128], part_in[h, source, d, 128:129])
                low, high = low + a, high + b
            if d == 0:
                firsts.append((low, high))
            else:
                words, power = quantized(jnp.concatenate([low, high], axis=0))
                sums_out[h, d - 1, 0:128] = words
                sums_out[h, d - 1, 128:136] = power
                sums_copy(h, d).start()
    for h in range(2):
        low, high = firsts[h]
        for d in range(1, 4):
            sums_copy(h, d).wait_recv()
        for source in range(3):
            a, b = restored(sums_in[h, source, 0:128], sums_in[h, source, 128:129])
            low, high = low + a, high + b
        columns = slice(h * 128, (h + 1) * 128)
        cand_out[0:128, columns] = low * 0.0625 * gates[0:128, columns]
        cand_out[128:256, columns] = high * 0.0625 * gates[128:256, columns]
    for number in range(len(SENDS)):
        block_copy(number).wait_send()
    for i, h in parts:
        part_copy(i, h).wait_send()
    for h in range(2):
        for d in range(1, 4):
            sums_copy(h, d).wait_send()
    own_rows.wait()
    own_codes.wait()
    others = pl.ds(1, 127)
    all_rows = pltpu.make_async_remote_copy(
        src_ref=rows_out.at[others], dst_ref=rows_in.at[others], send_sem=rows_send, recv_sem=rows_recv,
        device_id=device(0, 1), device_id_type=MESH,
    )
    all_codes = pltpu.make_async_remote_copy(
        src_ref=codes_out.at[others], dst_ref=codes_in.at[others], send_sem=codes_send, recv_sem=codes_recv,
        device_id=device(0, 1), device_id_type=MESH,
    )
    all_rows.wait()
    all_codes.wait()


def table_kernel(
    rows_hbm, codes_hbm, cand_hbm, table_out, cand_out, rows_ref, codes_ref, powers_ref, cand_ref, values, t0, t1, t2, t3, sem
):
    tables = (t0, t1, t2, t3)
    loads = [
        pltpu.make_async_copy(codes_hbm, codes_ref, sem.at[9]),
        pltpu.make_async_copy(codes_hbm, powers_ref, sem.at[10]),
        pltpu.make_async_copy(rows_hbm, rows_ref, sem.at[11]),
        pltpu.make_async_copy(cand_hbm, cand_ref, sem.at[12]),
    ]
    for load in loads:
        load.start()
    cand_copy = pltpu.make_async_copy(cand_ref, cand_out, sem.at[8])

    def clear(c, carry):
        for t in tables:
            t[pl.ds(c * 512, 512)] = jnp.zeros((512, 256), jnp.float32)
        return carry

    lax.fori_loop(0, 8, clear, 0)
    for t in tables:
        t[4096:4104] = jnp.zeros((8, 256), jnp.float32)

    for load in loads:
        load.wait()
    cand_copy.start()
    powers = jnp.transpose(powers_ref[...].astype(jnp.float32))[16:32]
    scales = jnp.exp2(powers - 143.0) * (1.0 / 0.99)
    for m in range(128):
        scale = scales[:, m : m + 1]
        rows = slice(m * 16, m * 16 + 16)
        words = rows_ref[rows]
        values[rows, 0:128] = ((words << 16) >> 16).astype(jnp.float32) * scale
        values[rows, 128:256] = (words >> 16).astype(jnp.float32) * scale

    def add_message(m, carry):
        for j in range(0, 16, 4):
            places = [pl.ds(codes_ref[m, j + i], 1) for i in range(4)]
            sums = [tables[i][places[i]] + values[pl.ds(m * 16 + j + i, 1)] for i in range(4)]
            for i in range(4):
                tables[i][places[i]] = sums[i]
        return carry

    lax.fori_loop(0, 128, add_message, 0)

    def out_copy(c):
        return pltpu.make_async_copy(
            t0.at[pl.ds(8 + c * 512, 512)], table_out.at[pl.ds(c * 512, 512)], sem.at[c]
        )

    def finish(c, carry):
        rows = pl.ds(8 + c * 512, 512)
        t0[rows] = (t0[rows] + t1[rows]) + (t2[rows] + t3[rows])
        out_copy(c).start()
        return carry

    lax.fori_loop(0, 8, finish, 0)
    for c in range(8):
        out_copy(c).wait()
    cand_copy.wait()


def add_rows(rows, codes, candidate_grad):
    hbm = pl.BlockSpec(memory_space=pltpu.HBM)
    return pl.pallas_call(
        table_kernel,
        out_shape=(
            jax.ShapeDtypeStruct((ITEM_DEV, 256), jnp.float32),
            jax.ShapeDtypeStruct((256, 256), jnp.float32),
        ),
        in_specs=[hbm, hbm, hbm],
        out_specs=(hbm, hbm),
        scratch_shapes=[
            pltpu.VMEM((2048, 128), jnp.int32),
            pltpu.SMEM((128, 128), jnp.int32),
            pltpu.VMEM((128, 128), jnp.int32),
            pltpu.VMEM((256, 256), jnp.float32),
            pltpu.VMEM((2048, 256), jnp.float32),
        ]
        + [pltpu.VMEM((ITEM_DEV + 8, 256), jnp.float32)] * 4
        + [pltpu.SemaphoreType.DMA((13,))],
        compiler_params=pltpu.CompilerParams(vmem_limit_bytes=64 * 1024 * 1024),
        cost_estimate=pl.CostEstimate(flops=2_000_000, bytes_accessed=5_500_000, transcendentals=0),
        name="table_rows",
    )(rows, codes, candidate_grad)


def attention(candidates, scenarios, users, gate_table, normalizer, forward_out, out_grad, history, items, lengths):
    vmem = pl.BlockSpec(memory_space=pltpu.VMEM)
    return pl.pallas_call(
        attention_kernel,
        out_shape=(
            jax.ShapeDtypeStruct((256, 256), jnp.float32),
            jax.ShapeDtypeStruct((128, 16, 128), jnp.int32),
            jax.ShapeDtypeStruct((128, 1, 128), jnp.int32),
        ),
        in_specs=[pl.BlockSpec(memory_space=pltpu.HBM)] * 10,
        out_specs=(vmem, pl.BlockSpec(memory_space=pl.ANY), pl.BlockSpec(memory_space=pl.ANY)),
        scratch_shapes=[
            pltpu.VMEM((256, 256), jnp.bfloat16),
            pltpu.VMEM((1, 256), jnp.int32),
            pltpu.VMEM((1, 256), jnp.int32),
            pltpu.VMEM((16, 256), jnp.float32),
            pltpu.VMEM((1, 256), jnp.float32),
            pltpu.VMEM((256, 256), jnp.bfloat16),
            pltpu.VMEM((256, 256), jnp.bfloat16),
            pltpu.VMEM((2, 512, 256), jnp.bfloat16),
            pltpu.VMEM((2, 512), jnp.int32),
            pltpu.SMEM((2,), jnp.int32),
            pltpu.VMEM((16, BLOCK, 256), jnp.bfloat16),
            pltpu.VMEM((2, 512, 256), jnp.bfloat16),
            pltpu.VMEM((256, 256), jnp.float32),
            pltpu.VMEM((16, 2, 136, 128), jnp.int32),
            pltpu.VMEM((2, 3, 4, 136, 128), jnp.int32),
            pltpu.VMEM((2, 3, 136, 128), jnp.int32),
            pltpu.VMEM((2, 3, 136, 128), jnp.int32),
            pltpu.VMEM((2, 512, 256), jnp.float32),
            pltpu.VMEM((128, 1024), jnp.float32),
            pltpu.VMEM((8, 1024), jnp.int32),
            pltpu.VMEM((1024, 512), jnp.bfloat16),
            pltpu.VMEM((128, 16, 128), jnp.int32),
            pltpu.VMEM((128, 1, 128), jnp.int32),
            pltpu.SemaphoreType.DMA((10,)),
            pltpu.SemaphoreType.DMA((len(SENDS),)),
            pltpu.SemaphoreType.DMA((16, 4)),
            pltpu.SemaphoreType.DMA((16, 2)),
            pltpu.SemaphoreType.DMA((2, 3, 4)),
            pltpu.SemaphoreType.DMA((2, 3)),
            pltpu.SemaphoreType.DMA((2, 3)),
            pltpu.SemaphoreType.DMA,
            pltpu.SemaphoreType.DMA,
            pltpu.SemaphoreType.DMA,
            pltpu.SemaphoreType.DMA,
            pltpu.SemaphoreType.DMA((2,)),
        ],
        compiler_params=pltpu.CompilerParams(
            collective_id=0, has_side_effects=True, vmem_limit_bytes=64 * 1024 * 1024
        ),
        cost_estimate=pl.CostEstimate(
            flops=5_400_000_000, bytes_accessed=4_000_000, transcendentals=2_100_000
        ),
        name="attention_grads",
    )(
        candidates, scenarios.reshape(1, -1), users.reshape(1, -1), gate_table, normalizer.reshape(1, -1),
        forward_out, out_grad, history, items, lengths,
    )


def local(
    candidates,
    scenarios,
    candidate_user,
    gate_table,
    log_normalizer,
    forward_out,
    out_grad,
    history,
    history_length,
    history_items,
):
    candidate_grad, rows, codes = attention(
        candidates, scenarios, candidate_user, gate_table, log_normalizer,
        forward_out, out_grad, history, history_items, history_length,
    )
    table_grad, candidate_grad = add_rows(rows.reshape(2048, 128), codes.reshape(128, 128), candidate_grad)
    return (candidate_grad, table_grad)


def solution(mesh):
    return jax.shard_map(
        local,
        mesh=mesh,
        in_specs=(
            P(("dp", "seq"), None),
            P(("dp", "seq")),
            P(("dp", "seq")),
            P(),
            P(("dp", "seq")),
            P(("dp", "seq"), None),
            P(("dp", "seq"), None),
            P("dp", "seq", None),
            P("dp"),
            P("dp", "seq"),
        ),
        out_specs=(P(("dp", "seq"), None), P(("dp", "seq"), None)),
        check_vma=False,
    )
```

```python
import math

import jax
import jax.numpy as jnp
from jax import lax
from jax.experimental import pallas as pl
from jax.experimental.pallas import tpu as pltpu
from jax.sharding import PartitionSpec as P

ITEM_DEV = 4096
MESH = pl.DeviceIdType.MESH

ORDER = [
    (0, 0), (0, 1), (0, 3), (1, 0), (3, 0), (0, 2), (2, 0),
    (1, 1), (1, 3), (3, 1), (3, 3), (1, 2), (3, 2), (2, 1), (2, 3), (2, 2),
]
SLOT = {offset: i for i, offset in enumerate(ORDER)}
QUARTERS = [(0, 128), (128, 128), (256, 128), (384, 144)]
BLOCK = 528
YP, YM, ZP, ZM = (1, 0), (-1, 0), (0, 1), (0, -1)


def forward_plan():
    plan = {i: [] for i in range(16)}

    def wait(step, offset, quarters):
        plan[step].append(("wait", offset, quarters))

    def send(step, offset, quarter, direction):
        plan[step].append(("send", offset, quarter, direction))

    a, b = (0, 1), (2, 3)
    for q in a:
        send(0, (0, 0), q, ZP)
        send(0, (0, 0), q, ZM)
    for q in b:
        send(0, (0, 0), q, YP)
        send(0, (0, 0), q, YM)
    for q in a:
        send(0, (0, 0), q, YP)
        send(0, (0, 0), q, YM)
    for q in b:
        send(0, (0, 0), q, ZP)
        send(0, (0, 0), q, ZM)
    for offset in ((0, 1), (0, 3)):
        wait(1, offset, a)
    for offset in ((1, 0), (3, 0)):
        wait(1, offset, b)
    send(1, (0, 3), 0, ZP)
    send(1, (0, 1), 1, ZM)
    send(1, (3, 0), 2, YP)
    send(1, (1, 0), 3, YM)
    for q in a:
        for offset in ((0, 1), (0, 3)):
            send(1, offset, q, YP)
            send(1, offset, q, YM)
    for q in b:
        for offset in ((1, 0), (3, 0)):
            send(1, offset, q, ZP)
            send(1, offset, q, ZM)
    for offset in ((0, 1), (0, 3)):
        wait(1, offset, b)
    for offset in ((1, 0), (3, 0)):
        wait(1, offset, a)
    send(1, (0, 3), 2, ZP)
    send(1, (0, 1), 3, ZM)
    send(1, (3, 0), 0, YP)
    send(1, (1, 0), 1, YM)
    wait(5, (0, 2), a)
    wait(5, (2, 0), b)
    for q in a:
        send(5, (0, 2), q, YP)
        send(5, (0, 2), q, YM)
    for q in b:
        send(5, (2, 0), q, ZP)
        send(5, (2, 0), q, ZM)
    wait(5, (0, 2), b)
    wait(5, (2, 0), a)
    for dz in (1, 3):
        wait(7, (3, dz), a)
        wait(7, (1, dz), a)
        send(7, (3, dz), 0, YP)
        send(7, (1, dz), 1, YM)
    for dy in (1, 3):
        wait(7, (dy, 3), b)
        wait(7, (dy, 1), b)
        send(7, (dy, 3), 2, ZP)
        send(7, (dy, 1), 3, ZM)
    wait(11, (3, 2), a)
    wait(11, (1, 2), a)
    send(11, (3, 2), 0, YP)
    send(11, (1, 2), 1, YM)
    wait(11, (2, 3), b)
    wait(11, (2, 1), b)
    send(11, (2, 3), 2, ZP)
    send(11, (2, 1), 3, ZM)
    wait(11, (1, 2), b)
    wait(11, (3, 2), b)
    wait(11, (2, 1), a)
    wait(11, (2, 3), a)
    wait(15, (2, 2), a + b)
    return plan


PLAN = forward_plan()
SENDS = [e for i in range(16) for e in PLAN[i] if e[0] == "send"]


def split3(x):
    hi = x.astype(jnp.bfloat16).astype(jnp.float32)
    rest = x - hi
    mid = rest.astype(jnp.bfloat16).astype(jnp.float32)
    return hi, mid, rest - mid


def nt(a, b):
    return lax.dot_general(a, b, (((1,), (1,)), ((), ())), preferred_element_type=jnp.float32)


def tn(a, b):
    return lax.dot_general(a, b, (((0,), (0,)), ((), ())), preferred_element_type=jnp.float32)


def power_of(top):
    power = jnp.ceil(jnp.log(jnp.maximum(top, 1e-33)) * (1.0 / math.log(2.0)))
    return jnp.clip(power, -110.0, 127.0)


def quantized(x):
    top = jnp.max(jnp.abs(x), axis=0, keepdims=True)
    power = power_of(top)
    q = jnp.round(x * (jnp.exp2(15.0 - power) * 0.99)).astype(jnp.int32)
    half = x.shape[0] // 2
    words = (q[half:] << 16) | (q[:half] & 0xFFFF)
    return words, jnp.broadcast_to(power.astype(jnp.int32), (8, x.shape[1]))


def restored(words, power):
    scale = jnp.exp2(power.astype(jnp.float32) - 15.0) * (1.0 / 0.99)
    low = ((words << 16) >> 16).astype(jnp.float32) * scale
    high = (words >> 16).astype(jnp.float32) * scale
    return low, high


def attention_kernel(
    cand_hbm, scen_hbm, user_hbm, gate_hbm, norm_hbm, fwd_hbm, grad_hbm, hist_hbm, item_hbm, length_hbm,
    cand_out, rows_in, codes_in,
    cand_ref, scen_ref, user_ref, gate_ref, norm_ref, fwd_ref, grad_ref, hist_ref, item_ref, length_ref,
    buf, keys, gates, part_out, part_in, sums_out, sums_in, hist_sum, alike, matches, places_of, halves, rows_out, codes_out,
    load_sem, send_sem, recv_sem, part_send, part_recv, sums_send, sums_recv,
    rows_send, rows_recv, codes_send, codes_recv, own_sem,
):
    loads = [
        pltpu.make_async_copy(there, here, load_sem.at[i])
        for i, (there, here) in enumerate([
            (scen_hbm, scen_ref), (gate_hbm, gate_ref), (user_hbm, user_ref), (norm_hbm, norm_ref),
            (cand_hbm, cand_ref), (grad_hbm, grad_ref), (fwd_hbm, fwd_ref),
            (hist_hbm, hist_ref), (length_hbm, length_ref), (item_hbm, item_ref),
        ])
    ]
    for load in loads:
        load.start()

    dp = lax.axis_index("dp")
    seq = lax.axis_index("seq")
    x, core = dp // 2, dp % 2
    y, z = seq // 4, seq % 4

    xs = [(x + d) % 4 for d in range(4)]
    ys = [(y + d) % 4 for d in range(4)]
    zs = [(z + d) % 4 for d in range(4)]
    cores = [core, 1 - core]

    def device(dy, dz):
        return (dp, ys[dy % 4] * 4 + zs[dz % 4])

    barrier = pltpu.get_barrier_semaphore()

    lines = [(ys[d] * 4 + z, dp) for d in range(1, 4)] + [(y * 4 + zs[d], dp) for d in range(1, 4)]
    lines += [(seq, xs[d] * 2 + c) for d in range(4) for c in cores][1:]
    for there, group in lines:
        pl.semaphore_signal(barrier, inc=1, device_id=(group, there), device_id_type=MESH)

    def block_copy(number):
        _, offset, quarter, (dy, dz) = SENDS[number]
        there = SLOT[(offset[0] - dy) % 4, (offset[1] - dz) % 4]
        rows = pl.ds(*QUARTERS[quarter])
        return pltpu.make_async_remote_copy(
            src_ref=buf.at[SLOT[offset], rows],
            dst_ref=buf.at[there, rows],
            send_sem=send_sem.at[number],
            recv_sem=recv_sem.at[there, quarter],
            device_id=device(dy, dz),
            device_id_type=MESH,
        )

    def block_arrival(offset, quarter):
        rows = pl.ds(*QUARTERS[quarter])
        slot = SLOT[offset]
        return pltpu.make_async_remote_copy(
            src_ref=buf.at[slot, rows],
            dst_ref=buf.at[slot, rows],
            send_sem=send_sem.at[0],
            recv_sem=recv_sem.at[slot, quarter],
            device_id=device(0, 1),
            device_id_type=MESH,
        )

    def part_copy(i, half):
        dy, dz = ORDER[i]
        step, across = (dz, dy) if half == 0 else (dy, dz)
        there = part_in.at[half, 3 - step, across]
        return pltpu.make_async_remote_copy(
            src_ref=part_out.at[i, half],
            dst_ref=there,
            send_sem=part_send.at[i, half],
            recv_sem=part_recv.at[half, 3 - step, across],
            device_id=device(0, step) if half == 0 else device(step, 0),
            device_id_type=MESH,
        )

    parts = [(i, h) for i in range(1, 16) for h in range(2) if ORDER[i][1 - h]]

    def sums_copy(half, step):
        return pltpu.make_async_remote_copy(
            src_ref=sums_out.at[half, step - 1],
            dst_ref=sums_in.at[half, 3 - step],
            send_sem=sums_send.at[half, step - 1],
            recv_sem=sums_recv.at[half, 3 - step],
            device_id=device(step, 0) if half == 0 else device(0, step),
            device_id_type=MESH,
        )

    for load in loads[:7]:
        load.wait()
    scen_rows = scen_ref[...] == lax.broadcasted_iota(jnp.int32, (16, 256), 0)
    gates[...] = lax.dot_general(
        scen_rows.astype(jnp.float32), gate_ref[...], (((0,), (0,)), ((), ())),
        precision=lax.Precision.HIGHEST, preferred_element_type=jnp.float32,
    )
    queries = (cand_ref[...].astype(jnp.float32) * gates[...]).astype(jnp.bfloat16)
    buf[0, 0:256] = queries * jnp.bfloat16(0.0625)
    grads = grad_ref[...]
    buf[0, 256:512] = grads
    inner = lax.dot_general(
        jnp.ones((8, 256), jnp.float32),
        grads.astype(jnp.float32) * fwd_ref[...].astype(jnp.float32),
        (((1,), (1,)), ((), ())),
        precision=lax.Precision.HIGHEST, preferred_element_type=jnp.float32,
    )[0:1]
    user = (user_ref[...] - 2 * dp).astype(jnp.float32)
    numbers = [*split3(norm_ref[...]), *split3(inner), 1.0 - user, user]
    numbers = jnp.concatenate(numbers + [jnp.zeros((8, 256), jnp.float32)], axis=0)
    buf[0, 512:528] = numbers.astype(jnp.bfloat16)

    pl.semaphore_wait(barrier, 13)

    def run_plan(step):
        for event in PLAN[step]:
            if event[0] == "wait":
                for quarter in event[2]:
                    block_arrival(event[1], quarter).wait_recv()
            else:
                block_copy(SENDS.index(event)).start()

    run_plan(0)

    first = seq * 512
    places = first + lax.broadcasted_iota(jnp.int32, (512, 256), 0)
    for load in loads[7:]:
        load.wait()
    for u in range(2):
        rows = hist_ref[u].astype(jnp.float32)
        keys[u] = jnp.where(places < length_ref[u], rows, 0.0).astype(jnp.bfloat16)
    hist_sum[...] = jnp.zeros_like(hist_sum)
    def rank_items():
        items = jnp.concatenate([item_ref[0:1], item_ref[1:2]], axis=1)
        owner = items // ITEM_DEV
        other = [owner // 32, owner // 16 % 2, owner // 4 % 4, owner % 4]
        message = (other[1] + core) % 2 * 64 + (other[2] - y + 4) % 4 * 16 + (other[0] - x + 4) % 4 * 4
        message = message + (other[3] - z + 4) % 4
        found = lax.broadcasted_iota(jnp.int32, (128, 1024), 0) == message
        column = jnp.transpose(jnp.broadcast_to(items.astype(jnp.float32), (128, 1024)))[:, 0:1]
        same = column == items.astype(jnp.float32)
        one, zero = jnp.float32(1.0), jnp.float32(0.0)
        alike[...] = jnp.where(same, one, zero).astype(jnp.bfloat16)
        number = lax.broadcasted_iota(jnp.int32, (1024, 1024), 0)
        other_number = lax.broadcasted_iota(jnp.int32, (1024, 1024), 1)
        repeats = jnp.sum(jnp.where(same & (number < other_number), one, zero), axis=0, keepdims=True)
        first = jnp.where(repeats == 0.0, one, zero)
        matches[...] = jnp.where(found, first, zero)
        counts = jnp.dot(
            matches[...].astype(jnp.bfloat16), jnp.where(number <= other_number, one, zero).astype(jnp.bfloat16),
            preferred_element_type=jnp.float32,
        )
        rank = jnp.sum(matches[...] * counts, axis=0, keepdims=True) - first
        rank = jnp.dot(
            jnp.broadcast_to(rank, (8, 1024)).astype(jnp.bfloat16), alike[...], preferred_element_type=jnp.float32
        )[0:1].astype(jnp.int32)
        places_of[0:1] = message * 16 + rank
        places_of[1:2] = rank
        places_of[2:3] = (items % ITEM_DEV) * 2 + 16

    def step(k, carry):
        for i in range(1, 16):
            if PLAN[i]:
                pl.when(k == i)(lambda i=i: run_plan(i))
        numbers = buf[k, 512:528].astype(jnp.float32)
        normalizer = numbers[0:1] + numbers[1:2] + numbers[2:3]
        inner_sum = numbers[3:4] + numbers[4:5] + numbers[5:6]
        pick = [numbers[6:7], numbers[7:8]]
        low = [w.astype(jnp.bfloat16) for w in pick]
        both = buf[k, 0:512]
        query_part = jnp.zeros((256, 256), jnp.float32)
        for c in range(2):
            rows = pl.ds(c * 256, 256)
            mine = keys[0, rows] * low[0] + keys[1, rows] * low[1]
            products = nt(mine, both)
            probability = jnp.exp(products[:, :256] - normalizer)
            score_grad = (probability * (products[:, 256:] - inner_sum)).astype(jnp.bfloat16)
            weights = jnp.concatenate([score_grad, probability.astype(jnp.bfloat16)], axis=1)
            key_part = jnp.dot(weights, both, preferred_element_type=jnp.float32)
            hist_sum[0, rows] += key_part * pick[0]
            hist_sum[1, rows] += key_part * pick[1]
            query_part += tn(score_grad, mine)

        words, power = quantized(query_part)
        for h in range(2):
            columns = slice(h * 128, (h + 1) * 128)
            part_out[k, h, 0:128] = words[:, columns]
            part_out[k, h, 128:136] = power[:, columns]
        for i in range(1, 16):

            @pl.when(k == i)
            def _(i=i):
                for h in range(2):
                    if (i, h) in parts:
                        part_copy(i, h).start()

        pl.when(k == 6)(rank_items)
        return carry

    lax.fori_loop(0, 16, step, 0)

    tops = []
    for u in range(2):
        hist_sum[u] = jnp.where(places < length_ref[u], hist_sum[u], 0.0)
        top = jnp.max(jnp.abs(hist_sum[u]), axis=1, keepdims=True) * 1.01
        tops.append(jnp.broadcast_to(top, (512, 128)).astype(jnp.bfloat16))
    power = power_of(jnp.dot(alike[...], jnp.concatenate(tops, axis=0), preferred_element_type=jnp.float32))
    scale = jnp.exp2(15.0 - power) * 0.99
    for u in range(2):
        rows = pl.ds(u * 512, 512)
        for h in range(2):
            q = jnp.round(hist_sum[u, :, h * 128 : h * 128 + 128] * scale[u * 512 : u * 512 + 512]).astype(jnp.int32)
            halves[rows, h * 128 : h * 128 + 128] = (q >> 8).astype(jnp.float32).astype(jnp.bfloat16)
            halves[rows, 256 + h * 128 : 384 + h * 128] = (q & 255).astype(jnp.float32).astype(jnp.bfloat16)
    first_lane = lax.broadcasted_iota(jnp.int32, (1024, 128), 1) == 0
    power = nt(jnp.ones((8, 128), jnp.bfloat16), jnp.where(first_lane, power, 0.0).astype(jnp.bfloat16))[0:1]
    column = lax.broadcasted_iota(jnp.int32, (128, 1024), 0)
    codes = jnp.where(column < 16, places_of[2:3].astype(jnp.float32), power + 128.0)
    ranked = (column % 16 == places_of[1:2]) & (column < 32)
    codes = lax.dot_general(
        matches[...], jnp.where(ranked, codes, 0.0), (((1,), (1,)), ((), ())),
        precision=lax.Precision.HIGHEST, preferred_element_type=jnp.float32,
    )
    codes_out[...] = codes.astype(jnp.int32).reshape(128, 1, 128)

    def rows_copy(m, there):
        return pltpu.make_async_remote_copy(
            src_ref=rows_out.at[m], dst_ref=rows_in.at[m], send_sem=rows_send, recv_sem=rows_recv,
            device_id=there, device_id_type=MESH,
        )

    def codes_copy(m, there):
        return pltpu.make_async_remote_copy(
            src_ref=codes_out.at[m], dst_ref=codes_in.at[m], send_sem=codes_send, recv_sem=codes_recv,
            device_id=there, device_id_type=MESH,
        )

    own_rows = pltpu.make_async_copy(rows_out.at[0], rows_in.at[0], own_sem.at[0])
    own_codes = pltpu.make_async_copy(codes_out.at[0], codes_in.at[0], own_sem.at[1])

    def send_chunk(c, carry):
        slots = lax.broadcasted_iota(jnp.int32, (256, 1024), 0) + c * 256
        chosen = jnp.where(slots == places_of[0:1], 1.0, 0.0).astype(jnp.bfloat16)
        moved = jnp.dot(chosen, halves[...], preferred_element_type=jnp.float32).astype(jnp.int32)
        value = (moved[:, 0:256] << 8) + moved[:, 256:512]
        words = (value[:, 128:256] << 16) | (value[:, 0:128] & 0xFFFF)
        rows_out[pl.ds(c * 16, 16)] = words.reshape(16, 16, 128)

        to_core = (core + c // 4) % 2
        to_y = (y + c % 4) % 4
        for j in range(16):
            m = c * 16 + j
            there = (xs[j // 4] * 2 + to_core, to_y * 4 + zs[j % 4])

            def send_one(m=m, there=there):
                rows_copy(m, there).start()
                codes_copy(m, there).start()

            if j == 0:
                pl.when(c > 0)(send_one)
            else:
                send_one()
        return carry

    lax.fori_loop(0, 8, send_chunk, 0)
    own_rows.start()
    own_codes.start()

    for i, h in parts:
        part_copy(i, h).wait_recv()
    firsts = []
    for h in range(2):
        for d in range(4):
            own = SLOT[(d, 0) if h == 0 else (0, d)]
            low, high = restored(part_out[own, h, 0:128], part_out[own, h, 128:129])
            for source in range(3):
                a, b = restored(part_in[h, source, d, 0:128], part_in[h, source, d, 128:129])
                low, high = low + a, high + b
            if d == 0:
                firsts.append((low, high))
            else:
                words, power = quantized(jnp.concatenate([low, high], axis=0))
                sums_out[h, d - 1, 0:128] = words
                sums_out[h, d - 1, 128:136] = power
                sums_copy(h, d).start()
    for h in range(2):
        low, high = firsts[h]
        for d in range(1, 4):
            sums_copy(h, d).wait_recv()
        for source in range(3):
            a, b = restored(sums_in[h, source, 0:128], sums_in[h, source, 128:129])
            low, high = low + a, high + b
        columns = slice(h * 128, (h + 1) * 128)
        cand_out[0:128, columns] = low * 0.0625 * gates[0:128, columns]
        cand_out[128:256, columns] = high * 0.0625 * gates[128:256, columns]
    for number in range(len(SENDS)):
        block_copy(number).wait_send()
    for i, h in parts:
        part_copy(i, h).wait_send()
    for h in range(2):
        for d in range(1, 4):
            sums_copy(h, d).wait_send()
    own_rows.wait()
    own_codes.wait()
    others = pl.ds(1, 127)
    all_rows = pltpu.make_async_remote_copy(
        src_ref=rows_out.at[others], dst_ref=rows_in.at[others], send_sem=rows_send, recv_sem=rows_recv,
        device_id=device(0, 1), device_id_type=MESH,
    )
    all_codes = pltpu.make_async_remote_copy(
        src_ref=codes_out.at[others], dst_ref=codes_in.at[others], send_sem=codes_send, recv_sem=codes_recv,
        device_id=device(0, 1), device_id_type=MESH,
    )
    all_rows.wait()
    all_codes.wait()


def table_kernel(
    rows_hbm, codes_hbm, cand_hbm, table_out, cand_out,
    rows_ref, codes_ref, powers_ref, cand_ref, values, t0, t1, table, sem
):
    loads = [
        pltpu.make_async_copy(codes_hbm, codes_ref, sem.at[9]),
        pltpu.make_async_copy(codes_hbm, powers_ref, sem.at[10]),
        pltpu.make_async_copy(rows_hbm, rows_ref, sem.at[11]),
        pltpu.make_async_copy(cand_hbm, cand_ref, sem.at[12]),
    ]
    for load in loads:
        load.start()
    cand_copy = pltpu.make_async_copy(cand_ref, cand_out, sem.at[8])

    def clear(c, carry):
        for t in (t0, t1):
            t[pl.ds(c * 1024, 1024)] = jnp.zeros((1024, 128), jnp.float32)
        return carry

    lax.fori_loop(0, 8, clear, 0)
    for t in (t0, t1):
        t[8192:8208] = jnp.zeros((16, 128), jnp.float32)

    for load in loads:
        load.wait()
    cand_copy.start()
    powers = jnp.transpose(powers_ref[...].astype(jnp.float32))[16:32]
    scales = jnp.exp2(powers - 143.0) * (1.0 / 0.99)
    for m in range(128):
        scale = scales[:, m : m + 1]
        words = rows_ref[m * 16 : m * 16 + 16]
        values[pl.ds(m * 32, 16, stride=2)] = ((words << 16) >> 16).astype(jnp.float32) * scale
        values[pl.ds(m * 32 + 1, 16, stride=2)] = (words >> 16).astype(jnp.float32) * scale

    def add_messages(i, carry):
        for t, m in ((t0, i * 2), (t1, i * 2 + 1)):
            places = [pl.ds(pl.multiple_of(codes_ref[m, j], 2), 2) for j in range(16)]
            sums = [t[places[j]] + values[pl.ds(m * 32 + j * 2, 2)] for j in range(16)]
            for j in range(16):
                t[places[j]] = sums[j]
        return carry

    lax.fori_loop(0, 64, add_messages, 0)

    def out_copy(c):
        rows = pl.ds(c * 512, 512)
        return pltpu.make_async_copy(table.at[rows], table_out.at[rows], sem.at[c])

    for c in range(8):
        for h in range(2):
            rows = pl.ds(16 + c * 1024 + h, 512, stride=2)
            table[c * 512 : c * 512 + 512, h * 128 : h * 128 + 128] = t0[rows] + t1[rows]
        out_copy(c).start()
    for c in range(8):
        out_copy(c).wait()
    cand_copy.wait()


def add_rows(rows, codes, candidate_grad):
    hbm = pl.BlockSpec(memory_space=pltpu.HBM)
    return pl.pallas_call(
        table_kernel,
        out_shape=(
            jax.ShapeDtypeStruct((ITEM_DEV, 256), jnp.float32),
            jax.ShapeDtypeStruct((256, 256), jnp.float32),
        ),
        in_specs=[hbm, hbm, hbm],
        out_specs=(hbm, hbm),
        scratch_shapes=[
            pltpu.VMEM((2048, 128), jnp.int32),
            pltpu.SMEM((128, 128), jnp.int32),
            pltpu.VMEM((128, 128), jnp.int32),
            pltpu.VMEM((256, 256), jnp.float32),
            pltpu.VMEM((4096, 128), jnp.float32),
            pltpu.VMEM((2 * ITEM_DEV + 16, 128), jnp.float32),
            pltpu.VMEM((2 * ITEM_DEV + 16, 128), jnp.float32),
            pltpu.VMEM((ITEM_DEV, 256), jnp.float32),
            pltpu.SemaphoreType.DMA((13,)),
        ],
        compiler_params=pltpu.CompilerParams(vmem_limit_bytes=64 * 1024 * 1024),
        cost_estimate=pl.CostEstimate(flops=2_000_000, bytes_accessed=5_500_000, transcendentals=0),
        name="table_rows",
    )(rows, codes, candidate_grad)


def attention(candidates, scenarios, users, gate_table, normalizer, forward_out, out_grad, history, items, lengths):
    vmem = pl.BlockSpec(memory_space=pltpu.VMEM)
    return pl.pallas_call(
        attention_kernel,
        out_shape=(
            jax.ShapeDtypeStruct((256, 256), jnp.float32),
            jax.ShapeDtypeStruct((128, 16, 128), jnp.int32),
            jax.ShapeDtypeStruct((128, 1, 128), jnp.int32),
        ),
        in_specs=[pl.BlockSpec(memory_space=pltpu.HBM)] * 10,
        out_specs=(vmem, pl.BlockSpec(memory_space=pl.ANY), pl.BlockSpec(memory_space=pl.ANY)),
        scratch_shapes=[
            pltpu.VMEM((256, 256), jnp.bfloat16),
            pltpu.VMEM((1, 256), jnp.int32),
            pltpu.VMEM((1, 256), jnp.int32),
            pltpu.VMEM((16, 256), jnp.float32),
            pltpu.VMEM((1, 256), jnp.float32),
            pltpu.VMEM((256, 256), jnp.bfloat16),
            pltpu.VMEM((256, 256), jnp.bfloat16),
            pltpu.VMEM((2, 512, 256), jnp.bfloat16),
            pltpu.VMEM((2, 512), jnp.int32),
            pltpu.SMEM((2,), jnp.int32),
            pltpu.VMEM((16, BLOCK, 256), jnp.bfloat16),
            pltpu.VMEM((2, 512, 256), jnp.bfloat16),
            pltpu.VMEM((256, 256), jnp.float32),
            pltpu.VMEM((16, 2, 136, 128), jnp.int32),
            pltpu.VMEM((2, 3, 4, 136, 128), jnp.int32),
            pltpu.VMEM((2, 3, 136, 128), jnp.int32),
            pltpu.VMEM((2, 3, 136, 128), jnp.int32),
            pltpu.VMEM((2, 512, 256), jnp.float32),
            pltpu.VMEM((1024, 1024), jnp.bfloat16),
            pltpu.VMEM((128, 1024), jnp.float32),
            pltpu.VMEM((8, 1024), jnp.int32),
            pltpu.VMEM((1024, 512), jnp.bfloat16),
            pltpu.VMEM((128, 16, 128), jnp.int32),
            pltpu.VMEM((128, 1, 128), jnp.int32),
            pltpu.SemaphoreType.DMA((10,)),
            pltpu.SemaphoreType.DMA((len(SENDS),)),
            pltpu.SemaphoreType.DMA((16, 4)),
            pltpu.SemaphoreType.DMA((16, 2)),
            pltpu.SemaphoreType.DMA((2, 3, 4)),
            pltpu.SemaphoreType.DMA((2, 3)),
            pltpu.SemaphoreType.DMA((2, 3)),
            pltpu.SemaphoreType.DMA,
            pltpu.SemaphoreType.DMA,
            pltpu.SemaphoreType.DMA,
            pltpu.SemaphoreType.DMA,
            pltpu.SemaphoreType.DMA((2,)),
        ],
        compiler_params=pltpu.CompilerParams(
            collective_id=0, has_side_effects=True, vmem_limit_bytes=64 * 1024 * 1024
        ),
        cost_estimate=pl.CostEstimate(
            flops=5_400_000_000, bytes_accessed=4_000_000, transcendentals=2_100_000
        ),
        name="attention_grads",
    )(
        candidates, scenarios.reshape(1, -1), users.reshape(1, -1), gate_table, normalizer.reshape(1, -1),
        forward_out, out_grad, history, items, lengths,
    )


def local(
    candidates,
    scenarios,
    candidate_user,
    gate_table,
    log_normalizer,
    forward_out,
    out_grad,
    history,
    history_length,
    history_items,
):
    candidate_grad, rows, codes = attention(
        candidates, scenarios, candidate_user, gate_table, log_normalizer,
        forward_out, out_grad, history, history_items, history_length,
    )
    table_grad, candidate_grad = add_rows(rows.reshape(2048, 128), codes.reshape(128, 128), candidate_grad)
    return (candidate_grad, table_grad)


def solution(mesh):
    return jax.shard_map(
        local,
        mesh=mesh,
        in_specs=(
            P(("dp", "seq"), None),
            P(("dp", "seq")),
            P(("dp", "seq")),
            P(),
            P(("dp", "seq")),
            P(("dp", "seq"), None),
            P(("dp", "seq"), None),
            P("dp", "seq", None),
            P("dp"),
            P("dp", "seq"),
        ),
        out_specs=(P(("dp", "seq"), None), P(("dp", "seq"), None)),
        check_vma=False,
    )
```

```python
import math

import jax
import jax.numpy as jnp
from jax import lax
from jax.experimental import pallas as pl
from jax.experimental.pallas import tpu as pltpu
from jax.sharding import PartitionSpec as P

ITEM_DEV = 4096
MESH = pl.DeviceIdType.MESH

ORDER = [
    (0, 0), (0, 1), (0, 3), (1, 0), (3, 0), (1, 1), (1, 3), (3, 1), (3, 3),
    (0, 2), (2, 0), (1, 2), (2, 1), (3, 2), (2, 3), (2, 2),
]
SLOT = {offset: i for i, offset in enumerate(ORDER)}
QUARTERS = [(0, 128), (128, 128), (256, 128), (384, 144)]
BLOCK = 528
YP, YM, ZP, ZM = (1, 0), (-1, 0), (0, 1), (0, -1)


def forward_plan():
    plan = {i: [] for i in range(16)}

    def wait(step, offset, quarters):
        plan[step].append(("wait", offset, quarters))

    def send(step, offset, quarter, direction):
        plan[step].append(("send", offset, quarter, direction))

    a, b = (0, 1), (2, 3)
    for q in a:
        send(0, (0, 0), q, ZP)
        send(0, (0, 0), q, ZM)
    for q in b:
        send(0, (0, 0), q, YP)
        send(0, (0, 0), q, YM)
    for q in a:
        send(0, (0, 0), q, YP)
        send(0, (0, 0), q, YM)
    for q in b:
        send(0, (0, 0), q, ZP)
        send(0, (0, 0), q, ZM)
    for q in (0, 1):
        for offset in ((0, 1), (0, 3)):
            wait(1, offset, (a[q],))
        for offset in ((1, 0), (3, 0)):
            wait(1, offset, (b[q],))
        if q == 0:
            send(1, (0, 3), 0, ZP)
            send(1, (3, 0), 2, YP)
        else:
            send(1, (0, 1), 1, ZM)
            send(1, (1, 0), 3, YM)
        for offset in ((0, 1), (0, 3)):
            send(1, offset, a[q], YP)
            send(1, offset, a[q], YM)
        for offset in ((1, 0), (3, 0)):
            send(1, offset, b[q], ZP)
            send(1, offset, b[q], ZM)
    for q in (0, 1):
        for offset in ((0, 1), (0, 3)):
            wait(1, offset, (b[q],))
        for offset in ((1, 0), (3, 0)):
            wait(1, offset, (a[q],))
        if q == 0:
            send(1, (0, 3), 2, ZP)
            send(1, (3, 0), 0, YP)
        else:
            send(1, (0, 1), 3, ZM)
            send(1, (1, 0), 1, YM)
    for q in (0, 1):
        wait(3, (0, 2), (a[q],))
        wait(3, (2, 0), (b[q],))
        send(3, (0, 2), a[q], YP)
        send(3, (0, 2), a[q], YM)
        send(3, (2, 0), b[q], ZP)
        send(3, (2, 0), b[q], ZM)
    wait(5, (1, 1), a + b)
    send(5, (1, 1), 1, YM)
    send(5, (1, 1), 3, ZM)
    wait(6, (1, 3), a + b)
    send(6, (1, 3), 1, YM)
    send(6, (1, 3), 2, ZP)
    wait(6, (3, 1), a + b)
    send(6, (3, 1), 0, YP)
    send(6, (3, 1), 3, ZM)
    wait(6, (3, 3), a + b)
    send(6, (3, 3), 0, YP)
    send(6, (3, 3), 2, ZP)
    wait(9, (0, 2), b)
    wait(9, (2, 0), a)
    wait(10, (3, 2), a)
    wait(10, (1, 2), a)
    send(10, (3, 2), 0, YP)
    send(10, (1, 2), 1, YM)
    wait(10, (2, 3), b)
    wait(10, (2, 1), b)
    send(10, (2, 3), 2, ZP)
    send(10, (2, 1), 3, ZM)
    plan[11] += [("parts", i) for i in range(1, 11)]
    wait(11, (1, 2), b)
    wait(12, (2, 1), a)
    wait(13, (3, 2), b)
    wait(14, (2, 3), a)
    wait(15, (2, 2), a + b)
    return plan


PLAN = forward_plan()
SENDS = [e for i in range(16) for e in PLAN[i] if e[0] == "send"]


def split3(x):
    hi = x.astype(jnp.bfloat16).astype(jnp.float32)
    rest = x - hi
    mid = rest.astype(jnp.bfloat16).astype(jnp.float32)
    return hi, mid, rest - mid


def nt(a, b):
    return lax.dot_general(a, b, (((1,), (1,)), ((), ())), preferred_element_type=jnp.float32)


def tn(a, b):
    return lax.dot_general(a, b, (((0,), (0,)), ((), ())), preferred_element_type=jnp.float32)


def power_of(top):
    power = jnp.ceil(jnp.log(jnp.maximum(top, 1e-33)) * (1.0 / math.log(2.0)))
    return jnp.clip(power, -110.0, 127.0)


def quantized(x):
    top = jnp.max(jnp.abs(x), axis=0, keepdims=True)
    power = power_of(top)
    q = jnp.round(x * (jnp.exp2(15.0 - power) * 0.99)).astype(jnp.int32)
    half = x.shape[0] // 2
    words = (q[half:] << 16) | (q[:half] & 0xFFFF)
    return words, jnp.broadcast_to(power.astype(jnp.int32), (8, x.shape[1]))


def restored(words, power):
    scale = jnp.exp2(power.astype(jnp.float32) - 15.0) * (1.0 / 0.99)
    low = ((words << 16) >> 16).astype(jnp.float32) * scale
    high = (words >> 16).astype(jnp.float32) * scale
    return low, high


def attention_kernel(
    cand_hbm, scen_hbm, user_hbm, gate_hbm, norm_hbm, fwd_hbm, grad_hbm, hist_hbm, item_hbm, length_hbm,
    cand_out, rows_in, codes_out_t,
    cand_ref, scen_ref, user_ref, gate_ref, norm_ref, fwd_ref, hist_ref, item_ref, length_ref,
    buf, keys, gates, part_out, part_in, mid_out, mid_in, sums_out, sums_in, hist_sum, alike, matches, places_of, halves, rows_out, codes_out, codes_in, code_rows, code_spots,
    load_sem, send_sem, recv_sem, part_send, part_recv, mid_send, mid_recv, sums_send, sums_recv,
    rows_send, rows_recv, codes_send, codes_recv, own_sem,
):
    loads = [
        pltpu.make_async_copy(there, here, load_sem.at[i])
        for i, (there, here) in enumerate([
            (grad_hbm, buf.at[0, pl.ds(256, 256)]), (scen_hbm, scen_ref), (gate_hbm, gate_ref),
            (cand_hbm, cand_ref), (user_hbm, user_ref), (norm_hbm, norm_ref), (fwd_hbm, fwd_ref),
            (hist_hbm, hist_ref), (length_hbm, length_ref), (item_hbm, item_ref),
        ])
    ]
    for load in loads:
        load.start()

    dp = lax.axis_index("dp")
    seq = lax.axis_index("seq")
    x, core = dp // 2, dp % 2
    y, z = seq // 4, seq % 4

    xs = [(x + d) % 4 for d in range(4)]
    ys = [(y + d) % 4 for d in range(4)]
    zs = [(z + d) % 4 for d in range(4)]
    cores = [core, 1 - core]

    def device(dy, dz):
        return (dp, ys[dy % 4] * 4 + zs[dz % 4])

    barrier = pltpu.get_barrier_semaphore()

    lines = [(ys[d] * 4 + z, dp) for d in range(1, 4)] + [(y * 4 + zs[d], dp) for d in range(1, 4)]
    lines += [(seq, xs[d] * 2 + c) for d in range(4) for c in cores][1:]
    for there, group in lines:
        pl.semaphore_signal(barrier, inc=1, device_id=(group, there), device_id_type=MESH)

    def block_copy(number):
        _, offset, quarter, (dy, dz) = SENDS[number]
        there = SLOT[(offset[0] - dy) % 4, (offset[1] - dz) % 4]
        rows = pl.ds(*QUARTERS[quarter])
        return pltpu.make_async_remote_copy(
            src_ref=buf.at[SLOT[offset], rows],
            dst_ref=buf.at[there, rows],
            send_sem=send_sem.at[number],
            recv_sem=recv_sem.at[there, quarter],
            device_id=device(dy, dz),
            device_id_type=MESH,
        )

    def block_arrival(offset, quarter):
        rows = pl.ds(*QUARTERS[quarter])
        slot = SLOT[offset]
        return pltpu.make_async_remote_copy(
            src_ref=buf.at[slot, rows],
            dst_ref=buf.at[slot, rows],
            send_sem=send_sem.at[0],
            recv_sem=recv_sem.at[slot, quarter],
            device_id=device(0, 1),
            device_id_type=MESH,
        )

    def line_copy(source, there, half, step, send, recv):
        return pltpu.make_async_remote_copy(
            src_ref=source, dst_ref=there, send_sem=send, recv_sem=recv,
            device_id=device(0, step) if half == 0 else device(step, 0),
            device_id_type=MESH,
        )

    def route(i, half):
        dy, dz = ORDER[i]
        return (dz, dy) if half == 0 else (dy, dz)

    def toward(across):
        return -1 if across % 2 == 0 else 1

    def part_copy(i, half):
        step, across = route(i, half)
        send = part_send.at[i, half]
        if step == 2:
            there, recv, step = mid_in.at[half, across], mid_recv.at[half, across], toward(across)
        else:
            there, recv, step = part_in.at[half, 1, across], part_recv.at[half, 1, across], -toward(across)
        return line_copy(part_out.at[i, half], there, half, step, send, recv)

    def mid_copy(half, across):
        return line_copy(
            mid_out.at[half, across], part_in.at[half, 0, across], half, toward(across),
            mid_send.at[half, across], part_recv.at[half, 0, across],
        )

    parts = []
    for i in range(1, 16):
        for h in range(2):
            step, across = route(i, h)
            if step == 2 or (step and step % 4 == -toward(across) % 4):
                parts.append((i, h))

    def send_parts(i):
        for h in range(2):
            if (i, h) in parts:
                part_copy(i, h).start()

    def pass_on(h, across):
        step = toward(across) % 4
        own = SLOT[(across, step) if h == 0 else (step, across)]
        line_copy(
            mid_out.at[h, across], mid_in.at[h, across], h, 1, mid_send.at[h, across], mid_recv.at[h, across]
        ).wait_recv()
        low, high = restored(part_out[own, h, 0:128], part_out[own, h, 128:129])
        a, b = restored(mid_in[h, across, 0:128], mid_in[h, across, 128:129])
        words, power = quantized(jnp.concatenate([low + a, high + b], axis=0))
        mid_out[h, across, 0:128] = words
        mid_out[h, across, 128:136] = power
        mid_copy(h, across).start()

    def sums_copy(half, step):
        return pltpu.make_async_remote_copy(
            src_ref=sums_out.at[half, step - 1],
            dst_ref=sums_in.at[half, 3 - step],
            send_sem=sums_send.at[half, step - 1],
            recv_sem=sums_recv.at[half, 3 - step],
            device_id=device(step, 0) if half == 0 else device(0, step),
            device_id_type=MESH,
        )

    def run_plan(step):
        for event in PLAN[step]:
            if event[0] == "wait":
                for quarter in event[2]:
                    block_arrival(event[1], quarter).wait_recv()
            elif event[0] == "send":
                block_copy(SENDS.index(event)).start()
            else:
                send_parts(event[1])

    early = [event for event in PLAN[0] if event[2] == 2]
    late = [event for event in PLAN[0] if event[2] != 2]
    loads[0].wait()
    pl.semaphore_wait(barrier, 13)
    for event in early:
        block_copy(SENDS.index(event)).start()
    for load in loads[1:7]:
        load.wait()
    scen_rows = scen_ref[...] == lax.broadcasted_iota(jnp.int32, (16, 256), 0)
    gates[...] = lax.dot_general(
        scen_rows.astype(jnp.float32), gate_ref[...], (((0,), (0,)), ((), ())),
        precision=lax.Precision.HIGHEST, preferred_element_type=jnp.float32,
    )
    queries = (cand_ref[...].astype(jnp.float32) * gates[...]).astype(jnp.bfloat16)
    buf[0, 0:256] = queries * jnp.bfloat16(0.0625)
    grads = buf[0, 256:512]
    inner = lax.dot_general(
        jnp.ones((8, 256), jnp.float32),
        grads.astype(jnp.float32) * fwd_ref[...].astype(jnp.float32),
        (((1,), (1,)), ((), ())),
        precision=lax.Precision.HIGHEST, preferred_element_type=jnp.float32,
    )[0:1]
    user = (user_ref[...] - 2 * dp).astype(jnp.float32)
    numbers = [*split3(norm_ref[...]), *split3(inner), 1.0 - user, user]
    numbers = jnp.concatenate(numbers + [jnp.zeros((8, 256), jnp.float32)], axis=0)
    buf[0, 512:528] = numbers.astype(jnp.bfloat16)

    for event in late:
        block_copy(SENDS.index(event)).start()

    first = seq * 512
    places = first + lax.broadcasted_iota(jnp.int32, (512, 256), 0)
    for load in loads[7:]:
        load.wait()
    for u in range(2):
        rows = hist_ref[u].astype(jnp.float32)
        keys[u] = jnp.where(places < length_ref[u], rows, 0.0).astype(jnp.bfloat16)
    hist_sum[...] = jnp.zeros_like(hist_sum)
    def rank_items():
        items = jnp.concatenate([item_ref[0:1], item_ref[1:2]], axis=1)
        owner = items // ITEM_DEV
        other = [owner // 32, owner // 16 % 2, owner // 4 % 4, owner % 4]
        off_x, off_y, off_z = (other[0] - x + 4) % 4, (other[2] - y + 4) % 4, (other[3] - z + 4) % 4
        message = (other[1] + core) % 2 * 64 + (off_z + 8 - off_x - off_y) % 4 * 16 + off_y * 4 + off_x
        found = lax.broadcasted_iota(jnp.int32, (128, 1024), 0) == message
        column = jnp.transpose(jnp.broadcast_to(items.astype(jnp.float32), (128, 1024)))[:, 0:1]
        same = column == items.astype(jnp.float32)
        one, zero = jnp.float32(1.0), jnp.float32(0.0)
        alike[...] = jnp.where(same, one, zero).astype(jnp.bfloat16)
        number = lax.broadcasted_iota(jnp.int32, (1024, 1024), 0)
        other_number = lax.broadcasted_iota(jnp.int32, (1024, 1024), 1)
        repeats = jnp.sum(jnp.where(same & (number < other_number), one, zero), axis=0, keepdims=True)
        first = jnp.where(repeats == 0.0, one, zero)
        matches[...] = jnp.where(found, first, zero)
        counts = jnp.dot(
            matches[...].astype(jnp.bfloat16), jnp.where(number <= other_number, one, zero).astype(jnp.bfloat16),
            preferred_element_type=jnp.float32,
        )
        rank = jnp.sum(matches[...] * counts, axis=0, keepdims=True) - first
        rank = jnp.dot(
            jnp.broadcast_to(rank, (8, 1024)).astype(jnp.bfloat16), alike[...], preferred_element_type=jnp.float32
        )[0:1].astype(jnp.int32)
        places_of[0:1] = message * 16 + rank
        places_of[1:2] = rank
        place = (items % ITEM_DEV) * 2 + 16
        column = lax.broadcasted_iota(jnp.int32, (128, 1024), 0)
        number = jnp.where(column < 16, place % 256, jnp.where(column < 32, 0, place // 256))
        ranked = (column % 16 == rank) & (column < 48)
        code_rows[...] = jnp.where(ranked, number, 0).astype(jnp.float32)
        code_spots[...] = jnp.where(ranked & (column >= 16) & (column < 32), one, zero)

    def products_of(k):
        numbers = buf[k, 512:528].astype(jnp.float32)
        normalizer = numbers[0:1] + numbers[1:2] + numbers[2:3]
        inner_sum = numbers[3:4] + numbers[4:5] + numbers[5:6]
        pick = [numbers[6:7], numbers[7:8]]
        low = [w.astype(jnp.bfloat16) for w in pick]
        both = buf[k, 0:512]
        mine = keys[0] * low[0] + keys[1] * low[1]
        products = nt(mine, both)
        probability = jnp.exp(products[:, :256] - normalizer)
        score_grad = (probability * (products[:, 256:] - inner_sum)).astype(jnp.bfloat16)
        weights = jnp.concatenate([score_grad, probability.astype(jnp.bfloat16)], axis=1)
        key_part = jnp.dot(weights, both, preferred_element_type=jnp.float32)
        return pick, key_part, tn(score_grad, mine)

    def keep_part(k, query_part):
        words, power = quantized(query_part)
        for h in range(2):
            columns = slice(h * 128, (h + 1) * 128)
            part_out[k, h, 0:128] = words[:, columns]
            part_out[k, h, 128:136] = power[:, columns]

    def one_step(k):
        pick, key_part, query_part = products_of(k)
        hist_sum[0] += key_part * pick[0]
        hist_sum[1] += key_part * pick[1]
        keep_part(k, query_part)

    def two_steps(n, carry):
        k = n * 2 + 1
        for i in range(1, 15, 2):
            if PLAN[i] or PLAN[i + 1]:

                @pl.when(k == i)
                def _(i=i):
                    run_plan(i)
                    run_plan(i + 1)

        pick, key_part, query_part = products_of(k)
        next_pick, next_key_part, next_query_part = products_of(k + 1)
        for u in range(2):
            hist_sum[u] += key_part * pick[u] + next_key_part * next_pick[u]
        keep_part(k, query_part)
        keep_part(k + 1, next_query_part)
        for i in range(11, 15, 2):

            @pl.when(k == i)
            def _(i=i):
                send_parts(i)
                send_parts(i + 1)

        return carry

    one_step(0)
    rank_items()
    lax.fori_loop(0, 7, two_steps, 0)
    run_plan(15)
    one_step(15)
    send_parts(15)

    tops = []
    for u in range(2):
        hist_sum[u] = jnp.where(places < length_ref[u], hist_sum[u], 0.0)
        top = jnp.max(jnp.abs(hist_sum[u]), axis=1, keepdims=True) * 1.01
        tops.append(jnp.broadcast_to(top, (512, 128)).astype(jnp.bfloat16))
    power = power_of(jnp.dot(alike[...], jnp.concatenate(tops, axis=0), preferred_element_type=jnp.float32))
    scale = jnp.exp2(15.0 - power) * 0.99
    for u in range(2):
        rows = pl.ds(u * 512, 512)
        for h in range(2):
            q = jnp.round(hist_sum[u, :, h * 128 : h * 128 + 128] * scale[u * 512 : u * 512 + 512]).astype(jnp.int32)
            halves[rows, h * 128 : h * 128 + 128] = (q >> 8).astype(jnp.float32).astype(jnp.bfloat16)
            halves[rows, 256 + h * 128 : 384 + h * 128] = (q & 255).astype(jnp.float32).astype(jnp.bfloat16)
    first_lane = lax.broadcasted_iota(jnp.int32, (1024, 128), 1) == 0
    power = nt(jnp.ones((8, 128), jnp.bfloat16), jnp.where(first_lane, power, 0.0).astype(jnp.bfloat16))[0:1]
    codes = nt(
        matches[...].astype(jnp.bfloat16),
        (code_rows[...] + code_spots[...] * (power + 128.0)).astype(jnp.bfloat16),
    )
    codes_out[...] = codes.astype(jnp.int32).reshape(128, 1, 128)

    def rows_copy(m, there):
        return pltpu.make_async_remote_copy(
            src_ref=rows_out.at[m], dst_ref=rows_in.at[m], send_sem=rows_send, recv_sem=rows_recv,
            device_id=there, device_id_type=MESH,
        )

    def codes_copy(m, there):
        return pltpu.make_async_remote_copy(
            src_ref=codes_out.at[m], dst_ref=codes_in.at[m], send_sem=codes_send, recv_sem=codes_recv,
            device_id=there, device_id_type=MESH,
        )

    own_rows = pltpu.make_async_copy(rows_out.at[0], rows_in.at[0], own_sem.at[0])
    own_codes = pltpu.make_async_copy(codes_out.at[0], codes_in.at[0], own_sem.at[1])

    def send_chunk(c, carry):
        slots = lax.broadcasted_iota(jnp.int32, (256, 1024), 0) + c * 256
        chosen = jnp.where(slots == places_of[0:1], 1.0, 0.0).astype(jnp.bfloat16)
        moved = jnp.dot(chosen, halves[...], preferred_element_type=jnp.float32).astype(jnp.int32)
        value = (moved[:, 0:256] << 8) + moved[:, 256:512]
        words = (value[:, 128:256] << 16) | (value[:, 0:128] & 0xFFFF)
        rows_out[pl.ds(c * 16, 16)] = words.reshape(16, 16, 128)

        to_core = (core + c // 4) % 2
        to_z = [(z + c + d) % 4 for d in range(4)]
        for j in range(16):
            m = c * 16 + j
            there = (xs[j % 4] * 2 + to_core, ys[j // 4] * 4 + to_z[(j + j // 4) % 4])

            def send_one(m=m, there=there):
                rows_copy(m, there).start()
                codes_copy(m, there).start()

            if j == 0:
                pl.when(c > 0)(send_one)
            else:
                send_one()
        return carry

    for across in (0, 1, 3, 2):
        for h in range(2):
            pass_on(h, across)

    lax.fori_loop(0, 8, send_chunk, 0)
    own_rows.start()
    own_codes.start()

    for h in range(2):
        for j in range(2):
            for across in range(4):
                line_copy(
                    part_in.at[h, j, across], part_in.at[h, j, across], h, 1,
                    mid_send.at[h, across], part_recv.at[h, j, across],
                ).wait_recv()
    firsts = []
    for h in range(2):
        for d in range(4):
            own = SLOT[(d, 0) if h == 0 else (0, d)]
            low, high = restored(part_out[own, h, 0:128], part_out[own, h, 128:129])
            for source in range(2):
                a, b = restored(part_in[h, source, d, 0:128], part_in[h, source, d, 128:129])
                low, high = low + a, high + b
            if d == 0:
                firsts.append((low, high))
            else:
                words, power = quantized(jnp.concatenate([low, high], axis=0))
                sums_out[h, d - 1, 0:128] = words
                sums_out[h, d - 1, 128:136] = power
                sums_copy(h, d).start()
    for h in range(2):
        low, high = firsts[h]
        for d in range(1, 4):
            sums_copy(h, d).wait_recv()
        for source in range(3):
            a, b = restored(sums_in[h, source, 0:128], sums_in[h, source, 128:129])
            low, high = low + a, high + b
        columns = slice(h * 128, (h + 1) * 128)
        cand_out[0:128, columns] = low * 0.0625 * gates[0:128, columns]
        cand_out[128:256, columns] = high * 0.0625 * gates[128:256, columns]
    for number in range(len(SENDS)):
        block_copy(number).wait_send()
    for i, h in parts:
        part_copy(i, h).wait_send()
    for h in range(2):
        for across in range(4):
            mid_copy(h, across).wait_send()
    for h in range(2):
        for d in range(1, 4):
            sums_copy(h, d).wait_send()
    own_rows.wait()
    own_codes.wait()
    others = pl.ds(1, 127)
    all_rows = pltpu.make_async_remote_copy(
        src_ref=rows_out.at[others], dst_ref=rows_in.at[others], send_sem=rows_send, recv_sem=rows_recv,
        device_id=device(0, 1), device_id_type=MESH,
    )
    all_codes = pltpu.make_async_remote_copy(
        src_ref=codes_out.at[others], dst_ref=codes_in.at[others], send_sem=codes_send, recv_sem=codes_recv,
        device_id=device(0, 1), device_id_type=MESH,
    )
    all_codes.wait()
    got = jnp.transpose(codes_in[...].reshape(128, 128).astype(jnp.float32)).astype(jnp.int32)
    codes_out_t[0:16] = got[0:16] + got[32:48] * 256
    codes_out_t[16:32] = got[16:32]
    all_rows.wait()


def table_kernel(
    rows_hbm, codes_hbm, cand_hbm, table_out, cand_out,
    rows_ref, codes_ref, powers_ref, cand_ref, values, t0, t1, table, sem
):
    loads = [
        pltpu.make_async_copy(codes_hbm.at[0:16], codes_ref, sem.at[9]),
        pltpu.make_async_copy(codes_hbm.at[16:32], powers_ref, sem.at[10]),
        pltpu.make_async_copy(cand_hbm, cand_ref, sem.at[11]),
    ]
    for part in range(4):
        rows = pl.ds(part * 512, 512)
        loads.append(pltpu.make_async_copy(rows_hbm.at[rows], rows_ref.at[rows], sem.at[12 + part]))
    for load in loads:
        load.start()
    cand_copy = pltpu.make_async_copy(cand_ref, cand_out, sem.at[8])

    def clear(c, carry):
        for t in (t0, t1):
            t[pl.ds(c * 1024, 1024)] = jnp.zeros((1024, 128), jnp.float32)
        return carry

    lax.fori_loop(0, 8, clear, 0)
    for t in (t0, t1):
        t[8192:8208] = jnp.zeros((16, 128), jnp.float32)

    for load in loads[:3]:
        load.wait()
    cand_copy.start()
    scales = jnp.exp2(powers_ref[...].astype(jnp.float32) - 143.0) * (1.0 / 0.99)
    for m in range(128):
        if m % 32 == 0:
            loads[3 + m // 32].wait()
        scale = scales[:, m : m + 1]
        words = rows_ref[m * 16 : m * 16 + 16]
        values[pl.ds(m * 32, 16, stride=2)] = ((words << 16) >> 16).astype(jnp.float32) * scale
        values[pl.ds(m * 32 + 1, 16, stride=2)] = (words >> 16).astype(jnp.float32) * scale

    def add_messages(i, carry):
        pair = ((t0, i * 2), (t1, i * 2 + 1))
        places = [[pl.ds(pl.multiple_of(codes_ref[j, m], 2), 2) for j in range(16)] for _, m in pair]
        sums = [
            [t[places[n][j]] + values[pl.ds(m * 32 + j * 2, 2)] for j in range(16)] for n, (t, m) in enumerate(pair)
        ]
        for n, (t, m) in enumerate(pair):
            for j in range(16):
                t[places[n][j]] = sums[n][j]
        return carry

    lax.fori_loop(0, 64, add_messages, 0)

    def out_copy(c):
        rows = pl.ds(c * 512, 512)
        return pltpu.make_async_copy(table.at[rows], table_out.at[rows], sem.at[c])

    for c in range(8):
        for h in range(2):
            rows = pl.ds(16 + c * 1024 + h, 512, stride=2)
            table[c * 512 : c * 512 + 512, h * 128 : h * 128 + 128] = t0[rows] + t1[rows]
        out_copy(c).start()
    for c in range(8):
        out_copy(c).wait()
    cand_copy.wait()


def add_rows(rows, codes, candidate_grad):
    hbm = pl.BlockSpec(memory_space=pltpu.HBM)
    return pl.pallas_call(
        table_kernel,
        out_shape=(
            jax.ShapeDtypeStruct((ITEM_DEV, 256), jnp.float32),
            jax.ShapeDtypeStruct((256, 256), jnp.float32),
        ),
        in_specs=[hbm, hbm, hbm],
        out_specs=(hbm, hbm),
        scratch_shapes=[
            pltpu.VMEM((2048, 128), jnp.int32),
            pltpu.SMEM((16, 128), jnp.int32),
            pltpu.VMEM((16, 128), jnp.int32),
            pltpu.VMEM((256, 256), jnp.float32),
            pltpu.VMEM((4104, 128), jnp.float32),
            pltpu.VMEM((2 * ITEM_DEV + 32, 128), jnp.float32),
            pltpu.VMEM((2 * ITEM_DEV + 32, 128), jnp.float32),
            pltpu.VMEM((ITEM_DEV, 256), jnp.float32),
            pltpu.SemaphoreType.DMA((16,)),
        ],
        compiler_params=pltpu.CompilerParams(vmem_limit_bytes=64 * 1024 * 1024),
        cost_estimate=pl.CostEstimate(flops=2_000_000, bytes_accessed=5_500_000, transcendentals=0),
        name="table_rows",
    )(rows, codes, candidate_grad)


def attention(candidates, scenarios, users, gate_table, normalizer, forward_out, out_grad, history, items, lengths):
    vmem = pl.BlockSpec(memory_space=pltpu.VMEM)
    return pl.pallas_call(
        attention_kernel,
        out_shape=(
            jax.ShapeDtypeStruct((256, 256), jnp.float32),
            jax.ShapeDtypeStruct((128, 16, 128), jnp.int32),
            jax.ShapeDtypeStruct((32, 128), jnp.int32),
        ),
        in_specs=[pl.BlockSpec(memory_space=pltpu.HBM)] * 10,
        out_specs=(vmem, pl.BlockSpec(memory_space=pl.ANY), vmem),
        scratch_shapes=[
            pltpu.VMEM((256, 256), jnp.bfloat16),
            pltpu.VMEM((1, 256), jnp.int32),
            pltpu.VMEM((1, 256), jnp.int32),
            pltpu.VMEM((16, 256), jnp.float32),
            pltpu.VMEM((1, 256), jnp.float32),
            pltpu.VMEM((256, 256), jnp.bfloat16),
            pltpu.VMEM((2, 512, 256), jnp.bfloat16),
            pltpu.VMEM((2, 512), jnp.int32),
            pltpu.SMEM((2,), jnp.int32),
            pltpu.VMEM((16, BLOCK, 256), jnp.bfloat16),
            pltpu.VMEM((2, 512, 256), jnp.bfloat16),
            pltpu.VMEM((256, 256), jnp.float32),
            pltpu.VMEM((16, 2, 136, 128), jnp.int32),
            pltpu.VMEM((2, 2, 4, 136, 128), jnp.int32),
            pltpu.VMEM((2, 4, 136, 128), jnp.int32),
            pltpu.VMEM((2, 4, 136, 128), jnp.int32),
            pltpu.VMEM((2, 3, 136, 128), jnp.int32),
            pltpu.VMEM((2, 3, 136, 128), jnp.int32),
            pltpu.VMEM((2, 512, 256), jnp.float32),
            pltpu.VMEM((1024, 1024), jnp.bfloat16),
            pltpu.VMEM((128, 1024), jnp.float32),
            pltpu.VMEM((8, 1024), jnp.int32),
            pltpu.VMEM((1024, 512), jnp.bfloat16),
            pltpu.VMEM((128, 16, 128), jnp.int32),
            pltpu.VMEM((128, 1, 128), jnp.int32),
            pltpu.VMEM((128, 1, 128), jnp.int32),
            pltpu.VMEM((128, 1024), jnp.float32),
            pltpu.VMEM((128, 1024), jnp.float32),
            pltpu.SemaphoreType.DMA((10,)),
            pltpu.SemaphoreType.DMA((len(SENDS),)),
            pltpu.SemaphoreType.DMA((16, 4)),
            pltpu.SemaphoreType.DMA((16, 2)),
            pltpu.SemaphoreType.DMA((2, 2, 4)),
            pltpu.SemaphoreType.DMA((2, 4)),
            pltpu.SemaphoreType.DMA((2, 4)),
            pltpu.SemaphoreType.DMA((2, 3)),
            pltpu.SemaphoreType.DMA((2, 3)),
            pltpu.SemaphoreType.DMA,
            pltpu.SemaphoreType.DMA,
            pltpu.SemaphoreType.DMA,
            pltpu.SemaphoreType.DMA,
            pltpu.SemaphoreType.DMA((2,)),
        ],
        compiler_params=pltpu.CompilerParams(
            collective_id=0, has_side_effects=True, vmem_limit_bytes=64 * 1024 * 1024
        ),
        cost_estimate=pl.CostEstimate(
            flops=5_400_000_000, bytes_accessed=4_000_000, transcendentals=2_100_000
        ),
        name="attention_grads",
    )(
        candidates, scenarios.reshape(1, -1), users.reshape(1, -1), gate_table, normalizer.reshape(1, -1),
        forward_out, out_grad, history, items, lengths,
    )


def local(
    candidates,
    scenarios,
    candidate_user,
    gate_table,
    log_normalizer,
    forward_out,
    out_grad,
    history,
    history_length,
    history_items,
):
    candidate_grad, rows, codes = attention(
        candidates, scenarios, candidate_user, gate_table, log_normalizer,
        forward_out, out_grad, history, history_items, history_length,
    )
    table_grad, candidate_grad = add_rows(rows.reshape(2048, 128), codes, candidate_grad)
    return (candidate_grad, table_grad)


def solution(mesh):
    return jax.shard_map(
        local,
        mesh=mesh,
        in_specs=(
            P(("dp", "seq"), None),
            P(("dp", "seq")),
            P(("dp", "seq")),
            P(),
            P(("dp", "seq")),
            P(("dp", "seq"), None),
            P(("dp", "seq"), None),
            P("dp", "seq", None),
            P("dp"),
            P("dp", "seq"),
        ),
        out_specs=(P(("dp", "seq"), None), P(("dp", "seq"), None)),
        check_vma=False,
    )
```

```python
import math

import jax
import jax.numpy as jnp
from jax import lax
from jax.experimental import pallas as pl
from jax.experimental.pallas import tpu as pltpu
from jax.sharding import PartitionSpec as P

ITEM_DEV = 4096
MESH = pl.DeviceIdType.MESH

ORDER = [
    (0, 0), (0, 1), (0, 3), (1, 0), (3, 0), (1, 1), (1, 3), (3, 1), (3, 3),
    (0, 2), (2, 0), (1, 2), (2, 1), (3, 2), (2, 3), (2, 2),
]
SLOT = {offset: i for i, offset in enumerate(ORDER)}
QUARTERS = [(0, 128), (128, 128), (256, 128), (384, 144)]
BLOCK = 528
YP, YM, ZP, ZM = (1, 0), (-1, 0), (0, 1), (0, -1)


def forward_plan():
    plan = {i: [] for i in range(16)}

    def wait(step, offset, quarters):
        plan[step].append(("wait", offset, quarters))

    def send(step, offset, quarter, direction):
        plan[step].append(("send", offset, quarter, direction))

    a, b = (0, 1), (2, 3)
    for q in a:
        send(0, (0, 0), q, ZP)
        send(0, (0, 0), q, ZM)
    for q in b:
        send(0, (0, 0), q, YP)
        send(0, (0, 0), q, YM)
    for q in a:
        send(0, (0, 0), q, YP)
        send(0, (0, 0), q, YM)
    for q in b:
        send(0, (0, 0), q, ZP)
        send(0, (0, 0), q, ZM)
    for q in (0, 1):
        for offset in ((0, 1), (0, 3)):
            wait(1, offset, (a[q],))
        for offset in ((1, 0), (3, 0)):
            wait(1, offset, (b[q],))
        if q == 0:
            send(1, (0, 3), 0, ZP)
            send(1, (3, 0), 2, YP)
        else:
            send(1, (0, 1), 1, ZM)
            send(1, (1, 0), 3, YM)
        for offset in ((0, 1), (0, 3)):
            send(1, offset, a[q], YP)
            send(1, offset, a[q], YM)
        for offset in ((1, 0), (3, 0)):
            send(1, offset, b[q], ZP)
            send(1, offset, b[q], ZM)
    for q in (0, 1):
        for offset in ((0, 1), (0, 3)):
            wait(1, offset, (b[q],))
        for offset in ((1, 0), (3, 0)):
            wait(1, offset, (a[q],))
        if q == 0:
            send(1, (0, 3), 2, ZP)
            send(1, (3, 0), 0, YP)
        else:
            send(1, (0, 1), 3, ZM)
            send(1, (1, 0), 1, YM)
    for q in (0, 1):
        wait(3, (0, 2), (a[q],))
        wait(3, (2, 0), (b[q],))
        send(3, (0, 2), a[q], YP)
        send(3, (0, 2), a[q], YM)
        send(3, (2, 0), b[q], ZP)
        send(3, (2, 0), b[q], ZM)
    wait(5, (1, 1), a + b)
    send(5, (1, 1), 1, YM)
    send(5, (1, 1), 3, ZM)
    wait(6, (1, 3), a + b)
    send(6, (1, 3), 1, YM)
    send(6, (1, 3), 2, ZP)
    wait(6, (3, 1), a + b)
    send(6, (3, 1), 0, YP)
    send(6, (3, 1), 3, ZM)
    wait(6, (3, 3), a + b)
    send(6, (3, 3), 0, YP)
    send(6, (3, 3), 2, ZP)
    wait(9, (0, 2), b)
    wait(9, (2, 0), a)
    wait(10, (3, 2), a)
    wait(10, (1, 2), a)
    send(10, (3, 2), 0, YP)
    send(10, (1, 2), 1, YM)
    wait(10, (2, 3), b)
    wait(10, (2, 1), b)
    send(10, (2, 3), 2, ZP)
    send(10, (2, 1), 3, ZM)
    plan[11] += [("parts", i) for i in range(1, 11)]
    wait(11, (1, 2), b)
    wait(12, (2, 1), a)
    wait(13, (3, 2), b)
    wait(14, (2, 3), a)
    wait(15, (2, 2), a + b)
    return plan


PLAN = forward_plan()
SENDS = [e for i in range(16) for e in PLAN[i] if e[0] == "send"]


def split3(x):
    hi = x.astype(jnp.bfloat16).astype(jnp.float32)
    rest = x - hi
    mid = rest.astype(jnp.bfloat16).astype(jnp.float32)
    return hi, mid, rest - mid


def nt(a, b):
    return lax.dot_general(a, b, (((1,), (1,)), ((), ())), preferred_element_type=jnp.float32)


def tn(a, b):
    return lax.dot_general(a, b, (((0,), (0,)), ((), ())), preferred_element_type=jnp.float32)


def power_of(top):
    power = jnp.ceil(jnp.log(jnp.maximum(top, 1e-33)) * (1.0 / math.log(2.0)))
    return jnp.clip(power, -110.0, 127.0)


def quantized(x):
    top = jnp.max(jnp.abs(x), axis=0, keepdims=True)
    power = power_of(top)
    q = jnp.round(x * (jnp.exp2(15.0 - power) * 0.99)).astype(jnp.int32)
    half = x.shape[0] // 2
    words = (q[half:] << 16) | (q[:half] & 0xFFFF)
    return words, jnp.broadcast_to(power.astype(jnp.int32), (8, x.shape[1]))


def restored(words, power):
    scale = jnp.exp2(power.astype(jnp.float32) - 15.0) * (1.0 / 0.99)
    low = ((words << 16) >> 16).astype(jnp.float32) * scale
    high = (words >> 16).astype(jnp.float32) * scale
    return low, high


def attention_kernel(
    cand_hbm, scen_hbm, user_hbm, gate_hbm, norm_hbm, fwd_hbm, grad_hbm, hist_hbm, item_hbm, length_hbm,
    cand_out, rows_in, codes_out_t,
    cand_ref, scen_ref, user_ref, gate_ref, norm_ref, fwd_ref, hist_ref, item_ref, length_ref,
    buf, keys, gates, part_out, part_in, mid_out, mid_in, sums_out, sums_in, hist_sum, alike, matches, places_of, halves, rows_out, codes_out, codes_in, code_rows, code_spots,
    load_sem, send_sem, recv_sem, part_send, part_recv, mid_send, mid_recv, sums_send, sums_recv,
    rows_send, rows_recv, codes_send, codes_recv, own_sem,
):
    loads = [
        pltpu.make_async_copy(there, here, load_sem.at[i])
        for i, (there, here) in enumerate([
            (grad_hbm, buf.at[0, pl.ds(256, 256)]), (scen_hbm, scen_ref), (gate_hbm, gate_ref),
            (cand_hbm, cand_ref), (user_hbm, user_ref), (norm_hbm, norm_ref), (fwd_hbm, fwd_ref),
            (hist_hbm, hist_ref), (length_hbm, length_ref), (item_hbm, item_ref),
        ])
    ]
    for load in loads:
        load.start()

    dp = lax.axis_index("dp")
    seq = lax.axis_index("seq")
    x, core = dp // 2, dp % 2
    y, z = seq // 4, seq % 4

    xs = [(x + d) % 4 for d in range(4)]
    ys = [(y + d) % 4 for d in range(4)]
    zs = [(z + d) % 4 for d in range(4)]
    cores = [core, 1 - core]

    def device(dy, dz):
        return (dp, ys[dy % 4] * 4 + zs[dz % 4])

    barrier = pltpu.get_barrier_semaphore()

    lines = [(ys[d] * 4 + z, dp) for d in range(1, 4)] + [(y * 4 + zs[d], dp) for d in range(1, 4)]
    lines += [(seq, xs[d] * 2 + c) for d in range(4) for c in cores][1:]
    for there, group in lines:
        pl.semaphore_signal(barrier, inc=1, device_id=(group, there), device_id_type=MESH)

    def block_copy(number):
        _, offset, quarter, (dy, dz) = SENDS[number]
        there = SLOT[(offset[0] - dy) % 4, (offset[1] - dz) % 4]
        rows = pl.ds(*QUARTERS[quarter])
        return pltpu.make_async_remote_copy(
            src_ref=buf.at[SLOT[offset], rows],
            dst_ref=buf.at[there, rows],
            send_sem=send_sem.at[number],
            recv_sem=recv_sem.at[there, quarter],
            device_id=device(dy, dz),
            device_id_type=MESH,
        )

    def block_arrival(offset, quarter):
        rows = pl.ds(*QUARTERS[quarter])
        slot = SLOT[offset]
        return pltpu.make_async_remote_copy(
            src_ref=buf.at[slot, rows],
            dst_ref=buf.at[slot, rows],
            send_sem=send_sem.at[0],
            recv_sem=recv_sem.at[slot, quarter],
            device_id=device(0, 1),
            device_id_type=MESH,
        )

    def line_copy(source, there, half, step, send, recv):
        return pltpu.make_async_remote_copy(
            src_ref=source, dst_ref=there, send_sem=send, recv_sem=recv,
            device_id=device(0, step) if half == 0 else device(step, 0),
            device_id_type=MESH,
        )

    def route(i, half):
        dy, dz = ORDER[i]
        return (dz, dy) if half == 0 else (dy, dz)

    def toward(across):
        return -1 if across % 2 == 0 else 1

    def part_copy(i, half):
        step, across = route(i, half)
        send = part_send.at[i, half]
        if step == 2:
            there, recv, step = mid_in.at[half, across], mid_recv.at[half, across], toward(across)
        else:
            there, recv, step = part_in.at[half, 1, across], part_recv.at[half, 1, across], -toward(across)
        return line_copy(part_out.at[i, half], there, half, step, send, recv)

    def mid_copy(half, across):
        return line_copy(
            mid_out.at[half, across], part_in.at[half, 0, across], half, toward(across),
            mid_send.at[half, across], part_recv.at[half, 0, across],
        )

    parts = []
    for i in range(1, 16):
        for h in range(2):
            step, across = route(i, h)
            if step == 2 or (step and step % 4 == -toward(across) % 4):
                parts.append((i, h))

    def send_parts(i):
        for h in range(2):
            if (i, h) in parts:
                part_copy(i, h).start()

    def pass_on(h, across):
        step = toward(across) % 4
        own = SLOT[(across, step) if h == 0 else (step, across)]
        line_copy(
            mid_out.at[h, across], mid_in.at[h, across], h, 1, mid_send.at[h, across], mid_recv.at[h, across]
        ).wait_recv()
        low, high = restored(part_out[own, h, 0:128], part_out[own, h, 128:129])
        a, b = restored(mid_in[h, across, 0:128], mid_in[h, across, 128:129])
        words, power = quantized(jnp.concatenate([low + a, high + b], axis=0))
        mid_out[h, across, 0:128] = words
        mid_out[h, across, 128:136] = power
        mid_copy(h, across).start()

    def sums_copy(half, step):
        return pltpu.make_async_remote_copy(
            src_ref=sums_out.at[half, step - 1],
            dst_ref=sums_in.at[half, 3 - step],
            send_sem=sums_send.at[half, step - 1],
            recv_sem=sums_recv.at[half, 3 - step],
            device_id=device(step, 0) if half == 0 else device(0, step),
            device_id_type=MESH,
        )

    def run_plan(step):
        for event in PLAN[step]:
            if event[0] == "wait":
                for quarter in event[2]:
                    block_arrival(event[1], quarter).wait_recv()
            elif event[0] == "send":
                block_copy(SENDS.index(event)).start()
            else:
                send_parts(event[1])

    early = [event for event in PLAN[0] if event[2] == 2]
    late = [event for event in PLAN[0] if event[2] != 2]
    loads[0].wait()
    pl.semaphore_wait(barrier, 13)
    for event in early:
        block_copy(SENDS.index(event)).start()
    for load in loads[1:7]:
        load.wait()
    scen_rows = scen_ref[...] == lax.broadcasted_iota(jnp.int32, (16, 256), 0)
    gates[...] = lax.dot_general(
        scen_rows.astype(jnp.float32), gate_ref[...], (((0,), (0,)), ((), ())),
        precision=lax.Precision.HIGHEST, preferred_element_type=jnp.float32,
    )
    queries = (cand_ref[...].astype(jnp.float32) * gates[...]).astype(jnp.bfloat16)
    buf[0, 0:256] = queries * jnp.bfloat16(0.0625)
    grads = buf[0, 256:512]
    inner = lax.dot_general(
        jnp.ones((8, 256), jnp.float32),
        grads.astype(jnp.float32) * fwd_ref[...].astype(jnp.float32),
        (((1,), (1,)), ((), ())),
        precision=lax.Precision.HIGHEST, preferred_element_type=jnp.float32,
    )[0:1]
    user = (user_ref[...] - 2 * dp).astype(jnp.float32)
    numbers = [*split3(norm_ref[...]), *split3(inner), 1.0 - user, user]
    numbers = jnp.concatenate(numbers + [jnp.zeros((8, 256), jnp.float32)], axis=0)
    buf[0, 512:528] = numbers.astype(jnp.bfloat16)

    for event in late:
        block_copy(SENDS.index(event)).start()

    first = seq * 512
    places = first + lax.broadcasted_iota(jnp.int32, (512, 256), 0)
    for load in loads[7:]:
        load.wait()
    for u in range(2):
        rows = hist_ref[u].astype(jnp.float32)
        keys[u] = jnp.where(places < length_ref[u], rows, 0.0).astype(jnp.bfloat16)
    hist_sum[...] = jnp.zeros_like(hist_sum)
    def rank_items():
        items = jnp.concatenate([item_ref[0:1], item_ref[1:2]], axis=1)
        owner = items // ITEM_DEV
        other = [owner // 32, owner // 16 % 2, owner // 4 % 4, owner % 4]
        off_x, off_y, off_z = (other[0] - x + 4) % 4, (other[2] - y + 4) % 4, (other[3] - z + 4) % 4
        message = (other[1] + core) % 2 * 64 + (off_z + 8 - off_x - off_y) % 4 * 16 + off_y * 4 + off_x
        found = lax.broadcasted_iota(jnp.int32, (128, 1024), 0) == message
        column = jnp.transpose(jnp.broadcast_to(items.astype(jnp.float32), (128, 1024)))[:, 0:1]
        same = column == items.astype(jnp.float32)
        one, zero = jnp.float32(1.0), jnp.float32(0.0)
        alike[...] = jnp.where(same, one, zero).astype(jnp.bfloat16)
        number = lax.broadcasted_iota(jnp.int32, (1024, 1024), 0)
        other_number = lax.broadcasted_iota(jnp.int32, (1024, 1024), 1)
        repeats = jnp.sum(jnp.where(same & (number < other_number), one, zero), axis=0, keepdims=True)
        first = jnp.where(repeats == 0.0, one, zero)
        matches[...] = jnp.where(found, first, zero)
        counts = jnp.dot(
            matches[...].astype(jnp.bfloat16), jnp.where(number <= other_number, one, zero).astype(jnp.bfloat16),
            preferred_element_type=jnp.float32,
        )
        rank = jnp.sum(matches[...] * counts, axis=0, keepdims=True) - first
        rank = jnp.dot(
            jnp.broadcast_to(rank, (8, 1024)).astype(jnp.bfloat16), alike[...], preferred_element_type=jnp.float32
        )[0:1].astype(jnp.int32)
        places_of[0:1] = message * 16 + rank
        places_of[1:2] = rank
        place = (items % ITEM_DEV) * 2 + 16
        column = lax.broadcasted_iota(jnp.int32, (128, 1024), 0)
        number = jnp.where(column < 16, place % 256, jnp.where(column < 32, 0, place // 256))
        ranked = (column % 16 == rank) & (column < 48)
        code_rows[...] = jnp.where(ranked, number, 0).astype(jnp.float32)
        code_spots[...] = jnp.where(ranked & (column >= 16) & (column < 32), one, zero)

    def products_of(k):
        numbers = buf[k, 512:528].astype(jnp.float32)
        normalizer = numbers[0:1] + numbers[1:2] + numbers[2:3]
        inner_sum = numbers[3:4] + numbers[4:5] + numbers[5:6]
        pick = [numbers[6:7], numbers[7:8]]
        low = [w.astype(jnp.bfloat16) for w in pick]
        both = buf[k, 0:512]
        mine = keys[0] * low[0] + keys[1] * low[1]
        products = nt(mine, both)
        probability = jnp.exp(products[:, :256] - normalizer)
        score_grad = (probability * (products[:, 256:] - inner_sum)).astype(jnp.bfloat16)
        weights = jnp.concatenate([score_grad, probability.astype(jnp.bfloat16)], axis=1)
        key_part = jnp.dot(weights, both, preferred_element_type=jnp.float32)
        return pick, key_part, tn(score_grad, mine)

    def keep_part(k, query_part):
        words, power = quantized(query_part)
        for h in range(2):
            columns = slice(h * 128, (h + 1) * 128)
            part_out[k, h, 0:128] = words[:, columns]
            part_out[k, h, 128:136] = power[:, columns]

    def one_step(k):
        pick, key_part, query_part = products_of(k)
        hist_sum[0] += key_part * pick[0]
        hist_sum[1] += key_part * pick[1]
        keep_part(k, query_part)

    def two_steps(n, carry):
        k = n * 2 + 1
        for i in range(1, 15, 2):
            if PLAN[i] or PLAN[i + 1]:

                @pl.when(k == i)
                def _(i=i):
                    run_plan(i)
                    run_plan(i + 1)

        pick, key_part, query_part = products_of(k)
        next_pick, next_key_part, next_query_part = products_of(k + 1)
        for u in range(2):
            hist_sum[u] += key_part * pick[u] + next_key_part * next_pick[u]
        keep_part(k, query_part)
        keep_part(k + 1, next_query_part)
        for i in range(11, 15, 2):

            @pl.when(k == i)
            def _(i=i):
                send_parts(i)
                send_parts(i + 1)

        return carry

    one_step(0)
    rank_items()
    lax.fori_loop(0, 7, two_steps, 0)
    run_plan(15)
    one_step(15)
    send_parts(15)

    tops = []
    for u in range(2):
        hist_sum[u] = jnp.where(places < length_ref[u], hist_sum[u], 0.0)
        top = jnp.max(jnp.abs(hist_sum[u]), axis=1, keepdims=True) * 1.01
        tops.append(jnp.broadcast_to(top, (512, 128)).astype(jnp.bfloat16))
    power = power_of(jnp.dot(alike[...], jnp.concatenate(tops, axis=0), preferred_element_type=jnp.float32))
    scale = jnp.exp2(15.0 - power) * 0.99
    for u in range(2):
        rows = pl.ds(u * 512, 512)
        for h in range(2):
            q = jnp.round(hist_sum[u, :, h * 128 : h * 128 + 128] * scale[u * 512 : u * 512 + 512]).astype(jnp.int32)
            halves[rows, h * 128 : h * 128 + 128] = (q >> 8).astype(jnp.float32).astype(jnp.bfloat16)
            halves[rows, 256 + h * 128 : 384 + h * 128] = (q & 255).astype(jnp.float32).astype(jnp.bfloat16)
    first_lane = lax.broadcasted_iota(jnp.int32, (1024, 128), 1) == 0
    power = nt(jnp.ones((8, 128), jnp.bfloat16), jnp.where(first_lane, power, 0.0).astype(jnp.bfloat16))[0:1]
    codes = nt(
        matches[...].astype(jnp.bfloat16),
        (code_rows[...] + code_spots[...] * (power + 128.0)).astype(jnp.bfloat16),
    )
    codes_out[...] = codes.astype(jnp.int32).reshape(128, 1, 128)

    def rows_copy(m, there):
        return pltpu.make_async_remote_copy(
            src_ref=rows_out.at[m], dst_ref=rows_in.at[m], send_sem=rows_send, recv_sem=rows_recv,
            device_id=there, device_id_type=MESH,
        )

    def codes_copy(m, there):
        return pltpu.make_async_remote_copy(
            src_ref=codes_out.at[m], dst_ref=codes_in.at[m], send_sem=codes_send, recv_sem=codes_recv,
            device_id=there, device_id_type=MESH,
        )

    own_rows = pltpu.make_async_copy(rows_out.at[0], rows_in.at[0], own_sem.at[0])
    own_codes = pltpu.make_async_copy(codes_out.at[0], codes_in.at[0], own_sem.at[1])

    def send_chunk(c, carry):
        slots = lax.broadcasted_iota(jnp.int32, (256, 1024), 0) + c * 256
        chosen = jnp.where(slots == places_of[0:1], 1.0, 0.0).astype(jnp.bfloat16)
        moved = jnp.dot(chosen, halves[...], preferred_element_type=jnp.float32).astype(jnp.int32)
        value = (moved[:, 0:256] << 8) + moved[:, 256:512]
        words = (value[:, 128:256] << 16) | (value[:, 0:128] & 0xFFFF)
        rows_out[pl.ds(c * 16, 16)] = words.reshape(16, 16, 128)

        to_core = (core + c // 4) % 2
        to_z = [(z + c + d) % 4 for d in range(4)]
        for j in range(16):
            m = c * 16 + j
            there = (xs[j % 4] * 2 + to_core, ys[j // 4] * 4 + to_z[(j + j // 4) % 4])

            def send_one(m=m, there=there):
                rows_copy(m, there).start()
                codes_copy(m, there).start()

            if j == 0:
                pl.when(c > 0)(send_one)
            else:
                send_one()
        return carry

    lax.fori_loop(0, 2, send_chunk, 0)
    for across in (0, 1, 3, 2):
        for h in range(2):
            pass_on(h, across)

    lax.fori_loop(2, 8, send_chunk, 0)
    own_rows.start()
    own_codes.start()

    for h in range(2):
        for j in range(2):
            for across in range(4):
                line_copy(
                    part_in.at[h, j, across], part_in.at[h, j, across], h, 1,
                    mid_send.at[h, across], part_recv.at[h, j, across],
                ).wait_recv()
    firsts = []
    for h in range(2):
        for d in range(4):
            own = SLOT[(d, 0) if h == 0 else (0, d)]
            low, high = restored(part_out[own, h, 0:128], part_out[own, h, 128:129])
            for source in range(2):
                a, b = restored(part_in[h, source, d, 0:128], part_in[h, source, d, 128:129])
                low, high = low + a, high + b
            if d == 0:
                firsts.append((low, high))
            else:
                words, power = quantized(jnp.concatenate([low, high], axis=0))
                sums_out[h, d - 1, 0:128] = words
                sums_out[h, d - 1, 128:136] = power
                sums_copy(h, d).start()
    for h in range(2):
        low, high = firsts[h]
        for d in range(1, 4):
            sums_copy(h, d).wait_recv()
        for source in range(3):
            a, b = restored(sums_in[h, source, 0:128], sums_in[h, source, 128:129])
            low, high = low + a, high + b
        columns = slice(h * 128, (h + 1) * 128)
        cand_out[0:128, columns] = low * 0.0625 * gates[0:128, columns]
        cand_out[128:256, columns] = high * 0.0625 * gates[128:256, columns]
    for number in range(len(SENDS)):
        block_copy(number).wait_send()
    for i, h in parts:
        part_copy(i, h).wait_send()
    for h in range(2):
        for across in range(4):
            mid_copy(h, across).wait_send()
    for h in range(2):
        for d in range(1, 4):
            sums_copy(h, d).wait_send()
    own_rows.wait()
    own_codes.wait()
    others = pl.ds(1, 127)
    all_rows = pltpu.make_async_remote_copy(
        src_ref=rows_out.at[others], dst_ref=rows_in.at[others], send_sem=rows_send, recv_sem=rows_recv,
        device_id=device(0, 1), device_id_type=MESH,
    )
    all_codes = pltpu.make_async_remote_copy(
        src_ref=codes_out.at[others], dst_ref=codes_in.at[others], send_sem=codes_send, recv_sem=codes_recv,
        device_id=device(0, 1), device_id_type=MESH,
    )
    all_codes.wait()
    got = jnp.transpose(codes_in[...].reshape(128, 128).astype(jnp.float32)).astype(jnp.int32)
    codes_out_t[0:16] = got[0:16] + got[32:48] * 256
    codes_out_t[16:32] = got[16:32]
    all_rows.wait()


def table_kernel(
    rows_hbm, codes_hbm, cand_hbm, table_out, cand_out,
    rows_ref, codes_ref, powers_ref, cand_ref, values, t0, t1, table, sem
):
    loads = [
        pltpu.make_async_copy(codes_hbm.at[0:16], codes_ref, sem.at[9]),
        pltpu.make_async_copy(codes_hbm.at[16:32], powers_ref, sem.at[10]),
        pltpu.make_async_copy(cand_hbm, cand_ref, sem.at[11]),
    ]
    for part in range(4):
        rows = pl.ds(part * 512, 512)
        loads.append(pltpu.make_async_copy(rows_hbm.at[rows], rows_ref.at[rows], sem.at[12 + part]))
    for load in loads:
        load.start()
    cand_copy = pltpu.make_async_copy(cand_ref, cand_out, sem.at[8])

    def clear(c, carry):
        for t in (t0, t1):
            t[pl.ds(c * 1024, 1024)] = jnp.zeros((1024, 128), jnp.float32)
        return carry

    lax.fori_loop(0, 8, clear, 0)
    for t in (t0, t1):
        t[8192:8208] = jnp.zeros((16, 128), jnp.float32)

    for load in loads[:3]:
        load.wait()
    cand_copy.start()
    scales = jnp.exp2(powers_ref[...].astype(jnp.float32) - 143.0) * (1.0 / 0.99)
    for m in range(128):
        if m % 32 == 0:
            loads[3 + m // 32].wait()
        scale = scales[:, m : m + 1]
        words = rows_ref[m * 16 : m * 16 + 16]
        values[pl.ds(m * 32, 16, stride=2)] = ((words << 16) >> 16).astype(jnp.float32) * scale
        values[pl.ds(m * 32 + 1, 16, stride=2)] = (words >> 16).astype(jnp.float32) * scale

    def add_messages(i, carry):
        pair = ((t0, i * 2), (t1, i * 2 + 1))
        places = [[pl.ds(pl.multiple_of(codes_ref[j, m], 2), 2) for j in range(16)] for _, m in pair]
        sums = [
            [t[places[n][j]] + values[pl.ds(m * 32 + j * 2, 2)] for j in range(16)] for n, (t, m) in enumerate(pair)
        ]
        for n, (t, m) in enumerate(pair):
            for j in range(16):
                t[places[n][j]] = sums[n][j]
        return carry

    lax.fori_loop(0, 64, add_messages, 0)

    def out_copy(c):
        rows = pl.ds(c * 512, 512)
        return pltpu.make_async_copy(table.at[rows], table_out.at[rows], sem.at[c])

    for c in range(8):
        for h in range(2):
            rows = pl.ds(16 + c * 1024 + h, 512, stride=2)
            table[c * 512 : c * 512 + 512, h * 128 : h * 128 + 128] = t0[rows] + t1[rows]
        out_copy(c).start()
    for c in range(8):
        out_copy(c).wait()
    cand_copy.wait()


def add_rows(rows, codes, candidate_grad):
    hbm = pl.BlockSpec(memory_space=pltpu.HBM)
    return pl.pallas_call(
        table_kernel,
        out_shape=(
            jax.ShapeDtypeStruct((ITEM_DEV, 256), jnp.float32),
            jax.ShapeDtypeStruct((256, 256), jnp.float32),
        ),
        in_specs=[hbm, hbm, hbm],
        out_specs=(hbm, hbm),
        scratch_shapes=[
            pltpu.VMEM((2048, 128), jnp.int32),
            pltpu.SMEM((16, 128), jnp.int32),
            pltpu.VMEM((16, 128), jnp.int32),
            pltpu.VMEM((256, 256), jnp.float32),
            pltpu.VMEM((4104, 128), jnp.float32),
            pltpu.VMEM((2 * ITEM_DEV + 32, 128), jnp.float32),
            pltpu.VMEM((2 * ITEM_DEV + 32, 128), jnp.float32),
            pltpu.VMEM((ITEM_DEV, 256), jnp.float32),
            pltpu.SemaphoreType.DMA((16,)),
        ],
        compiler_params=pltpu.CompilerParams(vmem_limit_bytes=64 * 1024 * 1024),
        cost_estimate=pl.CostEstimate(flops=2_000_000, bytes_accessed=5_500_000, transcendentals=0),
        name="table_rows",
    )(rows, codes, candidate_grad)


def attention(candidates, scenarios, users, gate_table, normalizer, forward_out, out_grad, history, items, lengths):
    vmem = pl.BlockSpec(memory_space=pltpu.VMEM)
    return pl.pallas_call(
        attention_kernel,
        out_shape=(
            jax.ShapeDtypeStruct((256, 256), jnp.float32),
            jax.ShapeDtypeStruct((128, 16, 128), jnp.int32),
            jax.ShapeDtypeStruct((32, 128), jnp.int32),
        ),
        in_specs=[pl.BlockSpec(memory_space=pltpu.HBM)] * 10,
        out_specs=(vmem, pl.BlockSpec(memory_space=pl.ANY), vmem),
        scratch_shapes=[
            pltpu.VMEM((256, 256), jnp.bfloat16),
            pltpu.VMEM((1, 256), jnp.int32),
            pltpu.VMEM((1, 256), jnp.int32),
            pltpu.VMEM((16, 256), jnp.float32),
            pltpu.VMEM((1, 256), jnp.float32),
            pltpu.VMEM((256, 256), jnp.bfloat16),
            pltpu.VMEM((2, 512, 256), jnp.bfloat16),
            pltpu.VMEM((2, 512), jnp.int32),
            pltpu.SMEM((2,), jnp.int32),
            pltpu.VMEM((16, BLOCK, 256), jnp.bfloat16),
            pltpu.VMEM((2, 512, 256), jnp.bfloat16),
            pltpu.VMEM((256, 256), jnp.float32),
            pltpu.VMEM((16, 2, 136, 128), jnp.int32),
            pltpu.VMEM((2, 2, 4, 136, 128), jnp.int32),
            pltpu.VMEM((2, 4, 136, 128), jnp.int32),
            pltpu.VMEM((2, 4, 136, 128), jnp.int32),
            pltpu.VMEM((2, 3, 136, 128), jnp.int32),
            pltpu.VMEM((2, 3, 136, 128), jnp.int32),
            pltpu.VMEM((2, 512, 256), jnp.float32),
            pltpu.VMEM((1024, 1024), jnp.bfloat16),
            pltpu.VMEM((128, 1024), jnp.float32),
            pltpu.VMEM((8, 1024), jnp.int32),
            pltpu.VMEM((1024, 512), jnp.bfloat16),
            pltpu.VMEM((128, 16, 128), jnp.int32),
            pltpu.VMEM((128, 1, 128), jnp.int32),
            pltpu.VMEM((128, 1, 128), jnp.int32),
            pltpu.VMEM((128, 1024), jnp.float32),
            pltpu.VMEM((128, 1024), jnp.float32),
            pltpu.SemaphoreType.DMA((10,)),
            pltpu.SemaphoreType.DMA((len(SENDS),)),
            pltpu.SemaphoreType.DMA((16, 4)),
            pltpu.SemaphoreType.DMA((16, 2)),
            pltpu.SemaphoreType.DMA((2, 2, 4)),
            pltpu.SemaphoreType.DMA((2, 4)),
            pltpu.SemaphoreType.DMA((2, 4)),
            pltpu.SemaphoreType.DMA((2, 3)),
            pltpu.SemaphoreType.DMA((2, 3)),
            pltpu.SemaphoreType.DMA,
            pltpu.SemaphoreType.DMA,
            pltpu.SemaphoreType.DMA,
            pltpu.SemaphoreType.DMA,
            pltpu.SemaphoreType.DMA((2,)),
        ],
        compiler_params=pltpu.CompilerParams(
            collective_id=0, has_side_effects=True, vmem_limit_bytes=64 * 1024 * 1024
        ),
        cost_estimate=pl.CostEstimate(
            flops=5_400_000_000, bytes_accessed=4_000_000, transcendentals=2_100_000
        ),
        name="attention_grads",
    )(
        candidates, scenarios.reshape(1, -1), users.reshape(1, -1), gate_table, normalizer.reshape(1, -1),
        forward_out, out_grad, history, items, lengths,
    )


def local(
    candidates,
    scenarios,
    candidate_user,
    gate_table,
    log_normalizer,
    forward_out,
    out_grad,
    history,
    history_length,
    history_items,
):
    candidate_grad, rows, codes = attention(
        candidates, scenarios, candidate_user, gate_table, log_normalizer,
        forward_out, out_grad, history, history_items, history_length,
    )
    table_grad, candidate_grad = add_rows(rows.reshape(2048, 128), codes, candidate_grad)
    return (candidate_grad, table_grad)


def solution(mesh):
    return jax.shard_map(
        local,
        mesh=mesh,
        in_specs=(
            P(("dp", "seq"), None),
            P(("dp", "seq")),
            P(("dp", "seq")),
            P(),
            P(("dp", "seq")),
            P(("dp", "seq"), None),
            P(("dp", "seq"), None),
            P("dp", "seq", None),
            P("dp"),
            P("dp", "seq"),
        ),
        out_specs=(P(("dp", "seq"), None), P(("dp", "seq"), None)),
        check_vma=False,
    )
```

```python
import math

import jax
import jax.numpy as jnp
from jax import lax
from jax.experimental import pallas as pl
from jax.experimental.pallas import tpu as pltpu
from jax.sharding import PartitionSpec as P

ITEM_DEV = 4096
MESH = pl.DeviceIdType.MESH

ORDER = [
    (0, 0), (0, 1), (0, 3), (1, 0), (3, 0), (1, 1), (1, 3), (3, 1), (3, 3),
    (0, 2), (2, 0), (1, 2), (2, 1), (3, 2), (2, 3), (2, 2),
]
SLOT = {offset: i for i, offset in enumerate(ORDER)}
QUARTERS = [(0, 128), (128, 128), (256, 128), (384, 144)]
BLOCK = 528
YP, YM, ZP, ZM = (1, 0), (-1, 0), (0, 1), (0, -1)


def forward_plan():
    plan = {i: [] for i in range(16)}

    def wait(step, offset, quarters):
        plan[step].append(("wait", offset, quarters))

    def send(step, offset, quarter, direction):
        plan[step].append(("send", offset, quarter, direction))

    a, b = (0, 1), (2, 3)
    for q in a:
        send(0, (0, 0), q, ZP)
        send(0, (0, 0), q, ZM)
    for q in b:
        send(0, (0, 0), q, YP)
        send(0, (0, 0), q, YM)
    for q in a:
        send(0, (0, 0), q, YP)
        send(0, (0, 0), q, YM)
    for q in b:
        send(0, (0, 0), q, ZP)
        send(0, (0, 0), q, ZM)
    for q in (0, 1):
        for offset in ((0, 1), (0, 3)):
            wait(1, offset, (a[q],))
        for offset in ((1, 0), (3, 0)):
            wait(1, offset, (b[q],))
        if q == 0:
            send(1, (0, 3), 0, ZP)
            send(1, (3, 0), 2, YP)
        else:
            send(1, (0, 1), 1, ZM)
            send(1, (1, 0), 3, YM)
        for offset in ((0, 1), (0, 3)):
            send(1, offset, a[q], YP)
            send(1, offset, a[q], YM)
        for offset in ((1, 0), (3, 0)):
            send(1, offset, b[q], ZP)
            send(1, offset, b[q], ZM)
    for q in (0, 1):
        for offset in ((0, 1), (0, 3)):
            wait(1, offset, (b[q],))
        for offset in ((1, 0), (3, 0)):
            wait(1, offset, (a[q],))
        if q == 0:
            send(1, (0, 3), 2, ZP)
            send(1, (3, 0), 0, YP)
        else:
            send(1, (0, 1), 3, ZM)
            send(1, (1, 0), 1, YM)
    for q in (0, 1):
        wait(3, (0, 2), (a[q],))
        wait(3, (2, 0), (b[q],))
        send(3, (0, 2), a[q], YP)
        send(3, (0, 2), a[q], YM)
        send(3, (2, 0), b[q], ZP)
        send(3, (2, 0), b[q], ZM)
    wait(5, (1, 1), a + b)
    send(5, (1, 1), 1, YM)
    send(5, (1, 1), 3, ZM)
    wait(6, (1, 3), a + b)
    send(6, (1, 3), 1, YM)
    send(6, (1, 3), 2, ZP)
    wait(6, (3, 1), a + b)
    send(6, (3, 1), 0, YP)
    send(6, (3, 1), 3, ZM)
    wait(6, (3, 3), a + b)
    send(6, (3, 3), 0, YP)
    send(6, (3, 3), 2, ZP)
    wait(9, (0, 2), b)
    wait(9, (2, 0), a)
    wait(10, (3, 2), a)
    wait(10, (1, 2), a)
    send(10, (3, 2), 0, YP)
    send(10, (1, 2), 1, YM)
    wait(10, (2, 3), b)
    wait(10, (2, 1), b)
    send(10, (2, 3), 2, ZP)
    send(10, (2, 1), 3, ZM)
    plan[11] += [("parts", i) for i in range(1, 11)]
    wait(11, (1, 2), b)
    wait(12, (2, 1), a)
    wait(13, (3, 2), b)
    wait(14, (2, 3), a)
    wait(15, (2, 2), a + b)
    return plan


PLAN = forward_plan()
SENDS = [e for i in range(16) for e in PLAN[i] if e[0] == "send"]


def split3(x):
    hi = x.astype(jnp.bfloat16).astype(jnp.float32)
    rest = x - hi
    mid = rest.astype(jnp.bfloat16).astype(jnp.float32)
    return hi, mid, rest - mid


def nt(a, b):
    return lax.dot_general(a, b, (((1,), (1,)), ((), ())), preferred_element_type=jnp.float32)


def tn(a, b):
    return lax.dot_general(a, b, (((0,), (0,)), ((), ())), preferred_element_type=jnp.float32)


def power_of(top):
    power = jnp.ceil(jnp.log(jnp.maximum(top, 1e-33)) * (1.0 / math.log(2.0)))
    return jnp.clip(power, -110.0, 127.0)


def quantized(x):
    top = jnp.max(jnp.abs(x), axis=0, keepdims=True)
    power = power_of(top)
    q = jnp.round(x * (jnp.exp2(15.0 - power) * 0.99)).astype(jnp.int32)
    half = x.shape[0] // 2
    words = (q[half:] << 16) | (q[:half] & 0xFFFF)
    return words, jnp.broadcast_to(power.astype(jnp.int32), (8, x.shape[1]))


def restored(words, power):
    scale = jnp.exp2(power.astype(jnp.float32) - 15.0) * (1.0 / 0.99)
    low = ((words << 16) >> 16).astype(jnp.float32) * scale
    high = (words >> 16).astype(jnp.float32) * scale
    return low, high


def attention_kernel(
    cand_hbm, scen_hbm, user_hbm, gate_hbm, norm_hbm, fwd_hbm, grad_hbm, hist_hbm, item_hbm, length_hbm,
    cand_out, rows_in, codes_out_t,
    cand_ref, scen_ref, user_ref, gate_ref, norm_ref, fwd_ref, hist_ref, item_ref, length_ref,
    buf, keys, gates, part_out, part_in, mid_out, mid_in, sums_out, sums_in, hist_sum, alike, matches, places_of, halves, rows_out, codes_out, codes_in, code_rows, code_spots,
    load_sem, send_sem, recv_sem, part_send, part_recv, mid_send, mid_recv, sums_send, sums_recv,
    rows_send, rows_recv, codes_send, codes_recv, own_sem,
):
    loads = [
        pltpu.make_async_copy(there, here, load_sem.at[i])
        for i, (there, here) in enumerate([
            (grad_hbm, buf.at[0, pl.ds(256, 256)]), (scen_hbm, scen_ref), (gate_hbm, gate_ref),
            (cand_hbm, cand_ref), (user_hbm, user_ref), (norm_hbm, norm_ref), (fwd_hbm, fwd_ref),
            (hist_hbm, hist_ref), (length_hbm, length_ref), (item_hbm, item_ref),
        ])
    ]
    for load in loads:
        load.start()

    dp = lax.axis_index("dp")
    seq = lax.axis_index("seq")
    x, core = dp // 2, dp % 2
    y, z = seq // 4, seq % 4

    xs = [(x + d) % 4 for d in range(4)]
    ys = [(y + d) % 4 for d in range(4)]
    zs = [(z + d) % 4 for d in range(4)]
    cores = [core, 1 - core]

    def device(dy, dz):
        return (dp, ys[dy % 4] * 4 + zs[dz % 4])

    barrier = pltpu.get_barrier_semaphore()

    lines = [(ys[d] * 4 + z, dp) for d in range(1, 4)] + [(y * 4 + zs[d], dp) for d in range(1, 4)]
    lines += [(seq, xs[d] * 2 + c) for d in range(4) for c in cores][1:]
    for there, group in lines:
        pl.semaphore_signal(barrier, inc=1, device_id=(group, there), device_id_type=MESH)

    def block_copy(number):
        _, offset, quarter, (dy, dz) = SENDS[number]
        there = SLOT[(offset[0] - dy) % 4, (offset[1] - dz) % 4]
        rows = pl.ds(*QUARTERS[quarter])
        return pltpu.make_async_remote_copy(
            src_ref=buf.at[SLOT[offset], rows],
            dst_ref=buf.at[there, rows],
            send_sem=send_sem.at[number],
            recv_sem=recv_sem.at[there, quarter],
            device_id=device(dy, dz),
            device_id_type=MESH,
        )

    def block_arrival(offset, quarter):
        rows = pl.ds(*QUARTERS[quarter])
        slot = SLOT[offset]
        return pltpu.make_async_remote_copy(
            src_ref=buf.at[slot, rows],
            dst_ref=buf.at[slot, rows],
            send_sem=send_sem.at[0],
            recv_sem=recv_sem.at[slot, quarter],
            device_id=device(0, 1),
            device_id_type=MESH,
        )

    def line_copy(source, there, half, step, send, recv):
        return pltpu.make_async_remote_copy(
            src_ref=source, dst_ref=there, send_sem=send, recv_sem=recv,
            device_id=device(0, step) if half == 0 else device(step, 0),
            device_id_type=MESH,
        )

    def route(i, half):
        dy, dz = ORDER[i]
        return (dz, dy) if half == 0 else (dy, dz)

    def toward(across):
        return -1 if across % 2 == 0 else 1

    def part_copy(i, half):
        step, across = route(i, half)
        send = part_send.at[i, half]
        if step == 2:
            there, recv, step = mid_in.at[half, across], mid_recv.at[half, across], toward(across)
        else:
            there, recv, step = part_in.at[half, 1, across], part_recv.at[half, 1, across], -toward(across)
        return line_copy(part_out.at[i, half], there, half, step, send, recv)

    def mid_copy(half, across):
        return line_copy(
            mid_out.at[half, across], part_in.at[half, 0, across], half, toward(across),
            mid_send.at[half, across], part_recv.at[half, 0, across],
        )

    parts = []
    for i in range(1, 16):
        for h in range(2):
            step, across = route(i, h)
            if step == 2 or (step and step % 4 == -toward(across) % 4):
                parts.append((i, h))

    def send_parts(i):
        for h in range(2):
            if (i, h) in parts:
                part_copy(i, h).start()

    def pass_on(h, across):
        step = toward(across) % 4
        own = SLOT[(across, step) if h == 0 else (step, across)]
        line_copy(
            mid_out.at[h, across], mid_in.at[h, across], h, 1, mid_send.at[h, across], mid_recv.at[h, across]
        ).wait_recv()
        low, high = restored(part_out[own, h, 0:128], part_out[own, h, 128:129])
        a, b = restored(mid_in[h, across, 0:128], mid_in[h, across, 128:129])
        words, power = quantized(jnp.concatenate([low + a, high + b], axis=0))
        mid_out[h, across, 0:128] = words
        mid_out[h, across, 128:136] = power
        mid_copy(h, across).start()

    def sums_copy(half, step):
        return pltpu.make_async_remote_copy(
            src_ref=sums_out.at[half, step - 1],
            dst_ref=sums_in.at[half, 3 - step],
            send_sem=sums_send.at[half, step - 1],
            recv_sem=sums_recv.at[half, 3 - step],
            device_id=device(step, 0) if half == 0 else device(0, step),
            device_id_type=MESH,
        )

    def run_plan(step):
        for event in PLAN[step]:
            if event[0] == "wait":
                for quarter in event[2]:
                    block_arrival(event[1], quarter).wait_recv()
            elif event[0] == "send":
                block_copy(SENDS.index(event)).start()
            else:
                send_parts(event[1])

    early = [event for event in PLAN[0] if event[2] == 2]
    late = [event for event in PLAN[0] if event[2] != 2]
    loads[0].wait()
    pl.semaphore_wait(barrier, 13)
    for event in early:
        block_copy(SENDS.index(event)).start()
    for load in loads[1:7]:
        load.wait()
    scen_rows = scen_ref[...] == lax.broadcasted_iota(jnp.int32, (16, 256), 0)
    gates[...] = lax.dot_general(
        scen_rows.astype(jnp.float32), gate_ref[...], (((0,), (0,)), ((), ())),
        precision=lax.Precision.HIGHEST, preferred_element_type=jnp.float32,
    )
    queries = (cand_ref[...].astype(jnp.float32) * gates[...]).astype(jnp.bfloat16)
    buf[0, 0:256] = queries * jnp.bfloat16(0.0625)
    grads = buf[0, 256:512]
    inner = lax.dot_general(
        jnp.ones((8, 256), jnp.float32),
        grads.astype(jnp.float32) * fwd_ref[...].astype(jnp.float32),
        (((1,), (1,)), ((), ())),
        precision=lax.Precision.HIGHEST, preferred_element_type=jnp.float32,
    )[0:1]
    user = (user_ref[...] - 2 * dp).astype(jnp.float32)
    numbers = [*split3(norm_ref[...]), *split3(inner), 1.0 - user, user]
    numbers = jnp.concatenate(numbers + [jnp.zeros((8, 256), jnp.float32)], axis=0)
    buf[0, 512:528] = numbers.astype(jnp.bfloat16)

    for event in late:
        block_copy(SENDS.index(event)).start()

    first = seq * 512
    places = first + lax.broadcasted_iota(jnp.int32, (512, 256), 0)
    for load in loads[7:]:
        load.wait()
    for u in range(2):
        rows = hist_ref[u].astype(jnp.float32)
        keys[u] = jnp.where(places < length_ref[u], rows, 0.0).astype(jnp.bfloat16)
    hist_sum[...] = jnp.zeros_like(hist_sum)
    def rank_items():
        items = jnp.concatenate([item_ref[0:1], item_ref[1:2]], axis=1)
        owner = items // ITEM_DEV
        other = [owner // 32, owner // 16 % 2, owner // 4 % 4, owner % 4]
        off_x, off_y, off_z = (other[0] - x + 4) % 4, (other[2] - y + 4) % 4, (other[3] - z + 4) % 4
        message = (other[1] + core) % 2 * 64 + (off_z + 8 - off_x - off_y) % 4 * 16 + off_y * 4 + off_x
        found = lax.broadcasted_iota(jnp.int32, (128, 1024), 0) == message
        column = jnp.transpose(jnp.broadcast_to(items.astype(jnp.float32), (128, 1024)))[:, 0:1]
        same = column == items.astype(jnp.float32)
        one, zero = jnp.float32(1.0), jnp.float32(0.0)
        alike[...] = jnp.where(same, one, zero).astype(jnp.bfloat16)
        number = lax.broadcasted_iota(jnp.int32, (1024, 1024), 0)
        other_number = lax.broadcasted_iota(jnp.int32, (1024, 1024), 1)
        repeats = jnp.sum(jnp.where(same & (number < other_number), one, zero), axis=0, keepdims=True)
        first = jnp.where(repeats == 0.0, one, zero)
        matches[...] = jnp.where(found, first, zero)
        counts = jnp.dot(
            matches[...].astype(jnp.bfloat16), jnp.where(number <= other_number, one, zero).astype(jnp.bfloat16),
            preferred_element_type=jnp.float32,
        )
        rank = jnp.sum(matches[...] * counts, axis=0, keepdims=True) - first
        rank = jnp.dot(
            jnp.broadcast_to(rank, (8, 1024)).astype(jnp.bfloat16), alike[...], preferred_element_type=jnp.float32
        )[0:1].astype(jnp.int32)
        places_of[0:1] = message * 16 + rank
        places_of[1:2] = rank
        place = (items % ITEM_DEV) * 2 + 16
        column = lax.broadcasted_iota(jnp.int32, (128, 1024), 0)
        number = jnp.where(column < 16, place % 256, jnp.where(column < 32, 0, place // 256))
        ranked = (column % 16 == rank) & (column < 48)
        code_rows[...] = jnp.where(ranked, number, 0).astype(jnp.float32)
        code_spots[...] = jnp.where(ranked & (column >= 16) & (column < 32), one, zero)

    def products_of(k):
        numbers = buf[k, 512:528].astype(jnp.float32)
        normalizer = numbers[0:1] + numbers[1:2] + numbers[2:3]
        inner_sum = numbers[3:4] + numbers[4:5] + numbers[5:6]
        pick = [numbers[6:7], numbers[7:8]]
        low = [w.astype(jnp.bfloat16) for w in pick]
        both = buf[k, 0:512]
        mine = keys[0] * low[0] + keys[1] * low[1]
        products = nt(mine, both)
        probability = jnp.exp(products[:, :256] - normalizer)
        score_grad = (probability * (products[:, 256:] - inner_sum)).astype(jnp.bfloat16)
        weights = jnp.concatenate([score_grad, probability.astype(jnp.bfloat16)], axis=1)
        key_part = jnp.dot(weights, both, preferred_element_type=jnp.float32)
        return pick, key_part, tn(score_grad, mine)

    def keep_part(k, query_part):
        words, power = quantized(query_part)
        for h in range(2):
            columns = slice(h * 128, (h + 1) * 128)
            part_out[k, h, 0:128] = words[:, columns]
            part_out[k, h, 128:136] = power[:, columns]

    def one_step(k):
        pick, key_part, query_part = products_of(k)
        hist_sum[0] += key_part * pick[0]
        hist_sum[1] += key_part * pick[1]
        keep_part(k, query_part)

    def two_steps(n, carry):
        k = n * 2 + 1
        for i in range(1, 15, 2):
            if PLAN[i] or PLAN[i + 1]:

                @pl.when(k == i)
                def _(i=i):
                    run_plan(i)
                    run_plan(i + 1)

        pick, key_part, query_part = products_of(k)
        next_pick, next_key_part, next_query_part = products_of(k + 1)
        for u in range(2):
            hist_sum[u] += key_part * pick[u] + next_key_part * next_pick[u]
        keep_part(k, query_part)
        keep_part(k + 1, next_query_part)
        for i in range(11, 15, 2):

            @pl.when(k == i)
            def _(i=i):
                send_parts(i)
                send_parts(i + 1)

        return carry

    one_step(0)
    rank_items()
    lax.fori_loop(0, 7, two_steps, 0)
    run_plan(15)
    one_step(15)
    send_parts(15)

    tops = []
    for u in range(2):
        hist_sum[u] = jnp.where(places < length_ref[u], hist_sum[u], 0.0)
        top = jnp.max(jnp.abs(hist_sum[u]), axis=1, keepdims=True) * 1.01
        tops.append(jnp.broadcast_to(top, (512, 128)).astype(jnp.bfloat16))
    power = power_of(jnp.dot(alike[...], jnp.concatenate(tops, axis=0), preferred_element_type=jnp.float32))
    scale = jnp.exp2(15.0 - power) * 0.99
    for u in range(2):
        rows = pl.ds(u * 512, 512)
        for h in range(2):
            q = jnp.round(hist_sum[u, :, h * 128 : h * 128 + 128] * scale[u * 512 : u * 512 + 512]).astype(jnp.int32)
            halves[rows, h * 128 : h * 128 + 128] = (q >> 8).astype(jnp.float32).astype(jnp.bfloat16)
            halves[rows, 256 + h * 128 : 384 + h * 128] = (q & 255).astype(jnp.float32).astype(jnp.bfloat16)
    first_lane = lax.broadcasted_iota(jnp.int32, (1024, 128), 1) == 0
    power = nt(jnp.ones((8, 128), jnp.bfloat16), jnp.where(first_lane, power, 0.0).astype(jnp.bfloat16))[0:1]
    codes = nt(
        matches[...].astype(jnp.bfloat16),
        (code_rows[...] + code_spots[...] * (power + 128.0)).astype(jnp.bfloat16),
    )
    codes_out[...] = codes.astype(jnp.int32).reshape(128, 1, 128)

    def rows_copy(m, there):
        return pltpu.make_async_remote_copy(
            src_ref=rows_out.at[m], dst_ref=rows_in.at[m], send_sem=rows_send, recv_sem=rows_recv,
            device_id=there, device_id_type=MESH,
        )

    def codes_copy(m, there):
        return pltpu.make_async_remote_copy(
            src_ref=codes_out.at[m], dst_ref=codes_in.at[m], send_sem=codes_send, recv_sem=codes_recv,
            device_id=there, device_id_type=MESH,
        )

    own_rows = pltpu.make_async_copy(rows_out.at[0], rows_in.at[0], own_sem.at[0])
    own_codes = pltpu.make_async_copy(codes_out.at[0], codes_in.at[0], own_sem.at[1])

    def send_chunk(c, carry):
        slots = lax.broadcasted_iota(jnp.int32, (256, 1024), 0) + c * 256
        chosen = jnp.where(slots == places_of[0:1], 1.0, 0.0).astype(jnp.bfloat16)
        moved = jnp.dot(chosen, halves[...], preferred_element_type=jnp.float32).astype(jnp.int32)
        value = (moved[:, 0:256] << 8) + moved[:, 256:512]
        words = (value[:, 128:256] << 16) | (value[:, 0:128] & 0xFFFF)
        rows_out[pl.ds(c * 16, 16)] = words.reshape(16, 16, 128)

        to_core = (core + c // 4) % 2
        to_z = [(z + c + d) % 4 for d in range(4)]
        for j in range(16):
            m = c * 16 + j
            there = (xs[j % 4] * 2 + to_core, ys[j // 4] * 4 + to_z[(j + j // 4) % 4])

            def send_one(m=m, there=there):
                rows_copy(m, there).start()
                codes_copy(m, there).start()

            if j == 0:
                pl.when(c > 0)(send_one)
            else:
                send_one()
        return carry

    lax.fori_loop(0, 1, send_chunk, 0)
    for across in (0, 1):
        for h in range(2):
            pass_on(h, across)

    lax.fori_loop(1, 3, send_chunk, 0)
    for across in (3, 2):
        for h in range(2):
            pass_on(h, across)

    lax.fori_loop(3, 8, send_chunk, 0)
    own_rows.start()
    own_codes.start()

    for h in range(2):
        for j in range(2):
            for across in range(4):
                line_copy(
                    part_in.at[h, j, across], part_in.at[h, j, across], h, 1,
                    mid_send.at[h, across], part_recv.at[h, j, across],
                ).wait_recv()
    firsts = []
    for h in range(2):
        for d in range(4):
            own = SLOT[(d, 0) if h == 0 else (0, d)]
            low, high = restored(part_out[own, h, 0:128], part_out[own, h, 128:129])
            for source in range(2):
                a, b = restored(part_in[h, source, d, 0:128], part_in[h, source, d, 128:129])
                low, high = low + a, high + b
            if d == 0:
                firsts.append((low, high))
            else:
                words, power = quantized(jnp.concatenate([low, high], axis=0))
                sums_out[h, d - 1, 0:128] = words
                sums_out[h, d - 1, 128:136] = power
                sums_copy(h, d).start()
    for h in range(2):
        low, high = firsts[h]
        for d in range(1, 4):
            sums_copy(h, d).wait_recv()
        for source in range(3):
            a, b = restored(sums_in[h, source, 0:128], sums_in[h, source, 128:129])
            low, high = low + a, high + b
        columns = slice(h * 128, (h + 1) * 128)
        cand_out[0:128, columns] = low * 0.0625 * gates[0:128, columns]
        cand_out[128:256, columns] = high * 0.0625 * gates[128:256, columns]
    for number in range(len(SENDS)):
        block_copy(number).wait_send()
    for i, h in parts:
        part_copy(i, h).wait_send()
    for h in range(2):
        for across in range(4):
            mid_copy(h, across).wait_send()
    for h in range(2):
        for d in range(1, 4):
            sums_copy(h, d).wait_send()
    own_rows.wait()
    own_codes.wait()
    others = pl.ds(1, 127)
    all_rows = pltpu.make_async_remote_copy(
        src_ref=rows_out.at[others], dst_ref=rows_in.at[others], send_sem=rows_send, recv_sem=rows_recv,
        device_id=device(0, 1), device_id_type=MESH,
    )
    all_codes = pltpu.make_async_remote_copy(
        src_ref=codes_out.at[others], dst_ref=codes_in.at[others], send_sem=codes_send, recv_sem=codes_recv,
        device_id=device(0, 1), device_id_type=MESH,
    )
    all_codes.wait()
    got = jnp.transpose(codes_in[...].reshape(128, 128).astype(jnp.float32)).astype(jnp.int32)
    codes_out_t[0:16] = got[0:16] + got[32:48] * 256
    codes_out_t[16:32] = got[16:32]
    all_rows.wait()


def table_kernel(
    rows_hbm, codes_hbm, cand_hbm, table_out, cand_out,
    rows_ref, codes_ref, powers_ref, cand_ref, values, t0, t1, table, sem
):
    loads = [
        pltpu.make_async_copy(codes_hbm.at[0:16], codes_ref, sem.at[9]),
        pltpu.make_async_copy(codes_hbm.at[16:32], powers_ref, sem.at[10]),
        pltpu.make_async_copy(cand_hbm, cand_ref, sem.at[11]),
    ]
    for part in range(4):
        rows = pl.ds(part * 512, 512)
        loads.append(pltpu.make_async_copy(rows_hbm.at[rows], rows_ref.at[rows], sem.at[12 + part]))
    for load in loads:
        load.start()
    cand_copy = pltpu.make_async_copy(cand_ref, cand_out, sem.at[8])

    def clear(c, carry):
        for t in (t0, t1):
            t[pl.ds(c * 1024, 1024)] = jnp.zeros((1024, 128), jnp.float32)
        return carry

    lax.fori_loop(0, 8, clear, 0)
    for t in (t0, t1):
        t[8192:8208] = jnp.zeros((16, 128), jnp.float32)

    for load in loads[:3]:
        load.wait()
    cand_copy.start()
    scales = jnp.exp2(powers_ref[...].astype(jnp.float32) - 143.0) * (1.0 / 0.99)
    for m in range(128):
        if m % 32 == 0:
            loads[3 + m // 32].wait()
        scale = scales[:, m : m + 1]
        words = rows_ref[m * 16 : m * 16 + 16]
        values[pl.ds(m * 32, 16, stride=2)] = ((words << 16) >> 16).astype(jnp.float32) * scale
        values[pl.ds(m * 32 + 1, 16, stride=2)] = (words >> 16).astype(jnp.float32) * scale

    def add_messages(i, carry):
        pair = ((t0, i * 2), (t1, i * 2 + 1))
        places = [[pl.ds(pl.multiple_of(codes_ref[j, m], 2), 2) for j in range(16)] for _, m in pair]
        sums = [
            [t[places[n][j]] + values[pl.ds(m * 32 + j * 2, 2)] for j in range(16)] for n, (t, m) in enumerate(pair)
        ]
        for n, (t, m) in enumerate(pair):
            for j in range(16):
                t[places[n][j]] = sums[n][j]
        return carry

    lax.fori_loop(0, 64, add_messages, 0)

    def out_copy(c):
        rows = pl.ds(c * 512, 512)
        return pltpu.make_async_copy(table.at[rows], table_out.at[rows], sem.at[c])

    for c in range(8):
        for h in range(2):
            rows = pl.ds(16 + c * 1024 + h, 512, stride=2)
            table[c * 512 : c * 512 + 512, h * 128 : h * 128 + 128] = t0[rows] + t1[rows]
        out_copy(c).start()
    for c in range(8):
        out_copy(c).wait()
    cand_copy.wait()


def add_rows(rows, codes, candidate_grad):
    hbm = pl.BlockSpec(memory_space=pltpu.HBM)
    return pl.pallas_call(
        table_kernel,
        out_shape=(
            jax.ShapeDtypeStruct((ITEM_DEV, 256), jnp.float32),
            jax.ShapeDtypeStruct((256, 256), jnp.float32),
        ),
        in_specs=[hbm, hbm, hbm],
        out_specs=(hbm, hbm),
        scratch_shapes=[
            pltpu.VMEM((2048, 128), jnp.int32),
            pltpu.SMEM((16, 128), jnp.int32),
            pltpu.VMEM((16, 128), jnp.int32),
            pltpu.VMEM((256, 256), jnp.float32),
            pltpu.VMEM((4104, 128), jnp.float32),
            pltpu.VMEM((2 * ITEM_DEV + 32, 128), jnp.float32),
            pltpu.VMEM((2 * ITEM_DEV + 32, 128), jnp.float32),
            pltpu.VMEM((ITEM_DEV, 256), jnp.float32),
            pltpu.SemaphoreType.DMA((16,)),
        ],
        compiler_params=pltpu.CompilerParams(vmem_limit_bytes=64 * 1024 * 1024),
        cost_estimate=pl.CostEstimate(flops=2_000_000, bytes_accessed=5_500_000, transcendentals=0),
        name="table_rows",
    )(rows, codes, candidate_grad)


def attention(candidates, scenarios, users, gate_table, normalizer, forward_out, out_grad, history, items, lengths):
    vmem = pl.BlockSpec(memory_space=pltpu.VMEM)
    return pl.pallas_call(
        attention_kernel,
        out_shape=(
            jax.ShapeDtypeStruct((256, 256), jnp.float32),
            jax.ShapeDtypeStruct((128, 16, 128), jnp.int32),
            jax.ShapeDtypeStruct((32, 128), jnp.int32),
        ),
        in_specs=[pl.BlockSpec(memory_space=pltpu.HBM)] * 10,
        out_specs=(vmem, pl.BlockSpec(memory_space=pl.ANY), vmem),
        scratch_shapes=[
            pltpu.VMEM((256, 256), jnp.bfloat16),
            pltpu.VMEM((1, 256), jnp.int32),
            pltpu.VMEM((1, 256), jnp.int32),
            pltpu.VMEM((16, 256), jnp.float32),
            pltpu.VMEM((1, 256), jnp.float32),
            pltpu.VMEM((256, 256), jnp.bfloat16),
            pltpu.VMEM((2, 512, 256), jnp.bfloat16),
            pltpu.VMEM((2, 512), jnp.int32),
            pltpu.SMEM((2,), jnp.int32),
            pltpu.VMEM((16, BLOCK, 256), jnp.bfloat16),
            pltpu.VMEM((2, 512, 256), jnp.bfloat16),
            pltpu.VMEM((256, 256), jnp.float32),
            pltpu.VMEM((16, 2, 136, 128), jnp.int32),
            pltpu.VMEM((2, 2, 4, 136, 128), jnp.int32),
            pltpu.VMEM((2, 4, 136, 128), jnp.int32),
            pltpu.VMEM((2, 4, 136, 128), jnp.int32),
            pltpu.VMEM((2, 3, 136, 128), jnp.int32),
            pltpu.VMEM((2, 3, 136, 128), jnp.int32),
            pltpu.VMEM((2, 512, 256), jnp.float32),
            pltpu.VMEM((1024, 1024), jnp.bfloat16),
            pltpu.VMEM((128, 1024), jnp.float32),
            pltpu.VMEM((8, 1024), jnp.int32),
            pltpu.VMEM((1024, 512), jnp.bfloat16),
            pltpu.VMEM((128, 16, 128), jnp.int32),
            pltpu.VMEM((128, 1, 128), jnp.int32),
            pltpu.VMEM((128, 1, 128), jnp.int32),
            pltpu.VMEM((128, 1024), jnp.float32),
            pltpu.VMEM((128, 1024), jnp.float32),
            pltpu.SemaphoreType.DMA((10,)),
            pltpu.SemaphoreType.DMA((len(SENDS),)),
            pltpu.SemaphoreType.DMA((16, 4)),
            pltpu.SemaphoreType.DMA((16, 2)),
            pltpu.SemaphoreType.DMA((2, 2, 4)),
            pltpu.SemaphoreType.DMA((2, 4)),
            pltpu.SemaphoreType.DMA((2, 4)),
            pltpu.SemaphoreType.DMA((2, 3)),
            pltpu.SemaphoreType.DMA((2, 3)),
            pltpu.SemaphoreType.DMA,
            pltpu.SemaphoreType.DMA,
            pltpu.SemaphoreType.DMA,
            pltpu.SemaphoreType.DMA,
            pltpu.SemaphoreType.DMA((2,)),
        ],
        compiler_params=pltpu.CompilerParams(
            collective_id=0, has_side_effects=True, vmem_limit_bytes=64 * 1024 * 1024
        ),
        cost_estimate=pl.CostEstimate(
            flops=5_400_000_000, bytes_accessed=4_000_000, transcendentals=2_100_000
        ),
        name="attention_grads",
    )(
        candidates, scenarios.reshape(1, -1), users.reshape(1, -1), gate_table, normalizer.reshape(1, -1),
        forward_out, out_grad, history, items, lengths,
    )


def local(
    candidates,
    scenarios,
    candidate_user,
    gate_table,
    log_normalizer,
    forward_out,
    out_grad,
    history,
    history_length,
    history_items,
):
    candidate_grad, rows, codes = attention(
        candidates, scenarios, candidate_user, gate_table, log_normalizer,
        forward_out, out_grad, history, history_items, history_length,
    )
    table_grad, candidate_grad = add_rows(rows.reshape(2048, 128), codes, candidate_grad)
    return (candidate_grad, table_grad)


def solution(mesh):
    return jax.shard_map(
        local,
        mesh=mesh,
        in_specs=(
            P(("dp", "seq"), None),
            P(("dp", "seq")),
            P(("dp", "seq")),
            P(),
            P(("dp", "seq")),
            P(("dp", "seq"), None),
            P(("dp", "seq"), None),
            P("dp", "seq", None),
            P("dp"),
            P("dp", "seq"),
        ),
        out_specs=(P(("dp", "seq"), None), P(("dp", "seq"), None)),
        check_vma=False,
    )
```
